32 devices in a mesh: col: 4 (over y, x), ta: 8 (over z, core).
Axes of the slice: x: 2, y: 2, z: 4, core: 2. Of those that a mesh axis runs over, the one named last changes fastest.
Arguments:
- frames: bfloat16 [672, 14, 14, 1024], P(('col', 'ta')), may hold values from -6 to 6
- out_grad: bfloat16 [672, 14, 14, 1024], P(('col', 'ta')), may hold values from -6 to 6
- held: int32 [4, 8], replicated, may hold values from 3 to 21, as said below
- clip_stride: int32 [4, 24], replicated, may hold values from 1 to 4, as said below
- w_reduce: bfloat16 [2, 1024, 256], replicated, may hold values from -0.1875 to 0.1875
- w_mid: bfloat16 [2, 256, 256], replicated, may hold values from -0.375 to 0.375
- depth_kernel: bfloat16 [2, 27, 256], replicated, may hold values from -1.25 to 1.25
- w_expand: bfloat16 [2, 256, 1024], replicated, may hold values from -0.375 to 0.375
- narrow_gain: bfloat16 [2, 2, 256], replicated, may hold values from 0.099609375 to 1.8984375
- narrow_bias: bfloat16 [2, 2, 256], replicated, may hold values from -3 to 3
- wide_gain: bfloat16 [2, 1024], replicated, may hold values from 0.099609375 to 1.8984375
- wide_bias: bfloat16 [2, 1024], replicated, may hold values from -3 to 3
Outputs:
- block_output: bfloat16 [672, 14, 14, 1024], P(('col', 'ta'))
- grad_frames: bfloat16 [672, 14, 14, 1024], P(('col', 'ta'))
- grad_w_reduce: float32 [2, 1024, 256], replicated
- grad_w_mid: float32 [2, 256, 256], replicated
- grad_depth_kernel: float32 [2, 27, 256], replicated
- grad_w_expand: float32 [2, 256, 1024], replicated
- grad_narrow_gain: float32 [2, 2, 256], replicated
- grad_narrow_bias: float32 [2, 2, 256], replicated
- grad_wide_gain: float32 [2, 1024], replicated
- grad_wide_bias: float32 [2, 1024], replicated
The draws below stay inside these ranges and needn't reach their ends.
Inputs may be any that keep to these rules, and one draw needn't show every extreme that they name: `held`: devices 2i and 2i + 1 of ta hold 24 live frames together, in every clip group. `clip_stride`: in each group a quarter of the clips have stride 1 (8 frames), a quarter stride 2 (4 frames) and half stride 4 (2 frames), in any order.
All inputs are finite; a program needn't handle non-finite values.
Results may differ from the reference program's by a relative error of at most 0.017.
Values may be sent and summed in bfloat16 or wider, within the bound.
A program may use at most 320 MiB of HBM per device.

```python
import jax
import jax.numpy as jnp
from jax import lax

D = 1024
BOT = 256
HH = 14
WW = 14
BLOCKS = 2
FR_DEV = 12
DMAX = 9
CAP = 21
FRAMES_G = 96
CLIPS_G = 24
SLOTS = 672
N_COL = 4
N_TA = 8


def draw_held(key, part):
    key = jax.random.fold_in(key, 11)
    key_shift, key_pick, key_sign = jax.random.split(key, 3)
    shifts = jax.random.randint(key_shift, (N_COL, N_TA // 2), -DMAX, DMAX + 1)
    picked = jax.random.randint(key_pick, (N_COL, 1), 0, N_TA // 2)
    sign_pick = 2 * jax.random.randint(key_sign, (N_COL, 1), 0, 2) - 1
    pair_ids = jnp.arange(N_TA // 2)[None, :]
    shifts = jnp.where(pair_ids == picked, sign_pick * DMAX, shifts)
    paired = jnp.stack([FR_DEV + shifts, FR_DEV - shifts], axis=2)
    return paired.reshape(N_COL, N_TA).astype(jnp.int32)


def draw_clip_stride(key, part):
    key = jax.random.fold_in(key, 23)
    quarter = CLIPS_G // 4
    ordered = jnp.concatenate([jnp.ones((quarter,), jnp.int32), jnp.full((quarter,), 2, jnp.int32), jnp.full((CLIPS_G - 2 * quarter,), 4, jnp.int32)])
    row_keys = jax.random.split(key, N_COL)
    shuffled = jax.vmap(lambda row_key: jax.random.permutation(row_key, ordered))(row_keys)
    return shuffled.astype(jnp.int32)


def level_of(own_key, shape, pieces, least, top_value):
    loudness = 1.0
    for dim, blocks in pieces:
        draws = jax.random.uniform(jax.random.fold_in(jax.random.fold_in(own_key, 6), dim), (blocks,), jnp.float32, least / len(pieces), top_value / len(pieces))
        loudness = loudness * jnp.repeat(jnp.exp(draws), shape[dim] // blocks).reshape((-1,) + (1,) * (len(shape) - 1 - dim))
    return loudness


def bell_draw(stream_key, dims, deviation, bound, cuts=(), kind=jnp.bfloat16):
    gain = level_of(stream_key, dims, cuts, -0.22, 0.18) if cuts else 1.0
    values = jax.random.normal(stream_key, dims, jnp.float32) * deviation * gain
    return jnp.minimum(jnp.maximum(values, -bound), bound).astype(kind)


def setup_inputs(seed: int = 0) -> dict:
    key_of = jax.random.split(jax.random.key(seed), 13)
    frames = bell_draw(key_of[0], (SLOTS, HH, WW, D), 1.0, 6.0, ((0, 32),))
    out_grad = bell_draw(key_of[1], (SLOTS, HH, WW, D), 1.0, 6.0, ((0, 32),))
    held = draw_held(jax.random.fold_in(key_of[12], 71), 0)
    clip_stride = draw_clip_stride(jax.random.fold_in(key_of[12], 71), 0)
    w_reduce = bell_draw(key_of[4], (BLOCKS, D, BOT), D ** -0.5, 0.1875)
    w_mid = bell_draw(key_of[5], (BLOCKS, BOT, BOT), BOT ** -0.5, 0.375)
    depth_kernel = bell_draw(key_of[6], (BLOCKS, 27, BOT), 27 ** -0.5, 1.25)
    w_expand = bell_draw(key_of[7], (BLOCKS, BOT, D), BOT ** -0.5, 0.375)
    narrow_gain = jnp.clip(1.0 + 0.18 * jax.random.normal(key_of[8], (BLOCKS, 2, BOT), jnp.float32), 0.099609375, 1.8984375).astype(jnp.bfloat16)
    narrow_bias = bell_draw(key_of[9], (BLOCKS, 2, BOT), 0.5, 3.0)
    wide_gain = jnp.clip(1.0 + 0.18 * jax.random.normal(key_of[10], (BLOCKS, D), jnp.float32), 0.099609375, 1.8984375).astype(jnp.bfloat16)
    wide_bias = bell_draw(key_of[11], (BLOCKS, D), 0.5, 3.0)
    return dict(frames=frames, out_grad=out_grad, held=held, clip_stride=clip_stride, w_reduce=w_reduce, w_mid=w_mid, depth_kernel=depth_kernel, w_expand=w_expand, narrow_gain=narrow_gain, narrow_bias=narrow_bias, wide_gain=wide_gain, wide_bias=wide_bias)


EPS = 1e-05

@jax.custom_vjp
def low(v):
    return lax.optimization_barrier(v.astype(jnp.bfloat16)).astype(jnp.float32)

@jax.custom_vjp
def low_back(v):
    return v

def low_keep(v):
    return (low(v), None)

def low_pass(kept, grad):
    return (grad,)

def back_keep(v):
    return (v, None)

def back_low(kept, grad):
    return (low(grad),)
low.defvjp(low_keep, low_pass)
low_back.defvjp(back_keep, back_low)

def matmul(left, right):
    flat_left = left.reshape(-1, left.shape[-1])
    product = jnp.dot(flat_left, right, precision=lax.Precision.HIGHEST, preferred_element_type=jnp.float32)
    return product.reshape(left.shape[:-1] + (right.shape[-1],))

def batch_norm(values, gain_vec, bias_vec):
    axes_all = (0, 1, 2, 3)
    average = lax.optimization_barrier(jnp.mean(values, axis=axes_all))
    centred = values - average
    spread = lax.optimization_barrier(jnp.mean(centred * centred, axis=axes_all))
    return gain_vec * centred * lax.rsqrt(spread + EPS) + bias_vec

def depthwise(source, kernel, prev_ok, next_ok):
    zero_frame = jnp.zeros_like(source[:, :1])
    earlier = jnp.concatenate([zero_frame, source[:, :-1]], axis=1) * prev_ok[:, :, None, None, None]
    later = jnp.concatenate([source[:, 1:], zero_frame], axis=1) * next_ok[:, :, None, None, None]
    result = jnp.zeros_like(source)
    for plane_id, plane in enumerate((earlier, source, later)):
        padded = jnp.pad(plane, ((0, 0), (0, 0), (1, 1), (1, 1), (0, 0)))
        for row_off in range(3):
            for col_off in range(3):
                result = result + kernel[plane_id * 9 + row_off * 3 + col_off] * padded[:, :, row_off:row_off + HH, col_off:col_off + WW, :]
    return result

def clip_masks(clip_stride):
    lengths = (8 // clip_stride).astype(jnp.int32)
    starts = (jnp.cumsum(lengths, axis=1) - lengths).astype(jnp.int32)
    frame_ids = jnp.arange(FRAMES_G, dtype=jnp.int32)
    begins = lax.optimization_barrier(jnp.sum((starts[:, None, :] == frame_ids[None, :, None]).astype(jnp.int32), axis=2))
    prev_ok = (1 - begins).astype(jnp.float32)
    next_ok = jnp.concatenate([prev_ok[:, 1:], jnp.zeros((N_COL, 1), jnp.float32)], axis=1)
    return (prev_ok, next_ok)

def slot_layout(held):
    offsets = (jnp.cumsum(held, axis=1) - held).astype(jnp.int32)
    frame_ids = jnp.arange(FRAMES_G, dtype=jnp.int32)
    owner = (lax.optimization_barrier(jnp.sum((offsets[:, None, :] <= frame_ids[None, :, None]).astype(jnp.int32), axis=2)) - 1).astype(jnp.int32)
    local = frame_ids[None, :] - jnp.take_along_axis(offsets, owner, axis=1)
    groups = jnp.arange(N_COL, dtype=jnp.int32)[:, None]
    frame_slot = ((groups * N_TA + owner) * CAP + local).reshape(-1).astype(jnp.int32)
    slot_ids = jnp.arange(SLOTS, dtype=jnp.int32)
    slot_group = (slot_ids // (N_TA * CAP)).astype(jnp.int32)
    slot_device = (slot_ids // CAP % N_TA).astype(jnp.int32)
    slot_local = (slot_ids % CAP).astype(jnp.int32)
    slot_alive = slot_local < held[slot_group, slot_device]
    slot_frame = slot_group * FRAMES_G + jnp.minimum(offsets[slot_group, slot_device] + slot_local, FRAMES_G - 1)
    return (frame_slot, slot_alive, slot_frame.astype(jnp.int32))

def reference(frames, out_grad, held, clip_stride, w_reduce, w_mid, depth_kernel, w_expand, narrow_gain, narrow_bias, wide_gain, wide_bias):
    frame_slot, slot_alive, slot_frame = slot_layout(held)
    prev_ok, next_ok = clip_masks(clip_stride)
    grid_shape = (N_COL, FRAMES_G, HH, WW, D)
    inputs = jnp.take(frames, frame_slot, axis=0).astype(jnp.float32).reshape(grid_shape)
    cotangent = jnp.take(out_grad, frame_slot, axis=0).astype(jnp.float32).reshape(grid_shape)
    params = tuple((weight_arg.astype(jnp.float32) for weight_arg in (w_reduce, w_mid, depth_kernel, w_expand, narrow_gain, narrow_bias, wide_gain, wide_bias)))

    def one_block(acts, w_one, w_two, kernel, w_three, n_gain, n_bias, g_wide, b_wide):
        h_one = low_back(matmul(low(acts), w_one))
        u_one = jax.nn.silu(batch_norm(h_one, n_gain[0], n_bias[0]))
        h_two = low(low_back(matmul(low(u_one), w_two)))
        depth = depthwise(h_two, kernel, prev_ok, next_ok)
        u_two = jax.nn.silu(batch_norm(depth, n_gain[1], n_bias[1]))
        h_three = low_back(matmul(low(u_two), w_three))
        return jax.nn.silu(acts + batch_norm(h_three, g_wide, b_wide))
    checked_block = jax.checkpoint(one_block)

    def forward(acts, w_one, w_two, kernels, w_three, n_gain, n_bias, g_wide, b_wide):
        for block_id in range(BLOCKS):
            acts = checked_block(acts, w_one[block_id], w_two[block_id], kernels[block_id], w_three[block_id], n_gain[block_id], n_bias[block_id], g_wide[block_id], b_wide[block_id])
        return acts
    result, pullback = jax.vjp(forward, inputs, *params)
    grads = pullback(cotangent)

    def to_slots(values):
        flat_rows = values.reshape(N_COL * FRAMES_G, HH, WW, D)
        picked = jnp.take(flat_rows, slot_frame, axis=0)
        return jnp.where(slot_alive[:, None, None, None], picked, jnp.zeros((), picked.dtype)).astype(jnp.bfloat16)
    return (to_slots(result), to_slots(grads[0]), grads[1], grads[2], grads[3], grads[4], grads[5], grads[6], grads[7], grads[8])
```

```python
import functools

import jax
import jax.numpy as jnp
from jax import lax
from jax.experimental import pallas as pl
from jax.experimental.pallas import tpu as pltpu
from jax.sharding import PartitionSpec as P

FR = 12
EPS = 1e-05
MESH = pl.DeviceIdType.MESH
F32 = jnp.float32
BF16 = jnp.bfloat16
ANY = pl.BlockSpec(memory_space=pl.ANY)
VM = pl.BlockSpec(memory_space=pltpu.VMEM)
SM = pl.BlockSpec(memory_space=pltpu.SMEM)


def loop(low, high, step):
    lax.fori_loop(low, high, step, 0)


def dot_nn(left, right):
    return lax.dot_general(left, right, (((1,), (0,)), ((), ())), preferred_element_type=F32)


def dot_nt(left, right):
    return lax.dot_general(left, right, (((1,), (1,)), ((), ())), preferred_element_type=F32)


def dot_tn(left, right):
    return lax.dot_general(left, right, (((0,), (0,)), ((), ())), preferred_element_type=F32)


def silu(values):
    half = 0.5 * values
    return half * jnp.tanh(half) + half


def silu_and_slope(values):
    half = 0.5 * values
    tan = jnp.tanh(half)
    act = half * tan + half
    sig = 0.5 * tan + 0.5
    return act, act + sig * (1.0 - act)


def main_kernel(
    dims,
    held,
    okmask,
    frames,
    gout,
    w1,
    w2,
    w3,
    taps,
    ngain,
    nbias,
    wgain,
    wbias,
    a2w,
    a2r,
    gw,
    gr,
    o_w1t,
    o_w2,
    o_w3,
    o_k,
    o_ng,
    o_nb,
    o_wg,
    o_wb,
    pool,
    a0,
    a1,
    pbuf,
    tile,
    ost,
    u2b,
    hbuf,
    x1b,
    x2b,
    cbuf,
    dbuf,
    dhb,
    wacc,
    w2acc,
    kacc,
    nbuf,
    tbuf,
    gbuf,
    sacc,
    prm,
    in_sem,
    rem_sem,
    halo_sem,
    out_sem,
    wout_sem,
    ns_sem,
    nr_sem,
    ts_sem,
    tr_sem,
    gs_sem,
    gr_sem,
):
    n_col, n_ta, cap, hh, ww, width, bot = dims
    n_dev = n_col * n_ta
    extra = cap - FR
    wp = 16
    rf = hh * wp
    stride = (hh + 2) * wp
    lead = 8
    n_local = float(FR * hh * ww)
    n_total = n_local * n_dev
    chunks = width // 256
    col, ta = lax.axis_index("col"), lax.axis_index("ta")
    me = col * n_ta + ta
    odd = lax.rem(ta, 2)
    sib = (col, ta + 1 - 2 * odd)
    nxt = (col, lax.rem(ta + 1, n_ta))
    prv = (col, lax.rem(ta + n_ta - 1, n_ta))

    def peer(k):
        other = lax.rem(me + k, n_dev)
        return (lax.div(other, n_ta), lax.rem(other, n_ta))

    own_cp = pltpu.make_async_copy(frames, pool.at[pl.ds(0, cap)], in_sem.at[0])
    own_cp.start()
    barrier = pltpu.get_barrier_semaphore()

    def greet(k, carry):
        pl.semaphore_signal(barrier, inc=1, device_id=peer(k), device_id_type=MESH)
        return carry

    loop(1, n_dev, greet)

    live_row = (lax.broadcasted_iota(jnp.int32, (wp, 1), 0) < ww).astype(F32)

    def masked(values):
        c = values.shape[-1]
        return (values.reshape(-1, wp, c) * live_row[None]).reshape(-1, c)

    def rowsum(values):
        return jnp.sum(values.reshape(-1, wp, values.shape[-1]), axis=0)

    def live_total(acc):
        return jnp.sum(acc * live_row, axis=0, keepdims=True)

    def zero_tile(f, carry):
        a0[f] = jnp.zeros((hh, wp, width), BF16)
        pbuf[f] = jnp.zeros((hh, wp, width), BF16)
        return carry

    loop(0, FR, zero_tile)
    for ref in (cbuf.at[0], cbuf.at[1], dbuf):

        def zero_conv(i, carry, ref=ref):
            for h in range(2):
                ref[h, pl.ds(pl.multiple_of(i * 64, 64), 64)] = jnp.zeros((64, 128), F32)
            return carry

        loop(0, ref.shape[1] // 64, zero_conv)

    pl.semaphore_wait(barrier, n_dev - 1)

    def swap_in(src):
        cp = pltpu.make_async_remote_copy(
            src_ref=src.at[pl.ds((1 - odd) * FR, extra)],
            dst_ref=pool.at[pl.ds(cap, extra)],
            send_sem=rem_sem.at[0],
            recv_sem=rem_sem.at[1],
            device_id=sib,
            device_id_type=MESH,
        )
        cp.start()
        return cp

    first_held = held[col, ta - odd]

    def gather_into(dst):
        def pick_frame(j, carry):
            own = jnp.where(odd == 0, j, j + FR - first_held)
            far = jnp.where(odd == 0, j - first_held, j)
            mine = jnp.where(odd == 0, j < first_held, own >= 0)
            pick = jnp.where(mine, jnp.clip(own, 0, cap - 1), cap + jnp.clip(far, 0, extra - 1))
            dst[j, :, 0:ww, :] = pool[pick]
            return carry

        loop(0, FR, pick_frame)

    cp = swap_in(frames)
    own_cp.wait()
    cp.wait()
    gather_into(a0)
    own_cp = pltpu.make_async_copy(gout, pool.at[pl.ds(0, cap)], in_sem.at[0])
    own_cp.start()

    def along_ta(k):
        return (col, lax.rem(ta + k, n_ta))

    def along_col(k):
        return (lax.rem(col + k, n_col), ta)

    stages = {
        "all": (nbuf, ns_sem, nr_sem, n_dev, me, peer),
        "ta": (tbuf, ts_sem, tr_sem, n_ta, ta, along_ta),
        "col": (gbuf, gs_sem, gr_sem, n_col, col, along_col),
    }
    used = {"all": 0, "ta": 0, "col": 0}

    def exchange(name, values, between=None):
        buf, ssem, rsem, size, mine, who = stages[name]
        par = used[name] % 2
        used[name] += 1
        buf[par, mine] = values

        def send(k, carry):
            pltpu.make_async_remote_copy(
                src_ref=buf.at[par, mine],
                dst_ref=buf.at[par, mine],
                send_sem=ssem.at[par],
                recv_sem=rsem.at[par],
                device_id=who(k),
                device_id_type=MESH,
            ).start()
            return carry

        loop(1, size, send)
        if between is not None:
            between()
        part = buf.at[par, pl.ds(0, size - 1)]
        pltpu.make_async_copy(part, part, rsem.at[par]).wait()
        pltpu.make_async_copy(part, part, ssem.at[par]).wait()
        return buf[par]

    def merge(name, mean_l, m2_l, per, size, between=None):
        got = exchange(name, jnp.concatenate([mean_l, m2_l], axis=0), between)
        total = jnp.sum(got, axis=0)
        mean = total[0:1] * (1.0 / size)
        dev = got - mean[None]
        spread = jnp.sum(dev * dev, axis=0)[0:1]
        return mean, total[1:2] + per * spread

    def moments(mean_l, m2_l, wide, between=None):
        if wide:
            mean, m2 = merge("ta", mean_l, m2_l, n_local, n_ta, between)
            mean, m2 = merge("col", mean, m2, n_local * n_ta, n_col)
        else:
            mean, m2 = merge("all", mean_l, m2_l, n_local, n_dev, between)
        return mean, lax.rsqrt(m2 * (1.0 / n_total) + EPS)

    def sums(s0, s1, wide, between=None):
        total = jnp.concatenate([s0, s1], axis=0)
        if wide:
            total = jnp.sum(exchange("ta", total, between), axis=0)
            total = jnp.sum(exchange("col", total), axis=0)
        else:
            total = jnp.sum(exchange("all", total, between), axis=0)
        return total[0:1], total[1:2]

    def rows(f):
        return pl.ds(pl.multiple_of(f * rf, rf), rf)

    def ld_h(f):
        return jnp.concatenate([hbuf[0, rows(f)], hbuf[1, rows(f)]], axis=1)

    def st_h(f, values):
        hbuf[0, rows(f)] = values[:, :128]
        hbuf[1, rows(f)] = values[:, 128:]

    def conv_rows(slot):
        return pl.ds(pl.multiple_of(lead + slot * stride + wp, 8), rf)

    def st_conv(ref, slot, values):
        ref[0, conv_rows(slot)] = values[:, :128]
        ref[1, conv_rows(slot)] = values[:, 128:]

    def local_m2(mean_l):
        sacc[0:wp, 0:bot] = jnp.zeros((wp, bot), F32)

        def to_m2(f, carry):
            d = ld_h(f) - mean_l
            sacc[0:wp, 0:bot] += rowsum(d * d)
            return carry

        loop(0, FR, to_m2)
        return live_total(sacc[0:wp, 0:bot])

    def conv_frame(src, wrow, f, flip):
        def half(h, carry):
            wts = []
            w_all = prm[h]
            for dt in range(3):
                scale = None
                if dt == 0:
                    scale = okmask[0, f]
                if dt == 2:
                    scale = okmask[1, f]
                for sp in range(9):
                    idx = dt * 9 + sp
                    row = w_all[26 - idx : 27 - idx] if flip else w_all[idx : idx + 1]
                    if scale is not None:
                        row = row * scale
                    wts.append(jnp.broadcast_to(row, (8, 128)))
            out = []
            for y in range(hh):
                for s in range(2):
                    acc = [None, None, None]
                    for dt in range(3):
                        for dy in range(3):
                            for dx in range(3):
                                off = lead + dt * stride + (y + dy) * wp + dx - 1 + s * 8
                                v = src[h, pl.ds(f * stride + off, 8)]
                                term = v * wts[dt * 9 + dy * 3 + dx]
                                acc[dx] = term if acc[dx] is None else acc[dx] + term
                    val = acc[0] + acc[1] + acc[2]
                    hbuf[h, pl.ds(pl.multiple_of(f * rf + y * wp + s * 8, 8), 8)] = val
            return carry

        loop(0, 2, half)

    def load_taps(b):
        k = taps[b].astype(F32)
        prm[0, 0:27] = k[:, :128]
        prm[1, 0:27] = k[:, 128:]

    def send_halos(ref, which):
        cps = []
        for i, (slot, land, dev) in enumerate(((1, FR + 1, prv), (FR, 0, nxt))):
            cp = pltpu.make_async_remote_copy(
                src_ref=ref.at[:, pl.ds(lead + slot * stride + wp, rf)],
                dst_ref=ref.at[:, pl.ds(lead + land * stride + wp, rf)],
                send_sem=halo_sem.at[which, i, 0],
                recv_sem=halo_sem.at[which, i, 1],
                device_id=dev,
                device_id_type=MESH,
            )
            cp.start()
            cps.append(cp)
        return cps

    def edge_first(step):
        step(0, 0)
        step(FR - 1, 0)

    def chunk(c):
        return pl.ds(c * 256, 256)

    def flat(ref, f, c):
        return ref[f, :, :, chunk(c)].reshape(rf, 256)

    def put(ref, f, c, values):
        ref[f, :, :, chunk(c)] = values.reshape(hh, wp, 256)

    def first_mm(src, b):
        sacc[0:wp, 0:bot] = jnp.zeros((wp, bot), F32)

        def to_h1(f, carry):
            h1 = dot_nn(src[f].reshape(rf, width), w1[b])
            st_h(f, h1)
            sacc[0:wp, 0:bot] += rowsum(h1)
            return carry

        loop(0, FR, to_h1)
        mean_l = live_total(sacc[0:wp, 0:bot]) * (1.0 / n_local)
        return mean_l, local_m2(mean_l)

    inv1, inv2, mean3, inv3 = {}, {}, {}, {}

    def vec(ref, b, j):
        return ref[b].astype(F32)[j : j + 1]

    def wvec(ref, b):
        return ref[...].astype(F32)[b : b + 1]

    def get_gout():
        own_cp.wait()

    def block_forward(b, src, after_first):
        mean_l, m2_l = first_mm(src, b)
        mean, inv = moments(mean_l, m2_l, False, None)
        inv1[b] = inv
        after_first()
        g, bb = vec(ngain, b, 0), vec(nbias, b, 0)

        def to_h2(f, carry):
            xhat = (ld_h(f) - mean) * inv
            x1b[b, rows(f)] = xhat.astype(BF16)
            u1 = masked(silu(xhat * g + bb)).astype(BF16)
            h2 = dot_nn(u1, w2[b]).astype(BF16).astype(F32)
            st_conv(cbuf.at[b], f + 1, h2)
            return carry

        edge_first(to_h2)
        cps = send_halos(cbuf.at[b], b)
        loop(1, FR - 1, to_h2)
        load_taps(b)

        def conv_step(f, carry):
            conv_frame(cbuf.at[b], None, f, False)
            return carry

        loop(1, FR - 1, conv_step)
        for cp in cps:
            cp.wait()
        conv_step(0, 0)
        conv_step(FR - 1, 0)
        sacc[0:wp, 0:bot] = jnp.zeros((wp, bot), F32)

        def dw_sum(f, carry):
            sacc[0:wp, 0:bot] += rowsum(ld_h(f))
            return carry

        loop(0, FR, dw_sum)
        mean_l = live_total(sacc[0:wp, 0:bot]) * (1.0 / n_local)
        m2_l = local_m2(mean_l)
        mean, inv = moments(mean_l, m2_l, False, None)
        inv2[b] = inv
        g, bb = vec(ngain, b, 1), vec(nbias, b, 1)
        sacc[0:wp, 0:bot] = jnp.zeros((wp, bot), F32)

        def to_u2(f, carry):
            xhat = (ld_h(f) - mean) * inv
            x2b[b, rows(f)] = xhat.astype(BF16)
            u2 = masked(silu(xhat * g + bb))
            u2b[b, rows(f)] = u2.astype(BF16)
            sacc[0:wp, 0:bot] += rowsum(u2)
            return carry

        loop(0, FR, to_u2)
        u_mean = live_total(sacc[0:wp, 0:bot]) * (1.0 / n_local)
        pivot = dot_nn(jnp.broadcast_to(u_mean, (16, bot)).astype(BF16), w3[b])[0:1]
        sacc[...] = jnp.zeros(sacc.shape, F32)

        def h3_stats(f, carry):
            left = u2b[b, rows(f)]
            for c in range(chunks):
                h3 = dot_nn(left, w3[b, :, chunk(c)]) - pivot[:, c * 256 : c * 256 + 256]
                sacc[0:wp, chunk(c)] += rowsum(h3)
                sacc[wp : 2 * wp, chunk(c)] += rowsum(h3 * h3)
            return carry

        loop(0, FR, h3_stats)
        s1 = live_total(sacc[0:wp]) * (1.0 / n_local)
        s2 = live_total(sacc[wp : 2 * wp])
        mean3[b], inv3[b] = moments(pivot + s1, s2 - n_local * s1 * s1, True, None)

    def second_in():
        nonlocal cp2
        cp2 = swap_in(gout)

    cp2 = None
    block_forward(0, a0, second_in)

    g3, b3 = wvec(wgain, 0), wvec(wbias, 0)
    sc, sh = g3 * inv3[0], b3 - mean3[0] * g3 * inv3[0]

    def to_a1(f, carry):
        left = u2b[0, rows(f)]
        for c in range(chunks):
            s = slice(c * 256, c * 256 + 256)
            h3 = dot_nn(left, w3[0, :, chunk(c)])
            pre = flat(a0, f, c).astype(F32) + (h3 * sc[:, s] + sh[:, s])
            put(a1, f, c, silu(pre).astype(BF16))
        return carry

    loop(0, FR, to_a1)

    def none():
        pass

    own_cp.wait()
    cp2.wait()
    gather_into(pbuf)
    block_forward(1, a1, none)

    g3, b3 = wvec(wgain, 1), wvec(wbias, 1)
    nxhat = mean3[1] * inv3[1]
    sacc[...] = jnp.zeros(sacc.shape, F32)

    def out_copy(f, dst):
        slot = lax.rem(f, 2)
        return pltpu.make_async_copy(ost.at[slot], dst.at[f], out_sem.at[slot])

    def turn(f, carry):
        @pl.when(f >= 2)
        def _():
            out_copy(f - 2, a2w).wait()

        slot = lax.rem(f, 2)
        left = u2b[1, rows(f)]
        for c in range(chunks):
            s = slice(c * 256, c * 256 + 256)
            h3 = dot_nn(left, w3[1, :, chunk(c)])
            xhat = h3 * inv3[1][:, s] - nxhat[:, s]
            pre = flat(a1, f, c).astype(F32) + (xhat * g3[:, s] + b3[:, s])
            act, slope = silu_and_slope(pre)
            ost[slot, :, :, chunk(c)] = act.astype(BF16).reshape(hh, wp, 256)[:, 0:ww]
            grad = flat(pbuf, f, c).astype(F32) * slope
            put(pbuf, f, c, grad.astype(BF16))
            sacc[0:wp, chunk(c)] += rowsum(grad)
            sacc[wp : 2 * wp, chunk(c)] += rowsum(grad * xhat)
        out_copy(f, a2w).start()
        return carry

    loop(0, FR, turn)
    out_copy(FR - 2, a2w).wait()
    out_copy(FR - 1, a2w).wait()

    def swap_out(src, dst, i):
        cp = pltpu.make_async_remote_copy(
            src_ref=src.at[pl.ds((1 - odd) * (FR - extra), extra)],
            dst_ref=dst,
            send_sem=rem_sem.at[2 + i],
            recv_sem=rem_sem.at[4 + i],
            device_id=sib,
            device_id_type=MESH,
        )
        cp.start()
        return cp

    ret_a = swap_out(a2w, a2r, 0)
    sum_p, sum_px = live_total(sacc[0:wp]), live_total(sacc[wp : 2 * wp])

    def put_out(src, dst, i):
        cp = pltpu.make_async_copy(src, dst, wout_sem.at[i])
        cp.start()
        return cp

    pending = {}

    def block_backward(b):
        nonlocal sum_p, sum_px
        act_src = a1 if b else a0
        s0, s1 = sums(sum_p, sum_px, True, None)
        o_wb[b : b + 1] = s0
        o_wg[b : b + 1] = s1
        k3 = wvec(wgain, b) * inv3[b]
        c0, c1 = s0 * (1.0 / n_total), s1 * (1.0 / n_total)
        ch = k3 * c1 * inv3[b]
        cc = ch * mean3[b] - k3 * c0
        g2, b2 = vec(ngain, b, 1), vec(nbias, b, 1)
        sacc[0 : 2 * wp, 0:bot] = jnp.zeros((2 * wp, bot), F32)
        if 3 in pending:
            pending.pop(3).wait()
        wacc[0] = jnp.zeros((bot, width), F32)

        def to_z2(f, carry):
            left = u2b[b, rows(f)]
            for c in range(chunks):
                s = slice(c * 256, c * 256 + 256)
                h3 = dot_nn(left, w3[b, :, chunk(c)])
                dh3 = flat(pbuf, f, c).astype(F32) * k3[:, s] - h3 * ch[:, s] + cc[:, s]
                tile[:, chunk(c)] = dh3.astype(BF16)
            du2 = dot_nt(tile[...], w3[b])
            for c in range(chunks):
                wacc[0, :, chunk(c)] += dot_tn(left, tile[:, chunk(c)])
            xhat = x2b[b, rows(f)].astype(F32)
            _, slope = silu_and_slope(xhat * g2 + b2)
            z = du2 * slope
            st_h(f, z)
            sacc[0:wp, 0:bot] += rowsum(z)
            sacc[wp : 2 * wp, 0:bot] += rowsum(z * xhat)
            return carry

        loop(0, FR, to_z2)
        pending[3] = put_out(wacc.at[0], o_w3.at[b], 0)
        s0, s1 = sums(live_total(sacc[0:wp, 0:bot]), live_total(sacc[wp : 2 * wp, 0:bot]), False)
        o_nb[b, 1:2] = s0
        o_ng[b, 1:2] = s1
        k2 = g2 * inv2[b]
        c0, c1 = s0 * (1.0 / n_total), s1 * (1.0 / n_total)

        def to_ddw(f, carry):
            xhat = x2b[b, rows(f)].astype(F32)
            st_conv(dbuf, f + 1, masked(k2 * (ld_h(f) - c0 - xhat * c1)))
            return carry

        edge_first(to_ddw)
        cps = send_halos(dbuf, 2)
        loop(1, FR - 1, to_ddw)
        load_taps(b)

        def conv_back(f, carry):
            conv_frame(dbuf, None, f, True)
            return carry

        loop(1, FR - 1, conv_back)
        for cp in cps:
            cp.wait()
        conv_back(0, 0)
        conv_back(FR - 1, 0)
        g1, b1 = vec(ngain, b, 0), vec(nbias, b, 0)
        sacc[0 : 2 * wp, 0:bot] = jnp.zeros((2 * wp, bot), F32)
        if 2 in pending:
            pending.pop(2).wait()
        w2acc[...] = jnp.zeros((bot, bot), F32)

        def to_z1(f, carry):
            dh2 = ld_h(f).astype(BF16)
            xhat = x1b[b, rows(f)].astype(F32)
            act, slope = silu_and_slope(xhat * g1 + b1)
            u1 = masked(act).astype(BF16)
            w2acc[...] += dot_tn(u1, dh2)
            z = dot_nt(dh2, w2[b]) * slope
            st_h(f, z)
            sacc[0:wp, 0:bot] += rowsum(z)
            sacc[wp : 2 * wp, 0:bot] += rowsum(z * xhat)
            return carry

        loop(0, FR, to_z1)
        pending[2] = put_out(w2acc, o_w2.at[b], 1)

        def tap_grads():
            kacc[...] = jnp.zeros(kacc.shape, F32)

            def frame(f, carry):
                def half(h, carry2):
                    for dt in range(3):
                        acc = [None] * 9
                        for y in range(hh):
                            for s in range(2):
                                base = lead + (y + 1) * wp + s * 8
                                gv = dbuf[h, pl.ds(pl.multiple_of(f * stride, 8) + stride + base, 8)]
                                for dy in range(3):
                                    for dx in range(3):
                                        off = lead + dt * stride + (y + dy) * wp + dx - 1 + s * 8
                                        v = cbuf[b, h, pl.ds(f * stride + off, 8)] * gv
                                        i = dy * 3 + dx
                                        acc[i] = v if acc[i] is None else acc[i] + v
                        for i in range(9):
                            val = acc[i]
                            if dt == 0:
                                val = val * okmask[0, f]
                            if dt == 2:
                                val = val * okmask[1, f]
                            kacc[h, dt * 9 + i] += val
                    return carry2

                loop(0, 2, half)
                return carry

            loop(0, FR, frame)
            for h in range(2):
                o_k[b, :, h * 128 : h * 128 + 128] = jnp.sum(kacc[h], axis=1)

        s0, s1 = sums(
            live_total(sacc[0:wp, 0:bot]), live_total(sacc[wp : 2 * wp, 0:bot]), False, tap_grads
        )
        o_nb[b, 0:1] = s0
        o_ng[b, 0:1] = s1
        k1 = g1 * inv1[b]
        c0, c1 = s0 * (1.0 / n_total), s1 * (1.0 / n_total)

        def to_dh1(f, carry):
            xhat = x1b[b, rows(f)].astype(F32)
            dhb[rows(f)] = masked(k1 * (ld_h(f) - c0 - xhat * c1)).astype(BF16)
            return carry

        loop(0, FR, to_dh1)

        def w1_grad():
            if 1 in pending:
                pending.pop(1).wait()
            wacc[1] = jnp.zeros((bot, width), F32)

            def to_w1(f, carry):
                left = dhb[rows(f)]
                for c in range(chunks):
                    wacc[1, :, chunk(c)] += dot_tn(left, flat(act_src, f, c))
                return carry

            loop(0, FR, to_w1)
            pending[1] = put_out(wacc.at[1], o_w1t.at[b], 2)

        return w1_grad

    w1_grad = block_backward(1)
    g3, b3 = wvec(wgain, 0), wvec(wbias, 0)
    nxhat = mean3[0] * inv3[0]
    sacc[...] = jnp.zeros(sacc.shape, F32)

    def middle(f, carry):
        left = u2b[0, rows(f)]
        dh1 = dhb[rows(f)]
        for c in range(chunks):
            s = slice(c * 256, c * 256 + 256)
            grad = dot_nt(dh1, w1[1, chunk(c), :]) + flat(pbuf, f, c).astype(F32)
            h3 = dot_nn(left, w3[0, :, chunk(c)])
            xhat = h3 * inv3[0][:, s] - nxhat[:, s]
            pre = flat(a0, f, c).astype(F32) + (xhat * g3[:, s] + b3[:, s])
            _, slope = silu_and_slope(pre)
            grad = grad * slope
            put(pbuf, f, c, grad.astype(BF16))
            sacc[0:wp, chunk(c)] += rowsum(grad)
            sacc[wp : 2 * wp, chunk(c)] += rowsum(grad * xhat)
        return carry

    loop(0, FR, middle)
    sum_p, sum_px = live_total(sacc[0:wp]), live_total(sacc[wp : 2 * wp])
    w1_grad()
    w1_grad = block_backward(0)

    def last(f, carry):
        @pl.when(f >= 2)
        def _():
            out_copy(f - 2, gw).wait()

        slot = lax.rem(f, 2)
        dh1 = dhb[rows(f)]
        for c in range(chunks):
            grad = dot_nt(dh1, w1[0, chunk(c), :]) + flat(pbuf, f, c).astype(F32)
            ost[slot, :, :, chunk(c)] = grad.astype(BF16).reshape(hh, wp, 256)[:, 0:ww]
        out_copy(f, gw).start()
        return carry

    loop(0, FR, last)
    out_copy(FR - 2, gw).wait()
    out_copy(FR - 1, gw).wait()
    ret_g = swap_out(gw, gr, 1)
    w1_grad()
    for i in (1, 2, 3):
        pending.pop(i).wait()
    ret_a.wait()
    ret_g.wait()


def run_main(dims, held, okmask, frames, gout, w1, w2, w3, taps, ngain, nbias, wgain, wbias):
    n_col, n_ta, cap, hh, ww, width, bot = dims
    n_dev = n_col * n_ta
    extra = cap - FR
    rf = hh * 16
    conv_rows = 8 + (FR + 2) * (hh + 2) * 16 + 8
    conv_rows = -(-conv_rows // 64) * 64
    sds = jax.ShapeDtypeStruct
    outs = (
        sds((FR, hh, ww, width), BF16),
        sds((extra, hh, ww, width), BF16),
        sds((FR, hh, ww, width), BF16),
        sds((extra, hh, ww, width), BF16),
        sds((2, bot, width), F32),
        sds((2, bot, bot), F32),
        sds((2, bot, width), F32),
        sds((2, 27, bot), F32),
        sds((2, 2, bot), F32),
        sds((2, 2, bot), F32),
        sds((2, width), F32),
        sds((2, width), F32),
    )
    vm = pltpu.VMEM
    dma = pltpu.SemaphoreType.DMA
    scratch = [
        vm((cap + extra, hh, ww, width), BF16),
        vm((FR, hh, 16, width), BF16),
        vm((FR, hh, 16, width), BF16),
        vm((FR, hh, 16, width), BF16),
        vm((rf, width), BF16),
        vm((2, hh, ww, width), BF16),
        vm((2, FR * rf, bot), BF16),
        vm((2, FR * rf, 128), F32),
        vm((2, FR * rf, bot), BF16),
        vm((2, FR * rf, bot), BF16),
        vm((2, 2, conv_rows, 128), F32),
        vm((2, conv_rows, 128), F32),
        vm((FR * rf, bot), BF16),
        vm((2, bot, width), F32),
        vm((bot, bot), F32),
        vm((2, 27, 8, 128), F32),
        vm((2, n_dev, 2, bot), F32),
        vm((2, n_ta, 2, width), F32),
        vm((2, n_col, 2, width), F32),
        vm((32, width), F32),
        vm((2, 32, 128), F32),
        dma((1,)),
        dma((6,)),
        dma((3, 2, 2)),
        dma((2,)),
        dma((3,)),
        dma((2,)),
        dma((2,)),
        dma((2,)),
        dma((2,)),
        dma((2,)),
        dma((2,)),
    ]
    return pl.pallas_call(
        functools.partial(main_kernel, dims),
        out_shape=outs,
        in_specs=[SM, SM, ANY, ANY] + [VM] * 8,
        out_specs=(ANY,) * 7 + (VM,) * 5,
        scratch_shapes=scratch,
        compiler_params=pltpu.CompilerParams(
            collective_id=0, has_side_effects=True, vmem_limit_bytes=66_000_000
        ),
        name="blocks",
    )(held, okmask, frames, gout, w1, w2, w3, taps, ngain, nbias, wgain, wbias)


def place_kernel(dims, where, a2w, a2r, gw, gr, out, grad, zero, sem):
    cap = dims[2]
    extra = cap - FR
    zero[...] = jnp.zeros(zero.shape, BF16)
    odd, first = where[0], where[1]
    live = jnp.where(odd == 0, first, 2 * FR - first)

    def each(j, act):
        pos = jnp.where(odd == 0, j, first + j)
        mine = jnp.where(odd == 0, pos < FR, pos >= FR)
        own = jnp.where(odd == 0, pos, pos - FR)
        far = jnp.where(odd == 0, pos - FR, pos - (FR - extra))
        for i, (work, back, dst) in enumerate(((a2w, a2r, out), (gw, gr, grad))):

            @pl.when((j < live) & mine)
            def _():
                act(pltpu.make_async_copy(work.at[own], dst.at[j], sem.at[i]))

            @pl.when((j < live) & jnp.logical_not(mine))
            def _():
                act(pltpu.make_async_copy(back.at[far], dst.at[j], sem.at[i]))

            @pl.when(j >= live)
            def _():
                act(pltpu.make_async_copy(zero, dst.at[j], sem.at[i]))

    def start(j, carry):
        each(j, lambda cp: cp.start())
        return carry

    loop(0, cap, start)
    pltpu.make_async_copy(out, out, sem.at[0]).wait()
    pltpu.make_async_copy(grad, grad, sem.at[1]).wait()


def place(dims, where, a2w, a2r, gw, gr):
    n_col, n_ta, cap, hh, ww, width, bot = dims
    sds = jax.ShapeDtypeStruct
    return pl.pallas_call(
        functools.partial(place_kernel, dims),
        out_shape=(sds((cap, hh, ww, width), BF16),) * 2,
        in_specs=[SM] + [ANY] * 4,
        out_specs=(ANY, ANY),
        scratch_shapes=[pltpu.VMEM((hh, ww, width), BF16), pltpu.SemaphoreType.DMA((2,))],
        name="place",
    )(where, a2w, a2r, gw, gr)


def body(
    n_col,
    n_ta,
    frames,
    out_grad,
    held,
    clip_stride,
    w_reduce,
    w_mid,
    depth_kernel,
    w_expand,
    narrow_gain,
    narrow_bias,
    wide_gain,
    wide_bias,
):
    cap, hh, ww, width = frames.shape
    dims = (n_col, n_ta, cap, hh, ww, width, w_mid.shape[1])
    col, ta = lax.axis_index("col"), lax.axis_index("ta")
    odd = lax.rem(ta, 2)
    lengths = 8 // lax.dynamic_index_in_dim(clip_stride, col, 0, keepdims=False)
    clips = lengths.shape[0]
    before = jnp.arange(clips)[:, None] < jnp.arange(clips)[None, :]
    starts = jnp.sum(jnp.where(before, lengths[:, None], 0), axis=0)
    ids = ta * FR + jnp.arange(FR + 1)
    begins = jnp.any(starts[None, :] == ids[:, None], axis=1) | (ids >= n_ta * FR)
    ok = jnp.logical_not(begins).astype(F32)
    okmask = jnp.stack([ok[:-1], ok[1:]])
    (a2w, a2r, gw, gr, g_w1t, g_w2, g_w3, g_k, g_ng, g_nb, g_wg, g_wb) = run_main(
        dims,
        held,
        okmask,
        frames,
        out_grad,
        w_reduce,
        w_mid,
        w_expand,
        depth_kernel,
        narrow_gain,
        narrow_bias,
        wide_gain,
        wide_bias,
    )
    where = jnp.stack([odd, held[col, ta - odd]]).astype(jnp.int32)
    out, grad = place(dims, where, a2w, a2r, gw, gr)
    g_w1t, g_w2, g_w3, g_k = lax.psum((g_w1t, g_w2, g_w3, g_k), ("col", "ta"))
    return (
        out,
        grad,
        jnp.swapaxes(g_w1t, 1, 2),
        g_w2,
        g_k,
        g_w3,
        g_ng,
        g_nb,
        g_wg,
        g_wb,
    )


def solution(mesh):
    split = P(("col", "ta"), None, None, None)
    return jax.shard_map(
        functools.partial(body, mesh.shape["col"], mesh.shape["ta"]),
        mesh=mesh,
        in_specs=(split, split) + (P(),) * 10,
        out_specs=(split, split) + (P(),) * 8,
        check_vma=False,
    )
```

```python
import functools

import jax
import jax.numpy as jnp
from jax import lax
from jax.experimental import pallas as pl
from jax.experimental.pallas import tpu as pltpu
from jax.sharding import PartitionSpec as P

FR = 12
EPS = 1e-05
MESH = pl.DeviceIdType.MESH
F32 = jnp.float32
BF16 = jnp.bfloat16
ANY = pl.BlockSpec(memory_space=pl.ANY)
VM = pl.BlockSpec(memory_space=pltpu.VMEM)
SM = pl.BlockSpec(memory_space=pltpu.SMEM)


def loop(low, high, step):
    lax.fori_loop(low, high, step, 0)


def dot_nn(left, right):
    return lax.dot_general(left, right, (((1,), (0,)), ((), ())), preferred_element_type=F32)


def dot_nt(left, right):
    return lax.dot_general(left, right, (((1,), (1,)), ((), ())), preferred_element_type=F32)


def dot_tn(left, right):
    return lax.dot_general(left, right, (((0,), (0,)), ((), ())), preferred_element_type=F32)


def silu(values):
    half = 0.5 * values
    return half * jnp.tanh(half) + half


def silu_and_slope(values):
    half = 0.5 * values
    tan = jnp.tanh(half)
    act = half * tan + half
    sig = 0.5 * tan + 0.5
    return act, act + sig * (1.0 - act)


def main_kernel(
    dims,
    held,
    okmask,
    frames,
    gout,
    w1,
    w2,
    w3,
    taps,
    ngain,
    nbias,
    wgain,
    wbias,
    a2w,
    a2r,
    gw,
    gr,
    o_pa,
    o_pb,
    o_ng,
    o_nb,
    o_wg,
    o_wb,
    pool,
    a0,
    a1,
    pbuf,
    tile,
    ost,
    u2b,
    hbuf,
    x1b,
    x2b,
    cbuf,
    dbuf,
    wacc,
    w2acc,
    kacc,
    ksum,
    nbuf,
    tbuf,
    gbuf,
    sacc,
    prm,
    pa_bufs,
    pb_bufs,
    in_sem,
    rem_sem,
    halo_sem,
    out_sem,
    pa_sem,
    pb_sem,
    ns_sem,
    nr_sem,
    ts_sem,
    tr_sem,
    gs_sem,
    gr_sem,
):
    n_col, n_ta, cap, hh, ww, width, bot = dims
    n_dev = n_col * n_ta
    extra = cap - FR
    wp = 16
    rf = hh * wp
    stride = (hh + 2) * wp
    lead = 8
    n_local = float(FR * hh * ww)
    n_total = n_local * n_dev
    chunks = width // 256
    col, ta = lax.axis_index("col"), lax.axis_index("ta")
    me = col * n_ta + ta
    odd = lax.rem(ta, 2)
    sib = (col, ta + 1 - 2 * odd)
    nxt = (col, lax.rem(ta + 1, n_ta))
    prv = (col, lax.rem(ta + n_ta - 1, n_ta))

    def peer(k):
        other = lax.rem(me + k, n_dev)
        return (lax.div(other, n_ta), lax.rem(other, n_ta))

    own_cp = pltpu.make_async_copy(frames, pool.at[pl.ds(0, cap)], in_sem.at[0])
    own_cp.start()
    barrier = pltpu.get_barrier_semaphore()

    def greet(k, carry):
        pl.semaphore_signal(barrier, inc=1, device_id=peer(k), device_id_type=MESH)
        return carry

    loop(1, n_dev, greet)

    live_row = (lax.broadcasted_iota(jnp.int32, (wp, 1), 0) < ww).astype(F32)

    def masked(values):
        c = values.shape[-1]
        return (values.reshape(-1, wp, c) * live_row[None]).reshape(-1, c)

    def rowsum(values):
        return jnp.sum(values.reshape(-1, wp, values.shape[-1]), axis=0)

    def live_total(acc):
        return jnp.sum(acc * live_row, axis=0, keepdims=True)

    def zero_tile(f, carry):
        a0[f] = jnp.zeros((hh, wp, width), BF16)
        pbuf[f] = jnp.zeros((hh, wp, width), BF16)
        return carry

    loop(0, FR, zero_tile)
    for ref in (cbuf.at[0], cbuf.at[1], dbuf):

        def zero_conv(i, carry, ref=ref):
            for h in range(2):
                ref[h, pl.ds(pl.multiple_of(i * 64, 64), 64)] = jnp.zeros((64, 128), F32)
            return carry

        loop(0, ref.shape[1] // 64, zero_conv)

    pl.semaphore_wait(barrier, n_dev - 1)

    def swap_in(src):
        cp = pltpu.make_async_remote_copy(
            src_ref=src.at[pl.ds((1 - odd) * FR, extra)],
            dst_ref=pool.at[pl.ds(cap, extra)],
            send_sem=rem_sem.at[0],
            recv_sem=rem_sem.at[1],
            device_id=sib,
            device_id_type=MESH,
        )
        cp.start()
        return cp

    first_held = held[col, ta - odd]

    def gather_into(dst):
        def pick_frame(j, carry):
            own = jnp.where(odd == 0, j, j + FR - first_held)
            far = jnp.where(odd == 0, j - first_held, j)
            mine = jnp.where(odd == 0, j < first_held, own >= 0)
            pick = jnp.where(mine, jnp.clip(own, 0, cap - 1), cap + jnp.clip(far, 0, extra - 1))
            dst[j, :, 0:ww, :] = pool[pick]
            return carry

        loop(0, FR, pick_frame)

    cp = swap_in(frames)
    own_cp.wait()
    cp.wait()
    gather_into(a0)
    own_cp = pltpu.make_async_copy(gout, pool.at[pl.ds(0, cap)], in_sem.at[0])
    own_cp.start()

    def along_ta(k):
        return (col, lax.rem(ta + k, n_ta))

    def along_col(k):
        return (lax.rem(col + k, n_col), ta)

    stages = {
        "all": (nbuf, ns_sem, nr_sem, n_dev, me, peer),
        "ta": (tbuf, ts_sem, tr_sem, n_ta, ta, along_ta),
        "col": (gbuf, gs_sem, gr_sem, n_col, col, along_col),
    }
    used = {"all": 0, "ta": 0, "col": 0}

    def exchange(name, values, between=None):
        buf, ssem, rsem, size, mine, who = stages[name]
        par = used[name] % 2
        used[name] += 1
        lanes = pl.ds(0, values.shape[1])
        buf[par, mine, :, lanes] = values

        def send(k, carry):
            pltpu.make_async_remote_copy(
                src_ref=buf.at[par, mine, :, lanes],
                dst_ref=buf.at[par, mine, :, lanes],
                send_sem=ssem.at[par],
                recv_sem=rsem.at[par],
                device_id=who(k),
                device_id_type=MESH,
            ).start()
            return carry

        loop(1, size, send)
        if between is not None:
            between()
        part = buf.at[par, pl.ds(0, size - 1), :, lanes]
        pltpu.make_async_copy(part, part, rsem.at[par]).wait()
        pltpu.make_async_copy(part, part, ssem.at[par]).wait()
        return buf[par, :, :, lanes]

    def merge(name, mean_l, m2_l, per, size, between=None):
        got = exchange(name, jnp.concatenate([mean_l, m2_l], axis=0), between)
        total = jnp.sum(got, axis=0)
        mean = total[0:1] * (1.0 / size)
        dev = got - mean[None]
        spread = jnp.sum(dev * dev, axis=0)[0:1]
        return mean, total[1:2] + per * spread

    def moments(mean_l, m2_l, wide, between=None):
        if wide or n_dev > 64:
            mean, m2 = merge("ta", mean_l, m2_l, n_local, n_ta, between)
            mean, m2 = merge("col", mean, m2, n_local * n_ta, n_col)
        else:
            mean, m2 = merge("all", mean_l, m2_l, n_local, n_dev, between)
        return mean, lax.rsqrt(m2 * (1.0 / n_total) + EPS)

    def sums(s0, s1, wide, between=None, later=None):
        total = jnp.concatenate([s0, s1], axis=0)
        if wide or n_dev > 64:
            total = jnp.sum(exchange("ta", total, between), axis=0)
            total = jnp.sum(exchange("col", total, later), axis=0)
        else:
            total = jnp.sum(exchange("all", total, between), axis=0)
        return total[0:1], total[1:2]

    def rows(f):
        return pl.ds(pl.multiple_of(f * rf, rf), rf)

    def ld_h(f):
        return jnp.concatenate([hbuf[0, rows(f)], hbuf[1, rows(f)]], axis=1)

    def st_h(f, values):
        hbuf[0, rows(f)] = values[:, :128]
        hbuf[1, rows(f)] = values[:, 128:]

    def conv_rows(slot):
        return pl.ds(pl.multiple_of(lead + slot * stride + wp, 8), rf)

    def st_conv(ref, slot, values):
        ref[0, conv_rows(slot)] = values[:, :128]
        ref[1, conv_rows(slot)] = values[:, 128:]

    def local_m2(mean_l):
        sacc[0:wp, 0:bot] = jnp.zeros((wp, bot), F32)

        def to_m2(f, carry):
            d = ld_h(f) - mean_l
            sacc[0:wp, 0:bot] += rowsum(d * d)
            return carry

        loop(0, FR, to_m2)
        return live_total(sacc[0:wp, 0:bot])

    def conv_frame(src, wrow, f, flip):
        def half(h, carry):
            wts = []
            w_all = prm[h]
            for dt in range(3):
                scale = None
                if dt == 0:
                    scale = okmask[0, f]
                if dt == 2:
                    scale = okmask[1, f]
                for sp in range(9):
                    idx = dt * 9 + sp
                    row = w_all[26 - idx : 27 - idx] if flip else w_all[idx : idx + 1]
                    if scale is not None:
                        row = row * scale
                    wts.append(jnp.broadcast_to(row, (8, 128)))
            out = []
            for y in range(hh):
                for s in range(2):
                    acc = [None, None, None]
                    for dt in range(3):
                        for dy in range(3):
                            for dx in range(3):
                                off = lead + dt * stride + (y + dy) * wp + dx - 1 + s * 8
                                v = src[h, pl.ds(f * stride + off, 8)]
                                term = v * wts[dt * 9 + dy * 3 + dx]
                                acc[dx] = term if acc[dx] is None else acc[dx] + term
                    val = acc[0] + acc[1] + acc[2]
                    hbuf[h, pl.ds(pl.multiple_of(f * rf + y * wp + s * 8, 8), 8)] = val
            return carry

        loop(0, 2, half)

    def load_taps(b):
        k = taps[b].astype(F32)
        prm[0, 0:27] = k[:, :128]
        prm[1, 0:27] = k[:, 128:]

    def send_halos(ref, which):
        cps = []
        for i, (slot, land, dev) in enumerate(((1, FR + 1, prv), (FR, 0, nxt))):
            cp = pltpu.make_async_remote_copy(
                src_ref=ref.at[:, pl.ds(lead + slot * stride + wp, rf)],
                dst_ref=ref.at[:, pl.ds(lead + land * stride + wp, rf)],
                send_sem=halo_sem.at[which, i, 0],
                recv_sem=halo_sem.at[which, i, 1],
                device_id=dev,
                device_id_type=MESH,
            )
            cp.start()
            cps.append(cp)
        return cps

    def edge_first(step):
        step(0, 0)
        step(FR - 1, 0)

    def chunk(c):
        return pl.ds(c * 256, 256)

    def flat(ref, f, c):
        return ref[f, :, :, chunk(c)].reshape(rf, 256)

    def put(ref, f, c, values):
        ref[f, :, :, chunk(c)] = values.reshape(hh, wp, 256)

    nz = n_ta // 2
    zpos = lax.div(ta, 2)
    if n_dev == 32:
        first = col * nz + zpos
        levels = [
            (
                n_dev // 2,
                16,
                first,
                lambda i: (lax.div(i, nz), 2 * lax.rem(i, nz) + odd),
            )
        ]
    else:
        levels = [
            (n_col, 4, col, lambda i: (i, ta)),
            (nz, 4, zpos, lambda i: (col, 2 * i + odd)),
        ]

    def package(bufs, sems, dst):
        send, land, final = bufs[0], bufs[1], bufs[2]
        halls = bufs[3:]

        def remote(src, to, i, dev):
            return pltpu.make_async_remote_copy(
                src_ref=src,
                dst_ref=to,
                send_sem=sems.at[2 * i],
                recv_sem=sems.at[2 * i + 1],
                device_id=dev,
                device_id_type=MESH,
            )

        cp = remote(send.at[1 - odd], land, 0, sib)
        cp.start()
        yield
        cp.wait()

        def add(r, carry):
            both = send[odd, r].astype(F32) + land[r].astype(F32)
            send[odd, r] = both.astype(BF16)
            return carry

        loop(0, 16, add)
        off, size = 0, 16
        spans = []
        for i, (n, m, mine, who) in enumerate(levels):
            hall = halls[i]
            size = size // m

            def scatter(k, carry, hall=hall, size=size, off=off, n=n, m=m, mine=mine, who=who, i=i):
                other = lax.rem(mine + k, n)
                part = send.at[odd, pl.ds(off + lax.rem(other, m) * size, size)]
                remote(part, hall.at[mine], 1 + i, who(other)).start()
                return carry

            loop(1, n, scatter)
            off = off + lax.rem(mine, m) * size
            hall[mine] = send[odd, pl.ds(off, size)]
            yield
            part = hall.at[pl.ds(0, n - 1)]
            pltpu.make_async_copy(part, part, sems.at[3 + 2 * i]).wait()
            pltpu.make_async_copy(part, part, sems.at[2 + 2 * i]).wait()
            last = i == len(levels) - 1

            def reduce(q, carry, hall=hall, n=n, off=off, last=last):
                total = jnp.sum(hall[:, q].astype(F32), axis=0).astype(BF16)
                if last:
                    final[odd, off + q] = total
                else:
                    send[odd, off + q] = total
                return carry

            loop(0, size, reduce)
            spans.append((off, size))
        base = 1 + len(levels)
        for i in reversed(range(len(levels))):
            n, m, mine, who = levels[i]
            off, size = spans[i]

            def spread(k, carry, off=off, size=size, m=m, mine=mine, who=who, i=i):
                other = lax.div(mine, m) * m + lax.rem(lax.rem(mine, m) + k, m)
                part = final.at[odd, pl.ds(off, size)]
                remote(part, part, base + i, who(other)).start()
                return carry

            loop(1, m, spread)
            yield
            part = final.at[odd, pl.ds(0, (m - 1) * size)]
            pltpu.make_async_copy(part, part, sems.at[2 * (base + i) + 1]).wait()
            pltpu.make_async_copy(part, part, sems.at[2 * (base + i)]).wait()
        cp = remote(final.at[odd], final.at[odd], base + len(levels), sib)
        cp.start()
        yield
        cp.wait()
        cp = pltpu.make_async_copy(final, dst, sems.at[2 * (base + len(levels)) + 2])
        cp.start()
        yield
        cp.wait()
        yield

    def finish(gen):
        for _ in gen:
            pass

    def advance(*gens):
        for gen in gens:
            next(gen, None)

    ksum[...] = jnp.zeros(ksum.shape, F32)
    pa_bufs[0][...] = jnp.zeros(pa_bufs[0].shape, BF16)
    half_w = width // 2

    def pack_a():
        def step(r, carry):
            rr = pl.ds(pl.multiple_of(r * 16, 16), 16)
            for p in range(2):
                pa_bufs[0][p, r, :, 0:half_w] = wacc[rr, p * half_w : p * half_w + half_w].astype(BF16)
                pa_bufs[0][p, r, :, half_w : half_w + 128] = w2acc[rr, p * 128 : p * 128 + 128].astype(BF16)
            return carry

        loop(0, 16, step)
        for p in range(2):
            for r in range(2):
                pa_bufs[0][p, r, :, half_w + 128 :] = ksum[p, r * 16 : r * 16 + 16].astype(BF16)

    def pack_b():
        def step(r, carry):
            rr = pl.ds(pl.multiple_of(r * 16, 16), 16)
            for p in range(2):
                pb_bufs[0][p, r] = wacc[rr, p * half_w : p * half_w + half_w].astype(BF16)
            return carry

        loop(0, 16, step)

    def first_mm(src, b):
        sacc[0:wp, 0:bot] = jnp.zeros((wp, bot), F32)

        def to_h1(f, carry):
            h1 = dot_nn(src[f].reshape(rf, width), w1[b])
            st_h(f, h1)
            sacc[0:wp, 0:bot] += rowsum(h1)
            return carry

        loop(0, FR, to_h1)
        mean_l = live_total(sacc[0:wp, 0:bot]) * (1.0 / n_local)
        return mean_l, local_m2(mean_l)

    inv1, inv2, mean3, inv3 = {}, {}, {}, {}

    def vec(ref, b, j):
        return ref[b].astype(F32)[j : j + 1]

    def wvec(ref, b):
        return ref[...].astype(F32)[b : b + 1]

    def get_gout():
        own_cp.wait()

    def block_forward(b, src, after_first):
        mean_l, m2_l = first_mm(src, b)
        mean, inv = moments(mean_l, m2_l, False, None)
        inv1[b] = inv
        after_first()
        g, bb = vec(ngain, b, 0), vec(nbias, b, 0)

        def to_h2(f, carry):
            xhat = (ld_h(f) - mean) * inv
            x1b[b, rows(f)] = xhat.astype(BF16)
            u1 = masked(silu(xhat * g + bb)).astype(BF16)
            h2 = dot_nn(u1, w2[b]).astype(BF16).astype(F32)
            st_conv(cbuf.at[b], f + 1, h2)
            return carry

        edge_first(to_h2)
        cps = send_halos(cbuf.at[b], b)
        loop(1, FR - 1, to_h2)
        load_taps(b)

        def conv_step(f, carry):
            conv_frame(cbuf.at[b], None, f, False)
            return carry

        loop(1, FR - 1, conv_step)
        for cp in cps:
            cp.wait()
        conv_step(0, 0)
        conv_step(FR - 1, 0)
        sacc[0:wp, 0:bot] = jnp.zeros((wp, bot), F32)

        def dw_sum(f, carry):
            sacc[0:wp, 0:bot] += rowsum(ld_h(f))
            return carry

        loop(0, FR, dw_sum)
        mean_l = live_total(sacc[0:wp, 0:bot]) * (1.0 / n_local)
        m2_l = local_m2(mean_l)
        mean, inv = moments(mean_l, m2_l, False, None)
        inv2[b] = inv
        g, bb = vec(ngain, b, 1), vec(nbias, b, 1)
        sacc[0:wp, 0:bot] = jnp.zeros((wp, bot), F32)

        def to_u2(f, carry):
            xhat = (ld_h(f) - mean) * inv
            x2b[b, rows(f)] = xhat.astype(BF16)
            u2 = masked(silu(xhat * g + bb))
            u2b[b, rows(f)] = u2.astype(BF16)
            sacc[0:wp, 0:bot] += rowsum(u2)
            return carry

        loop(0, FR, to_u2)
        u_mean = live_total(sacc[0:wp, 0:bot]) * (1.0 / n_local)
        pivot = dot_nn(jnp.broadcast_to(u_mean, (16, bot)).astype(BF16), w3[b])[0:1]
        sacc[...] = jnp.zeros(sacc.shape, F32)

        def h3_stats(f, carry):
            left = u2b[b, rows(f)]
            for c in range(chunks):
                h3 = dot_nn(left, w3[b, :, chunk(c)]) - pivot[:, c * 256 : c * 256 + 256]
                sacc[0:wp, chunk(c)] += rowsum(h3)
                sacc[wp : 2 * wp, chunk(c)] += rowsum(h3 * h3)
            return carry

        loop(0, FR, h3_stats)
        s1 = live_total(sacc[0:wp]) * (1.0 / n_local)
        s2 = live_total(sacc[wp : 2 * wp])
        mean3[b], inv3[b] = moments(pivot + s1, s2 - n_local * s1 * s1, True, None)

    def second_in():
        nonlocal cp2
        cp2 = swap_in(gout)

    cp2 = None
    block_forward(0, a0, second_in)

    g3, b3 = wvec(wgain, 0), wvec(wbias, 0)
    sc, sh = g3 * inv3[0], b3 - mean3[0] * g3 * inv3[0]

    def to_a1(f, carry):
        left = u2b[0, rows(f)]
        for c in range(chunks):
            s = slice(c * 256, c * 256 + 256)
            h3 = dot_nn(left, w3[0, :, chunk(c)])
            pre = flat(a0, f, c).astype(F32) + (h3 * sc[:, s] + sh[:, s])
            put(a1, f, c, silu(pre).astype(BF16))
        return carry

    loop(0, FR, to_a1)

    def none():
        pass

    own_cp.wait()
    cp2.wait()
    gather_into(pbuf)
    block_forward(1, a1, none)

    g3, b3 = wvec(wgain, 1), wvec(wbias, 1)
    nxhat = mean3[1] * inv3[1]
    sacc[...] = jnp.zeros(sacc.shape, F32)

    def out_copy(f, dst):
        slot = lax.rem(f, 2)
        return pltpu.make_async_copy(ost.at[slot], dst.at[f], out_sem.at[slot])

    def turn(f, carry):
        @pl.when(f >= 2)
        def _():
            out_copy(f - 2, a2w).wait()

        slot = lax.rem(f, 2)
        left = u2b[1, rows(f)]
        for c in range(chunks):
            s = slice(c * 256, c * 256 + 256)
            h3 = dot_nn(left, w3[1, :, chunk(c)])
            xhat = h3 * inv3[1][:, s] - nxhat[:, s]
            pre = flat(a1, f, c).astype(F32) + (xhat * g3[:, s] + b3[:, s])
            act, slope = silu_and_slope(pre)
            ost[slot, :, :, chunk(c)] = act.astype(BF16).reshape(hh, wp, 256)[:, 0:ww]
            grad = flat(pbuf, f, c).astype(F32) * slope
            put(pbuf, f, c, grad.astype(BF16))
            sacc[0:wp, chunk(c)] += rowsum(grad)
            sacc[wp : 2 * wp, chunk(c)] += rowsum(grad * xhat)
        out_copy(f, a2w).start()
        return carry

    loop(0, FR, turn)
    out_copy(FR - 2, a2w).wait()
    out_copy(FR - 1, a2w).wait()

    def swap_out(src, dst, i):
        cp = pltpu.make_async_remote_copy(
            src_ref=src.at[pl.ds((1 - odd) * (FR - extra), extra)],
            dst_ref=dst,
            send_sem=rem_sem.at[2 + i],
            recv_sem=rem_sem.at[4 + i],
            device_id=sib,
            device_id_type=MESH,
        )
        cp.start()
        return cp

    ret_a = swap_out(a2w, a2r, 0)
    sum_p, sum_px = live_total(sacc[0:wp]), live_total(sacc[wp : 2 * wp])

    def block_backward(b, act_src, windows):
        s0, s1 = sums(sum_p, sum_px, True, windows[0], windows[1])
        o_wb[b : b + 1] = s0
        o_wg[b : b + 1] = s1
        k3 = wvec(wgain, b) * inv3[b]
        c0, c1 = s0 * (1.0 / n_total), s1 * (1.0 / n_total)
        ch = k3 * c1 * inv3[b]
        cc = ch * mean3[b] - k3 * c0
        g2, b2 = vec(ngain, b, 1), vec(nbias, b, 1)
        sacc[0 : 2 * wp, 0:bot] = jnp.zeros((2 * wp, bot), F32)
        wacc[...] = jnp.zeros((bot, width), F32)

        def to_z2(f, carry):
            left = u2b[b, rows(f)]
            for c in range(chunks):
                s = slice(c * 256, c * 256 + 256)
                h3 = dot_nn(left, w3[b, :, chunk(c)])
                dh3 = flat(pbuf, f, c).astype(F32) * k3[:, s] - h3 * ch[:, s] + cc[:, s]
                tile[:, chunk(c)] = dh3.astype(BF16)
            du2 = dot_nt(tile[...], w3[b])
            for c in range(chunks):
                wacc[:, chunk(c)] += dot_tn(left, tile[:, chunk(c)])
            xhat = x2b[b, rows(f)].astype(F32)
            _, slope = silu_and_slope(xhat * g2 + b2)
            z = du2 * slope
            st_h(f, z)
            sacc[0:wp, 0:bot] += rowsum(z)
            sacc[wp : 2 * wp, 0:bot] += rowsum(z * xhat)
            return carry

        loop(0, FR, to_z2)
        s0, s1 = sums(
            live_total(sacc[0:wp, 0:bot]), live_total(sacc[wp : 2 * wp, 0:bot]), False, windows[2]
        )
        o_nb[b, 1:2] = s0
        o_ng[b, 1:2] = s1
        k2 = g2 * inv2[b]
        c0, c1 = s0 * (1.0 / n_total), s1 * (1.0 / n_total)

        def to_ddw(f, carry):
            xhat = x2b[b, rows(f)].astype(F32)
            st_conv(dbuf, f + 1, masked(k2 * (ld_h(f) - c0 - xhat * c1)))
            return carry

        edge_first(to_ddw)
        cps = send_halos(dbuf, 2)
        loop(1, FR - 1, to_ddw)
        load_taps(b)

        def conv_back(f, carry):
            conv_frame(dbuf, None, f, True)
            return carry

        loop(1, FR - 1, conv_back)
        windows[3]()
        for cp in cps:
            cp.wait()
        conv_back(0, 0)
        conv_back(FR - 1, 0)
        g1, b1 = vec(ngain, b, 0), vec(nbias, b, 0)
        sacc[0 : 2 * wp, 0:bot] = jnp.zeros((2 * wp, bot), F32)
        w2acc[...] = jnp.zeros((bot, bot), F32)

        def to_z1(f, carry):
            dh2 = ld_h(f).astype(BF16)
            xhat = x1b[b, rows(f)].astype(F32)
            act, slope = silu_and_slope(xhat * g1 + b1)
            u1 = masked(act).astype(BF16)
            w2acc[...] += dot_tn(u1, dh2)
            z = dot_nt(dh2, w2[b]) * slope
            st_h(f, z)
            sacc[0:wp, 0:bot] += rowsum(z)
            sacc[wp : 2 * wp, 0:bot] += rowsum(z * xhat)
            return carry

        loop(0, FR, to_z1)
        def tap_grads():
            kacc[...] = jnp.zeros(kacc.shape, F32)

            def frame(f, carry):
                def half(h, carry2):
                    for dt in range(3):
                        acc = [None] * 9
                        for y in range(hh):
                            for s in range(2):
                                base = lead + (y + 1) * wp + s * 8
                                gv = dbuf[h, pl.ds(pl.multiple_of(f * stride, 8) + stride + base, 8)]
                                for dy in range(3):
                                    for dx in range(3):
                                        off = lead + dt * stride + (y + dy) * wp + dx - 1 + s * 8
                                        v = cbuf[b, h, pl.ds(f * stride + off, 8)] * gv
                                        i = dy * 3 + dx
                                        acc[i] = v if acc[i] is None else acc[i] + v
                        for i in range(9):
                            val = acc[i]
                            if dt == 0:
                                val = val * okmask[0, f]
                            if dt == 2:
                                val = val * okmask[1, f]
                            kacc[h, dt * 9 + i] += val
                    return carry2

                loop(0, 2, half)
                return carry

            loop(0, FR, frame)
            for h in range(2):
                ksum[h, 0:27] = jnp.sum(kacc[h], axis=1)
            windows[4]()
            pack_a()
            gen = package(pa_bufs, pa_sem, o_pa.at[b])
            next(gen)
            made.append(gen)

        made = []

        s0, s1 = sums(
            live_total(sacc[0:wp, 0:bot]), live_total(sacc[wp : 2 * wp, 0:bot]), False, tap_grads
        )
        o_nb[b, 0:1] = s0
        o_ng[b, 0:1] = s1
        k1 = g1 * inv1[b]
        c0, c1 = s0 * (1.0 / n_total), s1 * (1.0 / n_total)

        def to_dh1(f, carry):
            xhat = x1b[b, rows(f)].astype(F32)
            x1b[b, rows(f)] = masked(k1 * (ld_h(f) - c0 - xhat * c1)).astype(BF16)
            return carry

        loop(0, FR, to_dh1)

        def w1_grad():
            wacc[...] = jnp.zeros((bot, width), F32)

            def to_w1(f, carry):
                left = x1b[b, rows(f)]
                for c in range(chunks):
                    wacc[:, chunk(c)] += dot_tn(left, flat(act_src, f, c))
                return carry

            loop(0, FR, to_w1)
            pack_b()
            gen = package(pb_bufs, pb_sem, o_pb.at[b])
            next(gen)
            return gen

        return w1_grad, made[0]

    def nothing():
        pass

    w1_grad, gen_a = block_backward(1, a1, [nothing] * 5)
    g3, b3 = wvec(wgain, 0), wvec(wbias, 0)
    nxhat = mean3[0] * inv3[0]
    sacc[...] = jnp.zeros(sacc.shape, F32)

    def middle(f, carry):
        left = u2b[0, rows(f)]
        dh1 = x1b[1, rows(f)]
        for c in range(chunks):
            s = slice(c * 256, c * 256 + 256)
            grad = dot_nt(dh1, w1[1, chunk(c), :]) + flat(pbuf, f, c).astype(F32)
            h3 = dot_nn(left, w3[0, :, chunk(c)])
            xhat = h3 * inv3[0][:, s] - nxhat[:, s]
            pre = flat(a0, f, c).astype(F32) + (xhat * g3[:, s] + b3[:, s])
            _, slope = silu_and_slope(pre)
            grad = grad * slope
            put(pbuf, f, c, grad.astype(BF16))
            sacc[0:wp, chunk(c)] += rowsum(grad)
            sacc[wp : 2 * wp, chunk(c)] += rowsum(grad * xhat)
        return carry

    loop(0, FR, middle)
    sum_p, sum_px = live_total(sacc[0:wp]), live_total(sacc[wp : 2 * wp])
    gens = [gen_a]

    def window0():
        advance(gen_a)
        gens.append(w1_grad())

    def window1():
        advance(*gens)

    def window4():
        for gen in gens:
            finish(gen)

    w1_last, last_a = block_backward(0, a0, [window0, window1, window1, window1, window4])
    last_b = w1_last()
    advance(last_a)

    def last(f, carry):
        @pl.when(f >= 2)
        def _():
            out_copy(f - 2, gw).wait()

        slot = lax.rem(f, 2)
        dh1 = x1b[0, rows(f)]
        for c in range(chunks):
            grad = dot_nt(dh1, w1[0, chunk(c), :]) + flat(pbuf, f, c).astype(F32)
            ost[slot, :, :, chunk(c)] = grad.astype(BF16).reshape(hh, wp, 256)[:, 0:ww]
        out_copy(f, gw).start()
        return carry

    half_way = FR // 2
    loop(0, half_way, last)
    advance(last_a, last_b)
    loop(half_way, FR, last)
    out_copy(FR - 2, gw).wait()
    out_copy(FR - 1, gw).wait()
    ret_g = swap_out(gw, gr, 1)
    for _ in range(8):
        advance(last_a, last_b)
    finish(last_a)
    finish(last_b)
    ret_a.wait()
    ret_g.wait()


def run_main(dims, held, okmask, frames, gout, w1, w2, w3, taps, ngain, nbias, wgain, wbias):
    n_col, n_ta, cap, hh, ww, width, bot = dims
    n_dev = n_col * n_ta
    extra = cap - FR
    rf = hh * 16
    conv_rows = 8 + (FR + 2) * (hh + 2) * 16 + 8
    conv_rows = -(-conv_rows // 64) * 64
    sds = jax.ShapeDtypeStruct
    la, lb = width // 2 + 256, width // 2

    def piece_bufs(lanes):
        halls = [(16, 1)] if n_dev == 32 else [(n_col, 4), (n_ta // 2, 1)]
        return [
            pltpu.VMEM((2, 16, 16, lanes), BF16),
            pltpu.VMEM((16, 16, lanes), BF16),
            pltpu.VMEM((2, 16, 16, lanes), BF16),
        ] + [pltpu.VMEM((n, size, 16, lanes), BF16) for n, size in halls]

    n_sems = 2 * (2 + 2 * (1 if n_dev == 32 else 2)) + 1
    outs = (
        sds((FR, hh, ww, width), BF16),
        sds((extra, hh, ww, width), BF16),
        sds((FR, hh, ww, width), BF16),
        sds((extra, hh, ww, width), BF16),
        sds((2, 2, 16, 16, la), BF16),
        sds((2, 2, 16, 16, lb), BF16),
        sds((2, 2, bot), F32),
        sds((2, 2, bot), F32),
        sds((2, width), F32),
        sds((2, width), F32),
    )
    vm = pltpu.VMEM
    dma = pltpu.SemaphoreType.DMA
    scratch = [
        vm((cap + extra, hh, ww, width), BF16),
        vm((FR, hh, 16, width), BF16),
        vm((FR, hh, 16, width), BF16),
        vm((FR, hh, 16, width), BF16),
        vm((rf, width), BF16),
        vm((2, hh, ww, width), BF16),
        vm((2, FR * rf, bot), BF16),
        vm((2, FR * rf, 128), F32),
        vm((2, FR * rf, bot), BF16),
        vm((2, FR * rf, bot), BF16),
        vm((2, 2, conv_rows, 128), F32),
        vm((2, conv_rows, 128), F32),
        vm((bot, width), F32),
        vm((bot, bot), F32),
        vm((2, 27, 8, 128), F32),
        vm((2, 32, 128), F32),
        vm((2, n_dev if n_dev <= 64 else 1, 2, bot), F32),
        vm((2, n_ta, 2, width), F32),
        vm((2, n_col, 2, width), F32),
        vm((32, width), F32),
        vm((2, 32, 128), F32),
        piece_bufs(la),
        piece_bufs(lb),
        dma((1,)),
        dma((6,)),
        dma((3, 2, 2)),
        dma((2,)),
        dma((n_sems,)),
        dma((n_sems,)),
        dma((2,)),
        dma((2,)),
        dma((2,)),
        dma((2,)),
        dma((2,)),
        dma((2,)),
    ]
    return pl.pallas_call(
        functools.partial(main_kernel, dims),
        out_shape=outs,
        in_specs=[SM, SM, ANY, ANY] + [VM] * 8,
        out_specs=(ANY,) * 6 + (VM,) * 4,
        scratch_shapes=scratch,
        compiler_params=pltpu.CompilerParams(
            collective_id=0, has_side_effects=True, vmem_limit_bytes=66_500_000
        ),
        name="blocks",
    )(held, okmask, frames, gout, w1, w2, w3, taps, ngain, nbias, wgain, wbias)


def place_kernel(
    cap,
    where,
    a2w,
    a2r,
    gw,
    gr,
    pa,
    pb,
    i_ng,
    i_nb,
    i_wg,
    i_wb,
    out,
    grad,
    o_w1,
    o_w2,
    o_k,
    o_w3,
    o_ng,
    o_nb,
    o_wg,
    o_wb,
    work,
    zero,
    in_sem,
    out_sem,
):
    half = pb.shape[-1]
    extra = cap - FR
    odd, first = where[0], where[1]
    live = jnp.where(odd == 0, first, 2 * FR - first)
    arrays = ((a2w, a2r, out), (gw, gr, grad))

    def source(j):
        pos = jnp.where(odd == 0, j, first + j)
        mine = jnp.where(odd == 0, pos < FR, pos >= FR)
        own = jnp.where(odd == 0, pos, pos - FR)
        far = jnp.where(odd == 0, pos - FR, pos - (FR - extra))
        return mine, own, far

    def fetch(j, carry):
        mine, own, far = source(j)
        for i, (near, back, _) in enumerate(arrays):

            @pl.when((j < live) & mine)
            def _():
                pltpu.make_async_copy(near.at[own], work.at[i, j], in_sem.at[i, j]).start()

            @pl.when((j < live) & jnp.logical_not(mine))
            def _():
                pltpu.make_async_copy(back.at[far], work.at[i, j], in_sem.at[i, j]).start()

        return carry

    loop(0, cap, fetch)
    zero[...] = jnp.zeros(zero.shape, BF16)

    def clear(j, carry):
        for i, (_, _, dst) in enumerate(arrays):
            pltpu.make_async_copy(zero, dst.at[j], out_sem.at[i]).start()
        return carry

    lax.fori_loop(live, cap, clear, 0)

    def ship(j, carry):
        for i, (near, _, dst) in enumerate(arrays):
            pltpu.make_async_copy(near.at[0], work.at[i, j], in_sem.at[i, j]).wait()
            pltpu.make_async_copy(work.at[i, j], dst.at[j], out_sem.at[i]).start()
        return carry

    lax.fori_loop(0, live, ship, 0)
    o_ng[...] = i_ng[...]
    o_nb[...] = i_nb[...]
    o_wg[...] = i_wg[...]
    o_wb[...] = i_wb[...]
    for b in range(2):
        for p in range(2):
            cols = slice(p * 128, p * 128 + 128)
            taps = pa[b, p, 0:2, :, half + 128 :].astype(F32).reshape(32, 128)
            o_k[b, :, cols] = taps[0:27]
            mid = pa[b, p, :, :, half : half + 128].astype(F32)
            o_w2[b, :, cols] = mid.reshape(256, 128)
            cols = slice(p * half, p * half + half)
            o_w3[b, :, cols] = pa[b, p, :, :, 0:half].astype(F32).reshape(256, half)
            o_w1[b, cols, :] = pb[b, p].astype(F32).reshape(256, half).T
    pltpu.make_async_copy(out, out, out_sem.at[0]).wait()
    pltpu.make_async_copy(grad, grad, out_sem.at[1]).wait()


def place(dims, where, *parts):
    n_col, n_ta, cap, hh, ww, width, bot = dims
    sds = jax.ShapeDtypeStruct
    return pl.pallas_call(
        functools.partial(place_kernel, cap),
        out_shape=(sds((cap, hh, ww, width), BF16),) * 2
        + (
            sds((2, width, bot), F32),
            sds((2, bot, bot), F32),
            sds((2, 27, bot), F32),
            sds((2, bot, width), F32),
            sds((2, 2, bot), F32),
            sds((2, 2, bot), F32),
            sds((2, width), F32),
            sds((2, width), F32),
        ),
        in_specs=[SM] + [ANY] * 4 + [VM] * 6,
        out_specs=(ANY, ANY) + (VM,) * 8,
        scratch_shapes=[
            pltpu.VMEM((2, cap, hh, ww, width), BF16),
            pltpu.VMEM((hh, ww, width), BF16),
            pltpu.SemaphoreType.DMA((2, cap)),
            pltpu.SemaphoreType.DMA((2,)),
        ],
        compiler_params=pltpu.CompilerParams(vmem_limit_bytes=64_000_000),
        name="place",
    )(where, *parts)


def body(
    n_col,
    n_ta,
    frames,
    out_grad,
    held,
    clip_stride,
    w_reduce,
    w_mid,
    depth_kernel,
    w_expand,
    narrow_gain,
    narrow_bias,
    wide_gain,
    wide_bias,
):
    cap, hh, ww, width = frames.shape
    dims = (n_col, n_ta, cap, hh, ww, width, w_mid.shape[1])
    col, ta = lax.axis_index("col"), lax.axis_index("ta")
    odd = lax.rem(ta, 2)
    lengths = 8 // lax.dynamic_index_in_dim(clip_stride, col, 0, keepdims=False)
    clips = lengths.shape[0]
    before = jnp.arange(clips)[:, None] < jnp.arange(clips)[None, :]
    starts = jnp.sum(jnp.where(before, lengths[:, None], 0), axis=0)
    ids = ta * FR + jnp.arange(FR + 1)
    begins = jnp.any(starts[None, :] == ids[:, None], axis=1) | (ids >= n_ta * FR)
    ok = jnp.logical_not(begins).astype(F32)
    okmask = jnp.stack([ok[:-1], ok[1:]])
    parts = run_main(
        dims,
        held,
        okmask,
        frames,
        out_grad,
        w_reduce,
        w_mid,
        w_expand,
        depth_kernel,
        narrow_gain,
        narrow_bias,
        wide_gain,
        wide_bias,
    )
    where = jnp.stack([odd, held[col, ta - odd]]).astype(jnp.int32)
    return place(dims, where, *parts)


def solution(mesh):
    split = P(("col", "ta"), None, None, None)
    return jax.shard_map(
        functools.partial(body, mesh.shape["col"], mesh.shape["ta"]),
        mesh=mesh,
        in_specs=(split, split) + (P(),) * 10,
        out_specs=(split, split) + (P(),) * 8,
        check_vma=False,
    )
```

```python
import functools

import jax
import jax.numpy as jnp
from jax import lax
from jax.experimental import pallas as pl
from jax.experimental.pallas import tpu as pltpu
from jax.sharding import PartitionSpec as P

FR = 12
EPS = 1e-05
MESH = pl.DeviceIdType.MESH
F32 = jnp.float32
BF16 = jnp.bfloat16
ANY = pl.BlockSpec(memory_space=pl.ANY)
VM = pl.BlockSpec(memory_space=pltpu.VMEM)
SM = pl.BlockSpec(memory_space=pltpu.SMEM)


def loop(low, high, step):
    lax.fori_loop(low, high, step, 0)


def dot_nn(left, right):
    return lax.dot_general(left, right, (((1,), (0,)), ((), ())), preferred_element_type=F32)


def dot_nt(left, right):
    return lax.dot_general(left, right, (((1,), (1,)), ((), ())), preferred_element_type=F32)


def dot_tn(left, right):
    return lax.dot_general(left, right, (((0,), (0,)), ((), ())), preferred_element_type=F32)


def silu(values):
    half = 0.5 * values
    return half * jnp.tanh(half) + half


def silu_and_slope(values):
    half = 0.5 * values
    tan = jnp.tanh(half)
    act = half * tan + half
    sig = 0.5 * tan + 0.5
    return act, act + sig * (1.0 - act)


def main_kernel(
    dims,
    held,
    okmask,
    frames,
    gout,
    w1,
    w2,
    w3,
    taps,
    ngain,
    nbias,
    wgain,
    wbias,
    a2w,
    a2r,
    gw,
    gr,
    o_pa,
    o_pb,
    o_ng,
    o_nb,
    o_wg,
    o_wb,
    pool,
    a0,
    a1,
    pbuf,
    tile,
    ost,
    u2b,
    hbuf,
    x1b,
    x2b,
    cbuf,
    dbuf,
    wacc,
    w2acc,
    kacc,
    ksum,
    nbuf,
    tbuf,
    gbuf,
    sacc,
    prm,
    pa_bufs,
    pb_bufs,
    in_sem,
    rem_sem,
    halo_sem,
    out_sem,
    pa_sem,
    pb_sem,
    ns_sem,
    nr_sem,
    ts_sem,
    tr_sem,
    gs_sem,
    gr_sem,
):
    n_col, n_ta, cap, hh, ww, width, bot = dims
    n_dev = n_col * n_ta
    extra = cap - FR
    N1, N3, NA, NZ2, NZ1, NW, NM = (3, 2, 2, 1, 3, 4, 2) if n_dev <= 64 else (1,) * 7
    wp = 16
    rf = hh * wp
    stride = (hh + 2) * wp
    lead = 8
    n_local = float(FR * hh * ww)
    n_total = n_local * n_dev
    chunks = width // 256
    col, ta = lax.axis_index("col"), lax.axis_index("ta")
    me = col * n_ta + ta
    odd = lax.rem(ta, 2)
    sib = (col, ta + 1 - 2 * odd)
    nxt = (col, lax.rem(ta + 1, n_ta))
    prv = (col, lax.rem(ta + n_ta - 1, n_ta))

    def peer(k):
        other = lax.rem(me + k, n_dev)
        return (lax.div(other, n_ta), lax.rem(other, n_ta))

    own_cp = pltpu.make_async_copy(frames, pool.at[pl.ds(0, cap)], in_sem.at[0])
    own_cp.start()
    barrier = pltpu.get_barrier_semaphore()

    def greet(k, carry):
        pl.semaphore_signal(barrier, inc=1, device_id=peer(k), device_id_type=MESH)
        return carry

    loop(1, n_dev, greet)

    live_row = (lax.broadcasted_iota(jnp.int32, (wp, 1), 0) < ww).astype(F32)

    def masked(values):
        c = values.shape[-1]
        return (values.reshape(-1, wp, c) * live_row[None]).reshape(-1, c)

    def rowsum(values):
        return jnp.sum(values.reshape(-1, wp, values.shape[-1]), axis=0)

    def live_total(acc):
        return jnp.sum(acc * live_row, axis=0, keepdims=True)

    def zero_tile(f, carry):
        a0[f] = jnp.zeros((hh, wp, width), BF16)
        pbuf[f] = jnp.zeros((hh, wp, width), BF16)
        return carry

    loop(0, FR, zero_tile)
    for ref in (cbuf.at[0], cbuf.at[1], dbuf):

        def zero_conv(i, carry, ref=ref):
            for h in range(2):
                ref[h, pl.ds(pl.multiple_of(i * 64, 64), 64)] = jnp.zeros((64, 128), F32)
            return carry

        loop(0, ref.shape[1] // 64, zero_conv)

    pl.semaphore_wait(barrier, n_dev - 1)

    def swap_in(src):
        cp = pltpu.make_async_remote_copy(
            src_ref=src.at[pl.ds((1 - odd) * FR, extra)],
            dst_ref=pool.at[pl.ds(cap, extra)],
            send_sem=rem_sem.at[0],
            recv_sem=rem_sem.at[1],
            device_id=sib,
            device_id_type=MESH,
        )
        cp.start()
        return cp

    first_held = held[col, ta - odd]

    def gather_into(dst):
        def pick_frame(j, carry):
            own = jnp.where(odd == 0, j, j + FR - first_held)
            far = jnp.where(odd == 0, j - first_held, j)
            mine = jnp.where(odd == 0, j < first_held, own >= 0)
            pick = jnp.where(mine, jnp.clip(own, 0, cap - 1), cap + jnp.clip(far, 0, extra - 1))
            dst[j, :, 0:ww, :] = pool[pick]
            return carry

        loop(0, FR, pick_frame)

    cp = swap_in(frames)
    own_cp.wait()
    cp.wait()
    gather_into(a0)
    own_cp = pltpu.make_async_copy(gout, pool.at[pl.ds(0, cap)], in_sem.at[0])
    own_cp.start()

    def along_ta(k):
        return (col, lax.rem(ta + k, n_ta))

    def along_col(k):
        return (lax.rem(col + k, n_col), ta)

    stages = {
        "all": (nbuf, ns_sem, nr_sem, n_dev, me, peer),
        "ta": (tbuf, ts_sem, tr_sem, n_ta, ta, along_ta),
        "col": (gbuf, gs_sem, gr_sem, n_col, col, along_col),
    }
    used = {"all": 0, "ta": 0, "col": 0}

    def exchange(name, values, between=None):
        buf, ssem, rsem, size, mine, who = stages[name]
        par = used[name] % 2
        used[name] += 1
        lanes = pl.ds(0, values.shape[1])
        buf[par, mine, :, lanes] = values

        def send(k, carry):
            pltpu.make_async_remote_copy(
                src_ref=buf.at[par, mine, :, lanes],
                dst_ref=buf.at[par, mine, :, lanes],
                send_sem=ssem.at[par],
                recv_sem=rsem.at[par],
                device_id=who(k),
                device_id_type=MESH,
            ).start()
            return carry

        loop(1, size, send)
        if between is not None:
            between()
        part = buf.at[par, pl.ds(0, size - 1), :, lanes]
        pltpu.make_async_copy(part, part, rsem.at[par]).wait()
        pltpu.make_async_copy(part, part, ssem.at[par]).wait()
        return buf[par, :, :, lanes]

    def merge(name, mean_l, m2_l, per, size, between=None):
        got = exchange(name, jnp.concatenate([mean_l, m2_l], axis=0), between)
        total = jnp.sum(got, axis=0)
        mean = total[0:1] * (1.0 / size)
        dev = got - mean[None]
        spread = jnp.sum(dev * dev, axis=0)[0:1]
        return mean, total[1:2] + per * spread

    def moments(mean_l, m2_l, wide, between=None):
        if wide or n_dev > 64:
            mean, m2 = merge("ta", mean_l, m2_l, n_local, n_ta, between)
            mean, m2 = merge("col", mean, m2, n_local * n_ta, n_col)
        else:
            mean, m2 = merge("all", mean_l, m2_l, n_local, n_dev, between)
        return mean, lax.rsqrt(m2 * (1.0 / n_total) + EPS)

    def sums(s0, s1, wide, between=None, later=None):
        total = jnp.concatenate([s0, s1], axis=0)
        if wide or n_dev > 64:
            total = jnp.sum(exchange("ta", total, between), axis=0)
            total = jnp.sum(exchange("col", total, later), axis=0)
        else:
            total = jnp.sum(exchange("all", total, between), axis=0)
        return total[0:1], total[1:2]

    def rows(f, n=1):
        return pl.ds(pl.multiple_of(f * (n * rf), rf), n * rf)

    def ld_h(f, n=1):
        return jnp.concatenate([hbuf[0, rows(f, n)], hbuf[1, rows(f, n)]], axis=1)

    def st_h(f, values, n=1):
        hbuf[0, rows(f, n)] = values[:, :128]
        hbuf[1, rows(f, n)] = values[:, 128:]

    def conv_rows(slot):
        return pl.ds(pl.multiple_of(lead + slot * stride + wp, 8), rf)

    def st_conv(ref, slot, values):
        ref[0, conv_rows(slot)] = values[:, :128]
        ref[1, conv_rows(slot)] = values[:, 128:]

    def local_m2(mean_l):
        sacc[0:wp, 0:bot] = jnp.zeros((wp, bot), F32)

        def to_m2(f, carry):
            d = ld_h(f) - mean_l
            sacc[0:wp, 0:bot] += rowsum(d * d)
            return carry

        loop(0, FR, to_m2)
        return live_total(sacc[0:wp, 0:bot])

    def conv_frame(src, wrow, f, flip):
        def half(h, carry):
            wts = []
            w_all = prm[h]
            for dt in range(3):
                scale = None
                if dt == 0:
                    scale = okmask[0, f]
                if dt == 2:
                    scale = okmask[1, f]
                for sp in range(9):
                    idx = dt * 9 + sp
                    row = w_all[26 - idx : 27 - idx] if flip else w_all[idx : idx + 1]
                    if scale is not None:
                        row = row * scale
                    wts.append(jnp.broadcast_to(row, (8, 128)))
            out = []
            for y in range(hh):
                for s in range(2):
                    acc = [None, None, None]
                    for dt in range(3):
                        for dy in range(3):
                            for dx in range(3):
                                off = lead + dt * stride + (y + dy) * wp + dx - 1 + s * 8
                                v = src[h, pl.ds(f * stride + off, 8)]
                                term = v * wts[dt * 9 + dy * 3 + dx]
                                acc[dx] = term if acc[dx] is None else acc[dx] + term
                    val = acc[0] + acc[1] + acc[2]
                    hbuf[h, pl.ds(pl.multiple_of(f * rf + y * wp + s * 8, 8), 8)] = val
            return carry

        loop(0, 2, half)

    def load_taps(b):
        k = taps[...].astype(F32)[:, b]
        prm[0, 0:27] = k[:, :128]
        prm[1, 0:27] = k[:, 128:]

    def send_halos(ref, which):
        cps = []
        for i, (slot, land, dev) in enumerate(((1, FR + 1, prv), (FR, 0, nxt))):
            cp = pltpu.make_async_remote_copy(
                src_ref=ref.at[:, pl.ds(lead + slot * stride + wp, rf)],
                dst_ref=ref.at[:, pl.ds(lead + land * stride + wp, rf)],
                send_sem=halo_sem.at[which, i, 0],
                recv_sem=halo_sem.at[which, i, 1],
                device_id=dev,
                device_id_type=MESH,
            )
            cp.start()
            cps.append(cp)
        return cps

    def edge_first(step):
        step(0, 0)
        step(FR - 1, 0)

    def chunk(c):
        return pl.ds(c * 256, 256)

    def flat(ref, f, c, n=1):
        return ref[pl.ds(f * n, n), :, :, chunk(c)].reshape(n * rf, 256)

    def put(ref, f, c, values, n=1):
        ref[pl.ds(f * n, n), :, :, chunk(c)] = values.reshape(n, hh, wp, 256)

    nz = n_ta // 2
    zpos = lax.div(ta, 2)
    if n_dev == 32:
        first = col * nz + zpos
        levels = [
            (
                n_dev // 2,
                16,
                first,
                lambda i: (lax.div(i, nz), 2 * lax.rem(i, nz) + odd),
            )
        ]
    else:
        levels = [
            (n_col, 4, col, lambda i: (i, ta)),
            (nz, 4, zpos, lambda i: (col, 2 * i + odd)),
        ]

    def package(bufs, sems, dst):
        send, land, final = bufs[0], bufs[1], bufs[2]
        halls = bufs[3:]

        def remote(src, to, i, dev):
            return pltpu.make_async_remote_copy(
                src_ref=src,
                dst_ref=to,
                send_sem=sems.at[2 * i],
                recv_sem=sems.at[2 * i + 1],
                device_id=dev,
                device_id_type=MESH,
            )

        cp = remote(send.at[1 - odd], land, 0, sib)
        cp.start()
        yield
        cp.wait()

        def add(r, carry):
            both = send[odd, r].astype(F32) + land[r].astype(F32)
            send[odd, r] = both.astype(BF16)
            return carry

        loop(0, 16, add)
        off, size = 0, 16
        spans = []
        for i, (n, m, mine, who) in enumerate(levels):
            hall = halls[i]
            size = size // m

            def scatter(k, carry, hall=hall, size=size, off=off, n=n, m=m, mine=mine, who=who, i=i):
                other = lax.rem(mine + k, n)
                part = send.at[odd, pl.ds(off + lax.rem(other, m) * size, size)]
                remote(part, hall.at[mine], 1 + i, who(other)).start()
                return carry

            loop(1, n, scatter)
            off = off + lax.rem(mine, m) * size
            hall[mine] = send[odd, pl.ds(off, size)]
            yield
            part = hall.at[pl.ds(0, n - 1)]
            pltpu.make_async_copy(part, part, sems.at[3 + 2 * i]).wait()
            pltpu.make_async_copy(part, part, sems.at[2 + 2 * i]).wait()
            last = i == len(levels) - 1

            def reduce(q, carry, hall=hall, n=n, off=off, last=last):
                total = jnp.sum(hall[:, q].astype(F32), axis=0).astype(BF16)
                if last:
                    final[odd, off + q] = total
                else:
                    send[odd, off + q] = total
                return carry

            loop(0, size, reduce)
            spans.append((off, size))
        base = 1 + len(levels)
        for i in reversed(range(len(levels))):
            n, m, mine, who = levels[i]
            off, size = spans[i]

            def spread(k, carry, off=off, size=size, m=m, mine=mine, who=who, i=i):
                other = lax.div(mine, m) * m + lax.rem(lax.rem(mine, m) + k, m)
                part = final.at[odd, pl.ds(off, size)]
                remote(part, part, base + i, who(other)).start()
                return carry

            loop(1, m, spread)
            yield
            part = final.at[odd, pl.ds(0, (m - 1) * size)]
            pltpu.make_async_copy(part, part, sems.at[2 * (base + i) + 1]).wait()
            pltpu.make_async_copy(part, part, sems.at[2 * (base + i)]).wait()
        cp = remote(final.at[odd], final.at[odd], base + len(levels), sib)
        cp.start()
        yield
        cp.wait()
        cp = pltpu.make_async_copy(final, dst, sems.at[2 * (base + len(levels)) + 2])
        cp.start()
        yield
        cp.wait()
        yield

    def finish(gen):
        for _ in gen:
            pass

    def advance(*gens):
        for gen in gens:
            next(gen, None)

    ksum[...] = jnp.zeros(ksum.shape, F32)
    pa_bufs[0][...] = jnp.zeros(pa_bufs[0].shape, BF16)
    half_w = width // 2

    def pack_a():
        def step(r, carry):
            rr = pl.ds(pl.multiple_of(r * 16, 16), 16)
            for p in range(2):
                pa_bufs[0][p, r, :, 0:half_w] = wacc[rr, p * half_w : p * half_w + half_w].astype(BF16)
                pa_bufs[0][p, r, :, half_w : half_w + 128] = w2acc[rr, p * 128 : p * 128 + 128].astype(BF16)
            return carry

        loop(0, 16, step)
        for p in range(2):
            for r in range(2):
                pa_bufs[0][p, r, :, half_w + 128 :] = ksum[p, r * 16 : r * 16 + 16].astype(BF16)

    def pack_b():
        def step(r, carry):
            rr = pl.ds(pl.multiple_of(r * 16, 16), 16)
            for p in range(2):
                pb_bufs[0][p, r] = wacc[rr, p * half_w : p * half_w + half_w].astype(BF16)
            return carry

        loop(0, 16, step)

    def first_mm(src, b):
        sacc[0:wp, 0:bot] = jnp.zeros((wp, bot), F32)

        def to_h1(f, carry):
            h1 = dot_nn(src[pl.ds(f * N1, N1)].reshape(N1 * rf, width), w1[b])
            st_h(f, h1, N1)
            sacc[0:wp, 0:bot] += rowsum(h1)
            return carry

        loop(0, FR // N1, to_h1)
        mean_l = live_total(sacc[0:wp, 0:bot]) * (1.0 / n_local)
        return mean_l, local_m2(mean_l)

    inv1, inv2, mean3, inv3 = {}, {}, {}, {}

    def vec(ref, b, j):
        return ref[b].astype(F32)[j : j + 1]

    def wvec(ref, b):
        return ref[...].astype(F32)[b : b + 1]

    def get_gout():
        own_cp.wait()

    def block_forward(b, src, after_first):
        mean_l, m2_l = first_mm(src, b)
        mean, inv = moments(mean_l, m2_l, False, None)
        inv1[b] = inv
        after_first()
        g, bb = vec(ngain, b, 0), vec(nbias, b, 0)

        def to_h2(f, carry):
            xhat = (ld_h(f) - mean) * inv
            x1b[b, rows(f)] = xhat.astype(BF16)
            u1 = masked(silu(xhat * g + bb)).astype(BF16)
            h2 = dot_nn(u1, w2[b]).astype(BF16).astype(F32)
            st_conv(cbuf.at[b], f + 1, h2)
            return carry

        edge_first(to_h2)
        cps = send_halos(cbuf.at[b], b)
        loop(1, FR - 1, to_h2)
        load_taps(b)

        def conv_step(f, carry):
            conv_frame(cbuf.at[b], None, f, False)
            return carry

        loop(1, FR - 1, conv_step)
        for cp in cps:
            cp.wait()
        conv_step(0, 0)
        conv_step(FR - 1, 0)
        sacc[0:wp, 0:bot] = jnp.zeros((wp, bot), F32)

        def dw_sum(f, carry):
            sacc[0:wp, 0:bot] += rowsum(ld_h(f))
            return carry

        loop(0, FR, dw_sum)
        mean_l = live_total(sacc[0:wp, 0:bot]) * (1.0 / n_local)
        m2_l = local_m2(mean_l)
        mean, inv = moments(mean_l, m2_l, False, None)
        inv2[b] = inv
        g, bb = vec(ngain, b, 1), vec(nbias, b, 1)
        sacc[0:wp, 0:bot] = jnp.zeros((wp, bot), F32)

        def to_u2(f, carry):
            xhat = (ld_h(f) - mean) * inv
            x2b[b, rows(f)] = xhat.astype(BF16)
            u2 = masked(silu(xhat * g + bb))
            u2b[b, rows(f)] = u2.astype(BF16)
            sacc[0:wp, 0:bot] += rowsum(u2)
            return carry

        loop(0, FR, to_u2)
        u_mean = live_total(sacc[0:wp, 0:bot]) * (1.0 / n_local)
        pivot = dot_nn(jnp.broadcast_to(u_mean, (16, bot)).astype(BF16), w3[b])[0:1]
        sacc[...] = jnp.zeros(sacc.shape, F32)

        def h3_stats(f, carry):
            left = u2b[b, rows(f, N3)]
            for c in range(chunks):
                h3 = dot_nn(left, w3[b, :, chunk(c)]) - pivot[:, c * 256 : c * 256 + 256]
                sacc[0:wp, chunk(c)] += rowsum(h3)
                sacc[wp : 2 * wp, chunk(c)] += rowsum(h3 * h3)
            return carry

        loop(0, FR // N3, h3_stats)
        s1 = live_total(sacc[0:wp]) * (1.0 / n_local)
        s2 = live_total(sacc[wp : 2 * wp])
        mean3[b], inv3[b] = moments(pivot + s1, s2 - n_local * s1 * s1, True, None)

    def second_in():
        nonlocal cp2
        cp2 = swap_in(gout)

    cp2 = None
    block_forward(0, a0, second_in)

    g3, b3 = wvec(wgain, 0), wvec(wbias, 0)
    sc, sh = g3 * inv3[0], b3 - mean3[0] * g3 * inv3[0]

    def to_a1(f, carry):
        left = u2b[0, rows(f, NA)]
        for c in range(chunks):
            s = slice(c * 256, c * 256 + 256)
            h3 = dot_nn(left, w3[0, :, chunk(c)])
            pre = flat(a0, f, c, NA).astype(F32) + (h3 * sc[:, s] + sh[:, s])
            put(a1, f, c, silu(pre).astype(BF16), NA)
        return carry

    loop(0, FR // NA, to_a1)

    def none():
        pass

    own_cp.wait()
    cp2.wait()
    gather_into(pbuf)
    block_forward(1, a1, none)

    g3, b3 = wvec(wgain, 1), wvec(wbias, 1)
    nxhat = mean3[1] * inv3[1]
    sacc[...] = jnp.zeros(sacc.shape, F32)

    def out_copy(f, dst):
        slot = lax.rem(f, 2)
        return pltpu.make_async_copy(ost.at[slot], dst.at[f], out_sem.at[slot])

    def turn(f, carry):
        @pl.when(f >= 2)
        def _():
            out_copy(f - 2, a2w).wait()

        slot = lax.rem(f, 2)
        left = u2b[1, rows(f)]
        for c in range(chunks):
            s = slice(c * 256, c * 256 + 256)
            h3 = dot_nn(left, w3[1, :, chunk(c)])
            xhat = h3 * inv3[1][:, s] - nxhat[:, s]
            pre = flat(a1, f, c).astype(F32) + (xhat * g3[:, s] + b3[:, s])
            act, slope = silu_and_slope(pre)
            ost[slot, :, :, chunk(c)] = act.astype(BF16).reshape(hh, wp, 256)[:, 0:ww]
            grad = flat(pbuf, f, c).astype(F32) * slope
            put(pbuf, f, c, grad.astype(BF16))
            sacc[0:wp, chunk(c)] += rowsum(grad)
            sacc[wp : 2 * wp, chunk(c)] += rowsum(grad * xhat)
        out_copy(f, a2w).start()
        return carry

    loop(0, FR, turn)
    out_copy(FR - 2, a2w).wait()
    out_copy(FR - 1, a2w).wait()

    def swap_out(src, dst, i):
        cp = pltpu.make_async_remote_copy(
            src_ref=src.at[pl.ds((1 - odd) * (FR - extra), extra)],
            dst_ref=dst,
            send_sem=rem_sem.at[2 + i],
            recv_sem=rem_sem.at[4 + i],
            device_id=sib,
            device_id_type=MESH,
        )
        cp.start()
        return cp

    ret_a = swap_out(a2w, a2r, 0)
    sum_p, sum_px = live_total(sacc[0:wp]), live_total(sacc[wp : 2 * wp])

    def block_backward(b, act_src, windows):
        s0, s1 = sums(sum_p, sum_px, True, windows[0], windows[1])
        o_wb[b : b + 1] = s0
        o_wg[b : b + 1] = s1
        k3 = wvec(wgain, b) * inv3[b]
        c0, c1 = s0 * (1.0 / n_total), s1 * (1.0 / n_total)
        ch = k3 * c1 * inv3[b]
        cc = ch * mean3[b] - k3 * c0
        g2, b2 = vec(ngain, b, 1), vec(nbias, b, 1)
        sacc[0 : 2 * wp, 0:bot] = jnp.zeros((2 * wp, bot), F32)
        wacc[...] = jnp.zeros((bot, width), F32)

        def to_z2(f, carry):
            left = u2b[b, rows(f, NZ2)]
            for c in range(chunks):
                s = slice(c * 256, c * 256 + 256)
                h3 = dot_nn(left, w3[b, :, chunk(c)])
                dh3 = flat(pbuf, f, c, NZ2).astype(F32) * k3[:, s] - h3 * ch[:, s] + cc[:, s]
                tile[:, chunk(c)] = dh3.astype(BF16)
            du2 = dot_nt(tile[...], w3[b])
            for c in range(chunks):
                wacc[:, chunk(c)] += dot_tn(left, tile[:, chunk(c)])
            xhat = x2b[b, rows(f, NZ2)].astype(F32)
            _, slope = silu_and_slope(xhat * g2 + b2)
            z = du2 * slope
            st_h(f, z, NZ2)
            sacc[0:wp, 0:bot] += rowsum(z)
            sacc[wp : 2 * wp, 0:bot] += rowsum(z * xhat)
            return carry

        loop(0, FR // NZ2, to_z2)
        s0, s1 = sums(
            live_total(sacc[0:wp, 0:bot]), live_total(sacc[wp : 2 * wp, 0:bot]), False, windows[2]
        )
        o_nb[b, 1:2] = s0
        o_ng[b, 1:2] = s1
        k2 = g2 * inv2[b]
        c0, c1 = s0 * (1.0 / n_total), s1 * (1.0 / n_total)

        def to_ddw(f, carry):
            xhat = x2b[b, rows(f)].astype(F32)
            st_conv(dbuf, f + 1, masked(k2 * (ld_h(f) - c0 - xhat * c1)))
            return carry

        edge_first(to_ddw)
        cps = send_halos(dbuf, 2)
        loop(1, FR - 1, to_ddw)
        load_taps(b)

        def conv_back(f, carry):
            conv_frame(dbuf, None, f, True)
            return carry

        loop(1, FR - 1, conv_back)
        windows[3]()
        for cp in cps:
            cp.wait()
        conv_back(0, 0)
        conv_back(FR - 1, 0)
        g1, b1 = vec(ngain, b, 0), vec(nbias, b, 0)
        sacc[0 : 2 * wp, 0:bot] = jnp.zeros((2 * wp, bot), F32)
        w2acc[...] = jnp.zeros((bot, bot), F32)

        def to_z1(f, carry):
            dh2 = ld_h(f, NZ1).astype(BF16)
            xhat = x1b[b, rows(f, NZ1)].astype(F32)
            act, slope = silu_and_slope(xhat * g1 + b1)
            u1 = masked(act).astype(BF16)
            w2acc[...] += dot_tn(u1, dh2)
            z = dot_nt(dh2, w2[b]) * slope
            st_h(f, z, NZ1)
            sacc[0:wp, 0:bot] += rowsum(z)
            sacc[wp : 2 * wp, 0:bot] += rowsum(z * xhat)
            return carry

        loop(0, FR // NZ1, to_z1)
        def tap_grads():
            kacc[...] = jnp.zeros(kacc.shape, F32)

            def frame(f, carry):
                def half(h, carry2):
                    for dt in range(3):
                        acc = [None] * 9
                        for y in range(hh):
                            for s in range(2):
                                base = lead + (y + 1) * wp + s * 8
                                gv = dbuf[h, pl.ds(pl.multiple_of(f * stride, 8) + stride + base, 8)]
                                for dy in range(3):
                                    for dx in range(3):
                                        off = lead + dt * stride + (y + dy) * wp + dx - 1 + s * 8
                                        v = cbuf[b, h, pl.ds(f * stride + off, 8)] * gv
                                        i = dy * 3 + dx
                                        acc[i] = v if acc[i] is None else acc[i] + v
                        for i in range(9):
                            val = acc[i]
                            if dt == 0:
                                val = val * okmask[0, f]
                            if dt == 2:
                                val = val * okmask[1, f]
                            kacc[h, dt * 9 + i] += val
                    return carry2

                loop(0, 2, half)
                return carry

            loop(0, FR, frame)
            for h in range(2):
                ksum[h, 0:27] = jnp.sum(kacc[h], axis=1)
            windows[4]()
            pack_a()
            gen = package(pa_bufs, pa_sem, o_pa.at[b])
            next(gen)
            made.append(gen)

        made = []

        s0, s1 = sums(
            live_total(sacc[0:wp, 0:bot]), live_total(sacc[wp : 2 * wp, 0:bot]), False, tap_grads
        )
        o_nb[b, 0:1] = s0
        o_ng[b, 0:1] = s1
        k1 = g1 * inv1[b]
        c0, c1 = s0 * (1.0 / n_total), s1 * (1.0 / n_total)

        def to_dh1(f, carry):
            xhat = x1b[b, rows(f)].astype(F32)
            x1b[b, rows(f)] = masked(k1 * (ld_h(f) - c0 - xhat * c1)).astype(BF16)
            return carry

        loop(0, FR, to_dh1)

        def w1_grad():
            wacc[...] = jnp.zeros((bot, width), F32)

            def to_w1(f, carry):
                left = x1b[b, rows(f, NW)]
                for c in range(chunks):
                    wacc[:, chunk(c)] += dot_tn(left, flat(act_src, f, c, NW))
                return carry

            loop(0, FR // NW, to_w1)
            pack_b()
            gen = package(pb_bufs, pb_sem, o_pb.at[b])
            next(gen)
            return gen

        return w1_grad, made[0]

    def nothing():
        pass

    w1_grad, gen_a = block_backward(1, a1, [nothing] * 5)
    g3, b3 = wvec(wgain, 0), wvec(wbias, 0)
    nxhat = mean3[0] * inv3[0]
    sacc[...] = jnp.zeros(sacc.shape, F32)

    def middle(f, carry):
        left = u2b[0, rows(f, NM)]
        dh1 = x1b[1, rows(f, NM)]
        for c in range(chunks):
            s = slice(c * 256, c * 256 + 256)
            grad = dot_nt(dh1, w1[1, chunk(c), :]) + flat(pbuf, f, c, NM).astype(F32)
            h3 = dot_nn(left, w3[0, :, chunk(c)])
            xhat = h3 * inv3[0][:, s] - nxhat[:, s]
            pre = flat(a0, f, c, NM).astype(F32) + (xhat * g3[:, s] + b3[:, s])
            _, slope = silu_and_slope(pre)
            grad = grad * slope
            put(pbuf, f, c, grad.astype(BF16), NM)
            sacc[0:wp, chunk(c)] += rowsum(grad)
            sacc[wp : 2 * wp, chunk(c)] += rowsum(grad * xhat)
        return carry

    advance(gen_a)
    loop(0, FR // NM, middle)
    sum_p, sum_px = live_total(sacc[0:wp]), live_total(sacc[wp : 2 * wp])
    gens = []

    def window0():
        gens.append(w1_grad())
        advance(gen_a)

    def window1():
        pass

    def window2():
        advance(gen_a, gens[0])

    def window3():
        advance(gen_a, gens[0])

    def window4():
        advance(gens[0])
        finish(gen_a)

    w1_last, last_a = block_backward(0, a0, [window0, window1, window2, window3, window4])
    finish(gens[0])
    last_b = w1_last()
    advance(last_a)

    def last(f, carry):
        @pl.when(f >= 2)
        def _():
            out_copy(f - 2, gw).wait()

        slot = lax.rem(f, 2)
        dh1 = x1b[0, rows(f)]
        for c in range(chunks):
            grad = dot_nt(dh1, w1[0, chunk(c), :]) + flat(pbuf, f, c).astype(F32)
            ost[slot, :, :, chunk(c)] = grad.astype(BF16).reshape(hh, wp, 256)[:, 0:ww]
        out_copy(f, gw).start()
        return carry

    half_way = FR // 2
    loop(0, half_way, last)
    advance(last_a, last_b)
    loop(half_way, FR, last)
    out_copy(FR - 2, gw).wait()
    out_copy(FR - 1, gw).wait()
    ret_g = swap_out(gw, gr, 1)
    for _ in range(8):
        advance(last_a, last_b)
    finish(last_a)
    finish(last_b)
    ret_a.wait()
    ret_g.wait()


def run_main(dims, held, okmask, frames, gout, w1, w2, w3, taps, ngain, nbias, wgain, wbias):
    n_col, n_ta, cap, hh, ww, width, bot = dims
    n_dev = n_col * n_ta
    extra = cap - FR
    rf = hh * 16
    conv_rows = 8 + (FR + 2) * (hh + 2) * 16 + 8
    conv_rows = -(-conv_rows // 64) * 64
    sds = jax.ShapeDtypeStruct
    la, lb = width // 2 + 256, width // 2

    def piece_bufs(lanes):
        halls = [(16, 1)] if n_dev == 32 else [(n_col, 4), (n_ta // 2, 1)]
        return [
            pltpu.VMEM((2, 16, 16, lanes), BF16),
            pltpu.VMEM((16, 16, lanes), BF16),
            pltpu.VMEM((2, 16, 16, lanes), BF16),
        ] + [pltpu.VMEM((n, size, 16, lanes), BF16) for n, size in halls]

    n_sems = 2 * (2 + 2 * (1 if n_dev == 32 else 2)) + 1
    outs = (
        sds((FR, hh, ww, width), BF16),
        sds((extra, hh, ww, width), BF16),
        sds((FR, hh, ww, width), BF16),
        sds((extra, hh, ww, width), BF16),
        sds((2, 2, 16, 16, la), BF16),
        sds((2, 2, 16, 16, lb), BF16),
        sds((2, 2, bot), F32),
        sds((2, 2, bot), F32),
        sds((2, width), F32),
        sds((2, width), F32),
    )
    vm = pltpu.VMEM
    dma = pltpu.SemaphoreType.DMA
    scratch = [
        vm((cap + extra, hh, ww, width), BF16),
        vm((FR, hh, 16, width), BF16),
        vm((FR, hh, 16, width), BF16),
        vm((FR, hh, 16, width), BF16),
        vm((rf, width), BF16),
        vm((2, hh, ww, width), BF16),
        vm((2, FR * rf, bot), BF16),
        vm((2, FR * rf, 128), F32),
        vm((2, FR * rf, bot), BF16),
        vm((2, FR * rf, bot), BF16),
        vm((2, 2, conv_rows, 128), F32),
        vm((2, conv_rows, 128), F32),
        vm((bot, width), F32),
        vm((bot, bot), F32),
        vm((2, 27, 8, 128), F32),
        vm((2, 32, 128), F32),
        vm((2, n_dev if n_dev <= 64 else 1, 2, bot), F32),
        vm((2, n_ta, 2, width), F32),
        vm((2, n_col, 2, width), F32),
        vm((32, width), F32),
        vm((2, 32, 128), F32),
        piece_bufs(la),
        piece_bufs(lb),
        dma((1,)),
        dma((6,)),
        dma((3, 2, 2)),
        dma((2,)),
        dma((n_sems,)),
        dma((n_sems,)),
        dma((2,)),
        dma((2,)),
        dma((2,)),
        dma((2,)),
        dma((2,)),
        dma((2,)),
    ]
    return pl.pallas_call(
        functools.partial(main_kernel, dims),
        out_shape=outs,
        in_specs=[SM, SM, ANY, ANY] + [VM] * 8,
        out_specs=(ANY,) * 6 + (VM,) * 4,
        scratch_shapes=scratch,
        compiler_params=pltpu.CompilerParams(
            collective_id=0, has_side_effects=True, vmem_limit_bytes=66_500_000
        ),
        name="blocks",
    )(held, okmask, frames, gout, w1, w2, w3, taps, ngain, nbias, wgain, wbias)


def place_kernel(
    cap,
    where,
    a2w,
    a2r,
    gw,
    gr,
    pa,
    pb,
    i_ng,
    i_nb,
    i_wg,
    i_wb,
    out,
    grad,
    o_w1,
    o_w2,
    o_k,
    o_w3,
    o_ng,
    o_nb,
    o_wg,
    o_wb,
    work,
    zero,
    in_sem,
    out_sem,
):
    half = pb.shape[-1]
    extra = cap - FR
    odd, first = where[0], where[1]
    live = jnp.where(odd == 0, first, 2 * FR - first)
    arrays = ((a2w, a2r, out), (gw, gr, grad))

    def source(j):
        pos = jnp.where(odd == 0, j, first + j)
        mine = jnp.where(odd == 0, pos < FR, pos >= FR)
        own = jnp.where(odd == 0, pos, pos - FR)
        far = jnp.where(odd == 0, pos - FR, pos - (FR - extra))
        return mine, own, far

    def fetch(j, carry):
        mine, own, far = source(j)
        for i, (near, back, _) in enumerate(arrays):

            @pl.when((j < live) & mine)
            def _():
                pltpu.make_async_copy(near.at[own], work.at[i, j], in_sem.at[i, j]).start()

            @pl.when((j < live) & jnp.logical_not(mine))
            def _():
                pltpu.make_async_copy(back.at[far], work.at[i, j], in_sem.at[i, j]).start()

        return carry

    loop(0, cap, fetch)
    zero[...] = jnp.zeros(zero.shape, BF16)

    def clear(j, carry):
        for i, (_, _, dst) in enumerate(arrays):
            pltpu.make_async_copy(zero, dst.at[j], out_sem.at[i]).start()
        return carry

    lax.fori_loop(live, cap, clear, 0)

    def ship(j, carry):
        for i, (near, _, dst) in enumerate(arrays):
            pltpu.make_async_copy(near.at[0], work.at[i, j], in_sem.at[i, j]).wait()
            pltpu.make_async_copy(work.at[i, j], dst.at[j], out_sem.at[i]).start()
        return carry

    lax.fori_loop(0, live, ship, 0)
    o_ng[...] = i_ng[...]
    o_nb[...] = i_nb[...]
    o_wg[...] = i_wg[...]
    o_wb[...] = i_wb[...]
    for b in range(2):
        for p in range(2):
            cols = slice(p * 128, p * 128 + 128)
            taps = pa[b, p, 0:2, :, half + 128 :].astype(F32).reshape(32, 128)
            o_k[:, b, cols] = taps[0:27]
            mid = pa[b, p, :, :, half : half + 128].astype(F32)
            o_w2[b, :, cols] = mid.reshape(256, 128)
            cols = slice(p * half, p * half + half)
            o_w3[b, :, cols] = pa[b, p, :, :, 0:half].astype(F32).reshape(256, half)
            o_w1[b, cols, :] = pb[b, p].astype(F32).reshape(256, half).T
    pltpu.make_async_copy(out, out, out_sem.at[0]).wait()
    pltpu.make_async_copy(grad, grad, out_sem.at[1]).wait()


def place(dims, where, *parts):
    n_col, n_ta, cap, hh, ww, width, bot = dims
    sds = jax.ShapeDtypeStruct
    return pl.pallas_call(
        functools.partial(place_kernel, cap),
        out_shape=(sds((cap, hh, ww, width), BF16),) * 2
        + (
            sds((2, width, bot), F32),
            sds((2, bot, bot), F32),
            sds((27, 2, bot), F32),
            sds((2, bot, width), F32),
            sds((2, 2, bot), F32),
            sds((2, 2, bot), F32),
            sds((2, width), F32),
            sds((2, width), F32),
        ),
        in_specs=[SM] + [ANY] * 4 + [VM] * 6,
        out_specs=(ANY, ANY) + (VM,) * 8,
        scratch_shapes=[
            pltpu.VMEM((2, cap, hh, ww, width), BF16),
            pltpu.VMEM((hh, ww, width), BF16),
            pltpu.SemaphoreType.DMA((2, cap)),
            pltpu.SemaphoreType.DMA((2,)),
        ],
        compiler_params=pltpu.CompilerParams(vmem_limit_bytes=64_000_000),
        name="place",
    )(where, *parts)


def body(
    n_col,
    n_ta,
    frames,
    out_grad,
    held,
    clip_stride,
    w_reduce,
    w_mid,
    depth_kernel,
    w_expand,
    narrow_gain,
    narrow_bias,
    wide_gain,
    wide_bias,
):
    cap, hh, ww, width = frames.shape
    dims = (n_col, n_ta, cap, hh, ww, width, w_mid.shape[1])
    col, ta = lax.axis_index("col"), lax.axis_index("ta")
    odd = lax.rem(ta, 2)
    lengths = 8 // lax.dynamic_index_in_dim(clip_stride, col, 0, keepdims=False)
    clips = lengths.shape[0]
    before = jnp.arange(clips)[:, None] < jnp.arange(clips)[None, :]
    starts = jnp.sum(jnp.where(before, lengths[:, None], 0), axis=0)
    ids = ta * FR + jnp.arange(FR + 1)
    begins = jnp.any(starts[None, :] == ids[:, None], axis=1) | (ids >= n_ta * FR)
    ok = jnp.logical_not(begins).astype(F32)
    okmask = jnp.stack([ok[:-1], ok[1:]])
    parts = run_main(
        dims,
        held,
        okmask,
        frames,
        out_grad,
        w_reduce,
        w_mid,
        w_expand,
        jnp.swapaxes(depth_kernel, 0, 1),
        narrow_gain,
        narrow_bias,
        wide_gain,
        wide_bias,
    )
    where = jnp.stack([odd, held[col, ta - odd]]).astype(jnp.int32)
    outs = place(dims, where, *parts)
    return outs[:4] + (jnp.swapaxes(outs[4], 0, 1),) + outs[5:]


def solution(mesh):
    split = P(("col", "ta"), None, None, None)
    return jax.shard_map(
        functools.partial(body, mesh.shape["col"], mesh.shape["ta"]),
        mesh=mesh,
        in_specs=(split, split) + (P(),) * 10,
        out_specs=(split, split) + (P(),) * 8,
        check_vma=False,
    )
```

```python
import functools

import jax
import jax.numpy as jnp
from jax import lax
from jax.experimental import pallas as pl
from jax.experimental.pallas import tpu as pltpu
from jax.sharding import PartitionSpec as P

FR = 12
EPS = 1e-05
MESH = pl.DeviceIdType.MESH
F32 = jnp.float32
BF16 = jnp.bfloat16
ANY = pl.BlockSpec(memory_space=pl.ANY)
VM = pl.BlockSpec(memory_space=pltpu.VMEM)
SM = pl.BlockSpec(memory_space=pltpu.SMEM)


def loop(low, high, step):
    lax.fori_loop(low, high, step, 0)


def dot_nn(left, right):
    return lax.dot_general(left, right, (((1,), (0,)), ((), ())), preferred_element_type=F32)


def dot_nt(left, right):
    return lax.dot_general(left, right, (((1,), (1,)), ((), ())), preferred_element_type=F32)


def dot_tn(left, right):
    return lax.dot_general(left, right, (((0,), (0,)), ((), ())), preferred_element_type=F32)


def silu(values):
    half = 0.5 * values
    return half * jnp.tanh(half) + half


def silu_and_slope(values):
    half = 0.5 * values
    tan = jnp.tanh(half)
    act = half * tan + half
    sig = 0.5 * tan + 0.5
    return act, act + sig * (1.0 - act)


def main_kernel(
    dims,
    held,
    okmask,
    frames,
    gout,
    w1,
    w2,
    w3,
    taps,
    ngain,
    nbias,
    wgain,
    wbias,
    a2w,
    a2r,
    gw,
    gr,
    o_pa,
    o_pb,
    o_ng,
    o_nb,
    o_wg,
    o_wb,
    pool,
    a0,
    a1,
    pbuf,
    tile,
    ost,
    u2b,
    hbuf,
    x1b,
    x2b,
    cbuf,
    dbuf,
    wacc,
    w2acc,
    kacc,
    ksum,
    nbuf,
    tbuf,
    gbuf,
    sacc,
    prm,
    pa_bufs,
    pb_bufs,
    in_sem,
    rem_sem,
    halo_sem,
    out_sem,
    pa_sem,
    pb_sem,
    ns_sem,
    nr_sem,
    ts_sem,
    tr_sem,
    gs_sem,
    gr_sem,
):
    n_col, n_ta, cap, hh, ww, width, bot = dims
    n_dev = n_col * n_ta
    extra = cap - FR
    N1, N3, NA, NZ2, NZ1, NW, NM = (3, 2, 2, 2, 3, 4, 2) if n_dev <= 64 else (1,) * 7
    wp = 16
    rf = hh * wp
    stride = (hh + 2) * wp
    lead = 8
    n_local = float(FR * hh * ww)
    n_total = n_local * n_dev
    chunks = width // 256
    col, ta = lax.axis_index("col"), lax.axis_index("ta")
    me = col * n_ta + ta
    odd = lax.rem(ta, 2)
    sib = (col, ta + 1 - 2 * odd)
    nxt = (col, lax.rem(ta + 1, n_ta))
    prv = (col, lax.rem(ta + n_ta - 1, n_ta))

    def peer(k):
        other = lax.rem(me + k, n_dev)
        return (lax.div(other, n_ta), lax.rem(other, n_ta))

    own_cp = pltpu.make_async_copy(frames, pool.at[pl.ds(0, cap)], in_sem.at[0])
    own_cp.start()
    barrier = pltpu.get_barrier_semaphore()

    def greet(k, carry):
        pl.semaphore_signal(barrier, inc=1, device_id=peer(k), device_id_type=MESH)
        return carry

    loop(1, n_dev, greet)

    live_row = (lax.broadcasted_iota(jnp.int32, (wp, 1), 0) < ww).astype(F32)

    def masked(values):
        c = values.shape[-1]
        return (values.reshape(-1, wp, c) * live_row[None]).reshape(-1, c)

    def rowsum(values):
        return jnp.sum(values.reshape(-1, wp, values.shape[-1]), axis=0)

    def live_total(acc):
        return jnp.sum(acc * live_row, axis=0, keepdims=True)

    def zero_tile(f, carry):
        a0[f] = jnp.zeros((hh, wp, width), BF16)
        pbuf[f] = jnp.zeros((hh, wp, width), BF16)
        return carry

    loop(0, FR, zero_tile)
    for ref in (cbuf.at[0], cbuf.at[1], dbuf):

        def zero_conv(i, carry, ref=ref):
            for h in range(2):
                ref[h, pl.ds(pl.multiple_of(i * 64, 64), 64)] = jnp.zeros((64, 128), F32)
            return carry

        loop(0, ref.shape[1] // 64, zero_conv)

    pl.semaphore_wait(barrier, n_dev - 1)

    def swap_in(src):
        cp = pltpu.make_async_remote_copy(
            src_ref=src.at[pl.ds((1 - odd) * FR, extra)],
            dst_ref=pool.at[pl.ds(cap, extra)],
            send_sem=rem_sem.at[0],
            recv_sem=rem_sem.at[1],
            device_id=sib,
            device_id_type=MESH,
        )
        cp.start()
        return cp

    first_held = held[col, ta - odd]

    def gather_into(dst):
        def pick_frame(j, carry):
            own = jnp.where(odd == 0, j, j + FR - first_held)
            far = jnp.where(odd == 0, j - first_held, j)
            mine = jnp.where(odd == 0, j < first_held, own >= 0)
            pick = jnp.where(mine, jnp.clip(own, 0, cap - 1), cap + jnp.clip(far, 0, extra - 1))
            dst[j, :, 0:ww, :] = pool[pick]
            return carry

        loop(0, FR, pick_frame)

    cp = swap_in(frames)
    own_cp.wait()
    cp.wait()
    gather_into(a0)
    own_cp = pltpu.make_async_copy(gout, pool.at[pl.ds(0, cap)], in_sem.at[0])
    own_cp.start()

    def along_ta(k):
        return (col, lax.rem(ta + k, n_ta))

    def along_col(k):
        return (lax.rem(col + k, n_col), ta)

    stages = {
        "all": (nbuf, ns_sem, nr_sem, n_dev, me, peer),
        "ta": (tbuf, ts_sem, tr_sem, n_ta, ta, along_ta),
        "col": (gbuf, gs_sem, gr_sem, n_col, col, along_col),
    }
    used = {"all": 0, "ta": 0, "col": 0}

    def exchange(name, values, between=None):
        buf, ssem, rsem, size, mine, who = stages[name]
        par = used[name] % 2
        used[name] += 1
        lanes = pl.ds(0, values.shape[1])
        buf[par, mine, :, lanes] = values

        def send(k, carry):
            pltpu.make_async_remote_copy(
                src_ref=buf.at[par, mine, :, lanes],
                dst_ref=buf.at[par, mine, :, lanes],
                send_sem=ssem.at[par],
                recv_sem=rsem.at[par],
                device_id=who(k),
                device_id_type=MESH,
            ).start()
            return carry

        loop(1, size, send)
        if between is not None:
            between()
        part = buf.at[par, pl.ds(0, size - 1), :, lanes]
        pltpu.make_async_copy(part, part, rsem.at[par]).wait()
        pltpu.make_async_copy(part, part, ssem.at[par]).wait()
        return buf[par, :, :, lanes]

    def merge(name, mean_l, m2_l, per, size, between=None):
        got = exchange(name, jnp.concatenate([mean_l, m2_l], axis=0), between)
        total = jnp.sum(got, axis=0)
        mean = total[0:1] * (1.0 / size)
        dev = got - mean[None]
        spread = jnp.sum(dev * dev, axis=0)[0:1]
        return mean, total[1:2] + per * spread

    def moments(mean_l, m2_l, wide, between=None):
        if wide or n_dev > 64:
            mean, m2 = merge("ta", mean_l, m2_l, n_local, n_ta, between)
            mean, m2 = merge("col", mean, m2, n_local * n_ta, n_col)
        else:
            mean, m2 = merge("all", mean_l, m2_l, n_local, n_dev, between)
        return mean, lax.rsqrt(m2 * (1.0 / n_total) + EPS)

    def sums(s0, s1, wide, between=None, later=None):
        total = jnp.concatenate([s0, s1], axis=0)
        if wide or n_dev > 64:
            total = jnp.sum(exchange("ta", total, between), axis=0)
            total = jnp.sum(exchange("col", total, later), axis=0)
        else:
            total = jnp.sum(exchange("all", total, between), axis=0)
        return total[0:1], total[1:2]

    def rows(f, n=1):
        return pl.ds(pl.multiple_of(f * (n * rf), rf), n * rf)

    def ld_h(f, n=1):
        return jnp.concatenate([hbuf[0, rows(f, n)], hbuf[1, rows(f, n)]], axis=1)

    def st_h(f, values, n=1):
        hbuf[0, rows(f, n)] = values[:, :128]
        hbuf[1, rows(f, n)] = values[:, 128:]

    def conv_rows(slot):
        return pl.ds(pl.multiple_of(lead + slot * stride + wp, 8), rf)

    def st_conv(ref, slot, values):
        ref[0, conv_rows(slot)] = values[:, :128]
        ref[1, conv_rows(slot)] = values[:, 128:]

    def local_m2(mean_l):
        sacc[0:wp, 0:bot] = jnp.zeros((wp, bot), F32)

        def to_m2(f, carry):
            d = ld_h(f) - mean_l
            sacc[0:wp, 0:bot] += rowsum(d * d)
            return carry

        loop(0, FR, to_m2)
        return live_total(sacc[0:wp, 0:bot])

    def conv_frame(src, wrow, f, flip):
        def half(h, carry):
            wts = []
            w_all = prm[h]
            for dt in range(3):
                scale = None
                if dt == 0:
                    scale = okmask[0, f]
                if dt == 2:
                    scale = okmask[1, f]
                for sp in range(9):
                    idx = dt * 9 + sp
                    row = w_all[26 - idx : 27 - idx] if flip else w_all[idx : idx + 1]
                    if scale is not None:
                        row = row * scale
                    wts.append(jnp.broadcast_to(row, (8, 128)))
            out = []
            for y in range(hh):
                for s in range(2):
                    acc = [None, None, None]
                    for dt in range(3):
                        for dy in range(3):
                            for dx in range(3):
                                off = lead + dt * stride + (y + dy) * wp + dx - 1 + s * 8
                                v = src[h, pl.ds(f * stride + off, 8)]
                                term = v * wts[dt * 9 + dy * 3 + dx]
                                acc[dx] = term if acc[dx] is None else acc[dx] + term
                    val = acc[0] + acc[1] + acc[2]
                    hbuf[h, pl.ds(pl.multiple_of(f * rf + y * wp + s * 8, 8), 8)] = val
            return carry

        loop(0, 2, half)

    def load_taps(b):
        k = taps[...].astype(F32)[:, b]
        prm[0, 0:27] = k[:, :128]
        prm[1, 0:27] = k[:, 128:]

    def send_halos(ref, which):
        cps = []
        for i, (slot, land, dev) in enumerate(((1, FR + 1, prv), (FR, 0, nxt))):
            cp = pltpu.make_async_remote_copy(
                src_ref=ref.at[:, pl.ds(lead + slot * stride + wp, rf)],
                dst_ref=ref.at[:, pl.ds(lead + land * stride + wp, rf)],
                send_sem=halo_sem.at[which, i, 0],
                recv_sem=halo_sem.at[which, i, 1],
                device_id=dev,
                device_id_type=MESH,
            )
            cp.start()
            cps.append(cp)
        return cps

    def edge_first(step):
        step(0, 0)
        step(FR - 1, 0)

    def chunk(c):
        return pl.ds(c * 256, 256)

    def flat(ref, f, c, n=1):
        return ref[pl.ds(f * n, n), :, :, chunk(c)].reshape(n * rf, 256)

    def put(ref, f, c, values, n=1):
        ref[pl.ds(f * n, n), :, :, chunk(c)] = values.reshape(n, hh, wp, 256)

    nz = n_ta // 2
    zpos = lax.div(ta, 2)
    if n_dev == 32:
        first = col * nz + zpos
        levels = [
            (
                n_dev // 2,
                16,
                first,
                lambda i: (lax.div(i, nz), 2 * lax.rem(i, nz) + odd),
            )
        ]
    else:
        levels = [
            (n_col, 4, col, lambda i: (i, ta)),
            (nz, 4, zpos, lambda i: (col, 2 * i + odd)),
        ]

    def package(bufs, sems, dst):
        send, land, final = bufs[0], bufs[1], bufs[2]
        halls = bufs[3:]

        def remote(src, to, i, dev):
            return pltpu.make_async_remote_copy(
                src_ref=src,
                dst_ref=to,
                send_sem=sems.at[2 * i],
                recv_sem=sems.at[2 * i + 1],
                device_id=dev,
                device_id_type=MESH,
            )

        cp = remote(send.at[1 - odd], land, 0, sib)
        cp.start()
        yield
        cp.wait()

        def add(r, carry):
            both = send[odd, r].astype(F32) + land[r].astype(F32)
            send[odd, r] = both.astype(BF16)
            return carry

        loop(0, 16, add)
        off, size = 0, 16
        spans = []
        for i, (n, m, mine, who) in enumerate(levels):
            hall = halls[i]
            size = size // m

            def scatter(k, carry, hall=hall, size=size, off=off, n=n, m=m, mine=mine, who=who, i=i):
                other = lax.rem(mine + k, n)
                part = send.at[odd, pl.ds(off + lax.rem(other, m) * size, size)]
                remote(part, hall.at[mine], 1 + i, who(other)).start()
                return carry

            loop(1, n, scatter)
            off = off + lax.rem(mine, m) * size
            hall[mine] = send[odd, pl.ds(off, size)]
            yield
            part = hall.at[pl.ds(0, n - 1)]
            pltpu.make_async_copy(part, part, sems.at[3 + 2 * i]).wait()
            pltpu.make_async_copy(part, part, sems.at[2 + 2 * i]).wait()
            last = i == len(levels) - 1

            def reduce(q, carry, hall=hall, n=n, off=off, last=last):
                total = jnp.sum(hall[:, q].astype(F32), axis=0).astype(BF16)
                if last:
                    final[odd, off + q] = total
                else:
                    send[odd, off + q] = total
                return carry

            loop(0, size, reduce)
            spans.append((off, size))
        base = 1 + len(levels)
        for i in reversed(range(len(levels))):
            n, m, mine, who = levels[i]
            off, size = spans[i]

            def spread(k, carry, off=off, size=size, m=m, mine=mine, who=who, i=i):
                other = lax.div(mine, m) * m + lax.rem(lax.rem(mine, m) + k, m)
                part = final.at[odd, pl.ds(off, size)]
                remote(part, part, base + i, who(other)).start()
                return carry

            loop(1, m, spread)
            yield
            part = final.at[odd, pl.ds(0, (m - 1) * size)]
            pltpu.make_async_copy(part, part, sems.at[2 * (base + i) + 1]).wait()
            pltpu.make_async_copy(part, part, sems.at[2 * (base + i)]).wait()
        cp = remote(final.at[odd], final.at[odd], base + len(levels), sib)
        cp.start()
        yield
        cp.wait()
        cp = pltpu.make_async_copy(final, dst, sems.at[2 * (base + len(levels)) + 2])
        cp.start()
        yield
        cp.wait()
        yield

    def finish(gen):
        for _ in gen:
            pass

    def advance(*gens):
        for gen in gens:
            next(gen, None)

    ksum[...] = jnp.zeros(ksum.shape, F32)
    pa_bufs[0][...] = jnp.zeros(pa_bufs[0].shape, BF16)
    half_w = width // 2

    def pack_a():
        def step(r, carry):
            rr = pl.ds(pl.multiple_of(r * 16, 16), 16)
            for p in range(2):
                pa_bufs[0][p, r, :, 0:half_w] = wacc[rr, p * half_w : p * half_w + half_w].astype(BF16)
                pa_bufs[0][p, r, :, half_w : half_w + 128] = w2acc[rr, p * 128 : p * 128 + 128].astype(BF16)
            return carry

        loop(0, 16, step)
        for p in range(2):
            for r in range(2):
                pa_bufs[0][p, r, :, half_w + 128 :] = ksum[p, r * 16 : r * 16 + 16].astype(BF16)

    def pack_b():
        def step(r, carry):
            rr = pl.ds(pl.multiple_of(r * 16, 16), 16)
            for p in range(2):
                pb_bufs[0][p, r] = wacc[rr, p * half_w : p * half_w + half_w].astype(BF16)
            return carry

        loop(0, 16, step)

    def first_mm(src, b):
        sacc[0:wp, 0:bot] = jnp.zeros((wp, bot), F32)

        def to_h1(f, carry):
            h1 = dot_nn(src[pl.ds(f * N1, N1)].reshape(N1 * rf, width), w1[b])
            st_h(f, h1, N1)
            sacc[0:wp, 0:bot] += rowsum(h1)
            return carry

        loop(0, FR // N1, to_h1)
        mean_l = live_total(sacc[0:wp, 0:bot]) * (1.0 / n_local)
        return mean_l, local_m2(mean_l)

    inv1, inv2, mean3, inv3 = {}, {}, {}, {}

    def vec(ref, b, j):
        return ref[b].astype(F32)[j : j + 1]

    def wvec(ref, b):
        return ref[...].astype(F32)[b : b + 1]

    def get_gout():
        own_cp.wait()

    def block_forward(b, src, after_first):
        mean_l, m2_l = first_mm(src, b)
        mean, inv = moments(mean_l, m2_l, False, None)
        inv1[b] = inv
        after_first()
        g, bb = vec(ngain, b, 0), vec(nbias, b, 0)

        def to_h2(f, carry):
            xhat = (ld_h(f) - mean) * inv
            x1b[b, rows(f)] = xhat.astype(BF16)
            u1 = masked(silu(xhat * g + bb)).astype(BF16)
            h2 = dot_nn(u1, w2[b]).astype(BF16).astype(F32)
            st_conv(cbuf.at[b], f + 1, h2)
            return carry

        edge_first(to_h2)
        cps = send_halos(cbuf.at[b], b)
        loop(1, FR - 1, to_h2)
        load_taps(b)

        def conv_step(f, carry):
            conv_frame(cbuf.at[b], None, f, False)
            return carry

        loop(1, FR - 1, conv_step)
        for cp in cps:
            cp.wait()
        conv_step(0, 0)
        conv_step(FR - 1, 0)
        sacc[0:wp, 0:bot] = jnp.zeros((wp, bot), F32)

        def dw_sum(f, carry):
            sacc[0:wp, 0:bot] += rowsum(ld_h(f))
            return carry

        loop(0, FR, dw_sum)
        mean_l = live_total(sacc[0:wp, 0:bot]) * (1.0 / n_local)
        m2_l = local_m2(mean_l)
        mean, inv = moments(mean_l, m2_l, False, None)
        inv2[b] = inv
        g, bb = vec(ngain, b, 1), vec(nbias, b, 1)
        sacc[0:wp, 0:bot] = jnp.zeros((wp, bot), F32)

        def to_u2(f, carry):
            xhat = (ld_h(f) - mean) * inv
            x2b[b, rows(f)] = xhat.astype(BF16)
            u2 = masked(silu(xhat * g + bb))
            u2b[b, rows(f)] = u2.astype(BF16)
            sacc[0:wp, 0:bot] += rowsum(u2)
            return carry

        loop(0, FR, to_u2)
        u_mean = live_total(sacc[0:wp, 0:bot]) * (1.0 / n_local)
        pivot = dot_nn(jnp.broadcast_to(u_mean, (16, bot)).astype(BF16), w3[b])[0:1]
        sacc[...] = jnp.zeros(sacc.shape, F32)

        def h3_stats(f, carry):
            left = u2b[b, rows(f, N3)]
            for c in range(chunks):
                h3 = dot_nn(left, w3[b, :, chunk(c)]) - pivot[:, c * 256 : c * 256 + 256]
                sacc[0:wp, chunk(c)] += rowsum(h3)
                sacc[wp : 2 * wp, chunk(c)] += rowsum(h3 * h3)
            return carry

        loop(0, FR // N3, h3_stats)
        s1 = live_total(sacc[0:wp]) * (1.0 / n_local)
        s2 = live_total(sacc[wp : 2 * wp])
        mean3[b], inv3[b] = moments(pivot + s1, s2 - n_local * s1 * s1, True, None)

    def second_in():
        nonlocal cp2
        cp2 = swap_in(gout)

    cp2 = None
    block_forward(0, a0, second_in)

    g3, b3 = wvec(wgain, 0), wvec(wbias, 0)
    sc, sh = g3 * inv3[0], b3 - mean3[0] * g3 * inv3[0]

    def to_a1(f, carry):
        left = u2b[0, rows(f, NA)]
        for c in range(chunks):
            s = slice(c * 256, c * 256 + 256)
            h3 = dot_nn(left, w3[0, :, chunk(c)])
            pre = flat(a0, f, c, NA).astype(F32) + (h3 * sc[:, s] + sh[:, s])
            put(a1, f, c, silu(pre).astype(BF16), NA)
        return carry

    loop(0, FR // NA, to_a1)

    def none():
        pass

    own_cp.wait()
    cp2.wait()
    gather_into(pbuf)
    block_forward(1, a1, none)

    g3, b3 = wvec(wgain, 1), wvec(wbias, 1)
    nxhat = mean3[1] * inv3[1]
    sacc[...] = jnp.zeros(sacc.shape, F32)

    def out_copy(f, dst):
        slot = lax.rem(f, 2)
        return pltpu.make_async_copy(ost.at[slot], dst.at[f], out_sem.at[slot])

    def turn(f, carry):
        @pl.when(f >= 2)
        def _():
            out_copy(f - 2, a2w).wait()

        slot = lax.rem(f, 2)
        left = u2b[1, rows(f)]
        for c in range(chunks):
            s = slice(c * 256, c * 256 + 256)
            h3 = dot_nn(left, w3[1, :, chunk(c)])
            xhat = h3 * inv3[1][:, s] - nxhat[:, s]
            pre = flat(a1, f, c).astype(F32) + (xhat * g3[:, s] + b3[:, s])
            act, slope = silu_and_slope(pre)
            ost[slot, :, :, chunk(c)] = act.astype(BF16).reshape(hh, wp, 256)[:, 0:ww]
            grad = flat(pbuf, f, c).astype(F32) * slope
            put(pbuf, f, c, grad.astype(BF16))
            sacc[0:wp, chunk(c)] += rowsum(grad)
            sacc[wp : 2 * wp, chunk(c)] += rowsum(grad * xhat)
        out_copy(f, a2w).start()
        return carry

    loop(0, FR, turn)
    out_copy(FR - 2, a2w).wait()
    out_copy(FR - 1, a2w).wait()

    def swap_out(src, dst, i):
        cp = pltpu.make_async_remote_copy(
            src_ref=src.at[pl.ds((1 - odd) * (FR - extra), extra)],
            dst_ref=dst,
            send_sem=rem_sem.at[2 + i],
            recv_sem=rem_sem.at[4 + i],
            device_id=sib,
            device_id_type=MESH,
        )
        cp.start()
        return cp

    ret_a = swap_out(a2w, a2r, 0)
    sum_p, sum_px = live_total(sacc[0:wp]), live_total(sacc[wp : 2 * wp])

    def block_backward(b, act_src, windows):
        s0, s1 = sums(sum_p, sum_px, True, windows[0], windows[1])
        o_wb[b : b + 1] = s0
        o_wg[b : b + 1] = s1
        k3 = wvec(wgain, b) * inv3[b]
        c0, c1 = s0 * (1.0 / n_total), s1 * (1.0 / n_total)
        ch = k3 * c1 * inv3[b]
        cc = ch * mean3[b] - k3 * c0
        g2, b2 = vec(ngain, b, 1), vec(nbias, b, 1)
        sacc[0 : 2 * wp, 0:bot] = jnp.zeros((2 * wp, bot), F32)
        wacc[...] = jnp.zeros((bot, width), F32)

        def to_z2(f, carry):
            left = u2b[b, rows(f, NZ2)]
            for c in range(chunks):
                s = slice(c * 256, c * 256 + 256)
                h3 = dot_nn(left, w3[b, :, chunk(c)])
                dh3 = flat(pbuf, f, c, NZ2).astype(F32) * k3[:, s] - h3 * ch[:, s] + cc[:, s]
                tile[:, chunk(c)] = dh3.astype(BF16)
            du2 = dot_nt(tile[...], w3[b])
            for c in range(chunks):
                wacc[:, chunk(c)] += dot_tn(left, tile[:, chunk(c)])
            xhat = x2b[b, rows(f, NZ2)].astype(F32)
            _, slope = silu_and_slope(xhat * g2 + b2)
            z = du2 * slope
            st_h(f, z, NZ2)
            sacc[0:wp, 0:bot] += rowsum(z)
            sacc[wp : 2 * wp, 0:bot] += rowsum(z * xhat)
            return carry

        loop(0, FR // NZ2, to_z2)
        s0, s1 = sums(
            live_total(sacc[0:wp, 0:bot]), live_total(sacc[wp : 2 * wp, 0:bot]), False, windows[2]
        )
        o_nb[b, 1:2] = s0
        o_ng[b, 1:2] = s1
        k2 = g2 * inv2[b]
        c0, c1 = s0 * (1.0 / n_total), s1 * (1.0 / n_total)

        def to_ddw(f, carry):
            xhat = x2b[b, rows(f)].astype(F32)
            st_conv(dbuf, f + 1, masked(k2 * (ld_h(f) - c0 - xhat * c1)))
            return carry

        edge_first(to_ddw)
        cps = send_halos(dbuf, 2)
        loop(1, FR - 1, to_ddw)
        load_taps(b)

        def conv_back(f, carry):
            conv_frame(dbuf, None, f, True)
            return carry

        loop(1, FR - 1, conv_back)
        windows[3]()
        for cp in cps:
            cp.wait()
        conv_back(0, 0)
        conv_back(FR - 1, 0)
        g1, b1 = vec(ngain, b, 0), vec(nbias, b, 0)
        sacc[0 : 2 * wp, 0:bot] = jnp.zeros((2 * wp, bot), F32)
        w2acc[...] = jnp.zeros((bot, bot), F32)

        def to_z1(f, carry):
            dh2 = ld_h(f, NZ1).astype(BF16)
            xhat = x1b[b, rows(f, NZ1)].astype(F32)
            act, slope = silu_and_slope(xhat * g1 + b1)
            u1 = masked(act).astype(BF16)
            w2acc[...] += dot_tn(u1, dh2)
            z = dot_nt(dh2, w2[b]) * slope
            st_h(f, z, NZ1)
            sacc[0:wp, 0:bot] += rowsum(z)
            sacc[wp : 2 * wp, 0:bot] += rowsum(z * xhat)
            return carry

        loop(0, FR // NZ1, to_z1)
        def tap_grads():
            kacc[...] = jnp.zeros(kacc.shape, F32)

            def frame(f, carry):
                def half(h, carry2):
                    for dt in range(3):
                        acc = [None] * 9
                        for y in range(hh):
                            for s in range(2):
                                base = lead + (y + 1) * wp + s * 8
                                gv = dbuf[h, pl.ds(pl.multiple_of(f * stride, 8) + stride + base, 8)]
                                for dy in range(3):
                                    for dx in range(3):
                                        off = lead + dt * stride + (y + dy) * wp + dx - 1 + s * 8
                                        v = cbuf[b, h, pl.ds(f * stride + off, 8)] * gv
                                        i = dy * 3 + dx
                                        acc[i] = v if acc[i] is None else acc[i] + v
                        for i in range(9):
                            val = acc[i]
                            if dt == 0:
                                val = val * okmask[0, f]
                            if dt == 2:
                                val = val * okmask[1, f]
                            kacc[h, dt * 9 + i] += val
                    return carry2

                loop(0, 2, half)
                return carry

            loop(0, FR, frame)
            for h in range(2):
                ksum[h, 0:27] = jnp.sum(kacc[h], axis=1)
            windows[4]()
            pack_a()
            gen = package(pa_bufs, pa_sem, o_pa.at[b])
            next(gen)
            made.append(gen)

        made = []

        s0, s1 = sums(
            live_total(sacc[0:wp, 0:bot]), live_total(sacc[wp : 2 * wp, 0:bot]), False, tap_grads
        )
        o_nb[b, 0:1] = s0
        o_ng[b, 0:1] = s1
        k1 = g1 * inv1[b]
        c0, c1 = s0 * (1.0 / n_total), s1 * (1.0 / n_total)

        def to_dh1(f, carry):
            xhat = x1b[b, rows(f)].astype(F32)
            x1b[b, rows(f)] = masked(k1 * (ld_h(f) - c0 - xhat * c1)).astype(BF16)
            return carry

        loop(0, FR, to_dh1)

        def w1_grad():
            wacc[...] = jnp.zeros((bot, width), F32)

            def to_w1(f, carry):
                left = x1b[b, rows(f, NW)]
                for c in range(chunks):
                    wacc[:, chunk(c)] += dot_tn(left, flat(act_src, f, c, NW))
                return carry

            loop(0, FR // NW, to_w1)
            pack_b()
            gen = package(pb_bufs, pb_sem, o_pb.at[b])
            next(gen)
            return gen

        return w1_grad, made[0]

    def nothing():
        pass

    w1_grad, gen_a = block_backward(1, a1, [nothing] * 5)
    g3, b3 = wvec(wgain, 0), wvec(wbias, 0)
    nxhat = mean3[0] * inv3[0]
    sacc[...] = jnp.zeros(sacc.shape, F32)

    def middle(f, carry):
        left = u2b[0, rows(f, NM)]
        dh1 = x1b[1, rows(f, NM)]
        for c in range(chunks):
            s = slice(c * 256, c * 256 + 256)
            grad = dot_nt(dh1, w1[1, chunk(c), :]) + flat(pbuf, f, c, NM).astype(F32)
            h3 = dot_nn(left, w3[0, :, chunk(c)])
            xhat = h3 * inv3[0][:, s] - nxhat[:, s]
            pre = flat(a0, f, c, NM).astype(F32) + (xhat * g3[:, s] + b3[:, s])
            _, slope = silu_and_slope(pre)
            grad = grad * slope
            put(pbuf, f, c, grad.astype(BF16), NM)
            sacc[0:wp, chunk(c)] += rowsum(grad)
            sacc[wp : 2 * wp, chunk(c)] += rowsum(grad * xhat)
        return carry

    advance(gen_a)
    loop(0, FR // NM, middle)
    sum_p, sum_px = live_total(sacc[0:wp]), live_total(sacc[wp : 2 * wp])
    gens = []

    def window0():
        gens.append(w1_grad())
        advance(gen_a)

    def window1():
        pass

    def window2():
        advance(gen_a, gens[0])

    def window3():
        advance(gen_a, gens[0])

    def window4():
        advance(gens[0])
        finish(gen_a)

    w1_last, last_a = block_backward(0, a0, [window0, window1, window2, window3, window4])
    finish(gens[0])
    last_b = w1_last()
    advance(last_a)

    def last(f, carry):
        @pl.when(f >= 2)
        def _():
            out_copy(f - 2, gw).wait()

        slot = lax.rem(f, 2)
        dh1 = x1b[0, rows(f)]
        for c in range(chunks):
            grad = dot_nt(dh1, w1[0, chunk(c), :]) + flat(pbuf, f, c).astype(F32)
            ost[slot, :, :, chunk(c)] = grad.astype(BF16).reshape(hh, wp, 256)[:, 0:ww]
        out_copy(f, gw).start()
        return carry

    half_way = FR // 2
    loop(0, half_way, last)
    advance(last_a, last_b)
    loop(half_way, FR, last)
    out_copy(FR - 2, gw).wait()
    out_copy(FR - 1, gw).wait()
    ret_g = swap_out(gw, gr, 1)
    for _ in range(8):
        advance(last_a, last_b)
    finish(last_a)
    finish(last_b)
    ret_a.wait()
    ret_g.wait()


def run_main(dims, held, okmask, frames, gout, w1, w2, w3, taps, ngain, nbias, wgain, wbias):
    n_col, n_ta, cap, hh, ww, width, bot = dims
    n_dev = n_col * n_ta
    extra = cap - FR
    rf = hh * 16
    conv_rows = 8 + (FR + 2) * (hh + 2) * 16 + 8
    conv_rows = -(-conv_rows // 64) * 64
    sds = jax.ShapeDtypeStruct
    la, lb = width // 2 + 256, width // 2

    def piece_bufs(lanes):
        halls = [(16, 1)] if n_dev == 32 else [(n_col, 4), (n_ta // 2, 1)]
        return [
            pltpu.VMEM((2, 16, 16, lanes), BF16),
            pltpu.VMEM((16, 16, lanes), BF16),
            pltpu.VMEM((2, 16, 16, lanes), BF16),
        ] + [pltpu.VMEM((n, size, 16, lanes), BF16) for n, size in halls]

    n_sems = 2 * (2 + 2 * (1 if n_dev == 32 else 2)) + 1
    outs = (
        sds((FR, hh, ww, width), BF16),
        sds((extra, hh, ww, width), BF16),
        sds((FR, hh, ww, width), BF16),
        sds((extra, hh, ww, width), BF16),
        sds((2, 2, 16, 16, la), BF16),
        sds((2, 2, 16, 16, lb), BF16),
        sds((2, 2, bot), F32),
        sds((2, 2, bot), F32),
        sds((2, width), F32),
        sds((2, width), F32),
    )
    vm = pltpu.VMEM
    dma = pltpu.SemaphoreType.DMA
    scratch = [
        vm((cap + extra, hh, ww, width), BF16),
        vm((FR, hh, 16, width), BF16),
        vm((FR, hh, 16, width), BF16),
        vm((FR, hh, 16, width), BF16),
        vm(((2 if n_dev <= 64 else 1) * rf, width), BF16),
        vm((2, hh, ww, width), BF16),
        vm((2, FR * rf, bot), BF16),
        vm((2, FR * rf, 128), F32),
        vm((2, FR * rf, bot), BF16),
        vm((2, FR * rf, bot), BF16),
        vm((2, 2, conv_rows, 128), F32),
        vm((2, conv_rows, 128), F32),
        vm((bot, width), F32),
        vm((bot, bot), F32),
        vm((2, 27, 8, 128), F32),
        vm((2, 32, 128), F32),
        vm((2, n_dev if n_dev <= 64 else 1, 2, bot), F32),
        vm((2, n_ta, 2, width), F32),
        vm((2, n_col, 2, width), F32),
        vm((32, width), F32),
        vm((2, 32, 128), F32),
        piece_bufs(la),
        piece_bufs(lb),
        dma((1,)),
        dma((6,)),
        dma((3, 2, 2)),
        dma((2,)),
        dma((n_sems,)),
        dma((n_sems,)),
        dma((2,)),
        dma((2,)),
        dma((2,)),
        dma((2,)),
        dma((2,)),
        dma((2,)),
    ]
    return pl.pallas_call(
        functools.partial(main_kernel, dims),
        out_shape=outs,
        in_specs=[SM, SM, ANY, ANY] + [VM] * 8,
        out_specs=(ANY,) * 6 + (VM,) * 4,
        scratch_shapes=scratch,
        compiler_params=pltpu.CompilerParams(
            collective_id=0, has_side_effects=True, vmem_limit_bytes=66_500_000
        ),
        name="blocks",
    )(held, okmask, frames, gout, w1, w2, w3, taps, ngain, nbias, wgain, wbias)


def place_kernel(
    cap,
    held,
    a2w,
    a2r,
    gw,
    gr,
    pa,
    pb,
    i_ng,
    i_nb,
    i_wg,
    i_wb,
    out,
    grad,
    o_w1,
    o_w2,
    o_k,
    o_w3,
    o_ng,
    o_nb,
    o_wg,
    o_wb,
    work,
    zero,
    in_sem,
    out_sem,
):
    half = pb.shape[-1]
    extra = cap - FR
    col, ta = lax.axis_index("col"), lax.axis_index("ta")
    odd = lax.rem(ta, 2)
    first = held[col, ta - odd]
    live = jnp.where(odd == 0, first, 2 * FR - first)
    arrays = ((a2w, a2r, out), (gw, gr, grad))

    def source(j):
        pos = jnp.where(odd == 0, j, first + j)
        mine = jnp.where(odd == 0, pos < FR, pos >= FR)
        own = jnp.where(odd == 0, pos, pos - FR)
        far = jnp.where(odd == 0, pos - FR, pos - (FR - extra))
        return mine, own, far

    def fetch(j, carry):
        mine, own, far = source(j)
        for i, (near, back, _) in enumerate(arrays):

            @pl.when((j < live) & mine)
            def _():
                pltpu.make_async_copy(near.at[own], work.at[i, j], in_sem.at[i, j]).start()

            @pl.when((j < live) & jnp.logical_not(mine))
            def _():
                pltpu.make_async_copy(back.at[far], work.at[i, j], in_sem.at[i, j]).start()

        return carry

    loop(0, cap, fetch)
    zero[...] = jnp.zeros(zero.shape, BF16)

    def clear(j, carry):
        for i, (_, _, dst) in enumerate(arrays):
            pltpu.make_async_copy(zero, dst.at[j], out_sem.at[i]).start()
        return carry

    lax.fori_loop(live, cap, clear, 0)

    def ship(j, carry):
        for i, (near, _, dst) in enumerate(arrays):
            pltpu.make_async_copy(near.at[0], work.at[i, j], in_sem.at[i, j]).wait()
            pltpu.make_async_copy(work.at[i, j], dst.at[j], out_sem.at[i]).start()
        return carry

    lax.fori_loop(0, live, ship, 0)
    o_ng[...] = i_ng[...]
    o_nb[...] = i_nb[...]
    o_wg[...] = i_wg[...]
    o_wb[...] = i_wb[...]
    for b in range(2):
        for p in range(2):
            cols = slice(p * 128, p * 128 + 128)
            taps = pa[b, p, 0:2, :, half + 128 :].astype(F32).reshape(32, 128)
            o_k[:, b, cols] = taps[0:27]
            mid = pa[b, p, :, :, half : half + 128].astype(F32)
            o_w2[b, :, cols] = mid.reshape(256, 128)
            cols = slice(p * half, p * half + half)
            o_w3[b, :, cols] = pa[b, p, :, :, 0:half].astype(F32).reshape(256, half)
            o_w1[b, cols, :] = pb[b, p].astype(F32).reshape(256, half).T
    pltpu.make_async_copy(out, out, out_sem.at[0]).wait()
    pltpu.make_async_copy(grad, grad, out_sem.at[1]).wait()


def place(dims, held, *parts):
    n_col, n_ta, cap, hh, ww, width, bot = dims
    sds = jax.ShapeDtypeStruct
    return pl.pallas_call(
        functools.partial(place_kernel, cap),
        out_shape=(sds((cap, hh, ww, width), BF16),) * 2
        + (
            sds((2, width, bot), F32),
            sds((2, bot, bot), F32),
            sds((27, 2, bot), F32),
            sds((2, bot, width), F32),
            sds((2, 2, bot), F32),
            sds((2, 2, bot), F32),
            sds((2, width), F32),
            sds((2, width), F32),
        ),
        in_specs=[SM] + [ANY] * 4 + [VM] * 6,
        out_specs=(ANY, ANY) + (VM,) * 8,
        scratch_shapes=[
            pltpu.VMEM((2, cap, hh, ww, width), BF16),
            pltpu.VMEM((hh, ww, width), BF16),
            pltpu.SemaphoreType.DMA((2, cap)),
            pltpu.SemaphoreType.DMA((2,)),
        ],
        compiler_params=pltpu.CompilerParams(vmem_limit_bytes=64_000_000),
        name="place",
    )(held, *parts)


def body(
    n_col,
    n_ta,
    frames,
    out_grad,
    held,
    clip_stride,
    w_reduce,
    w_mid,
    depth_kernel,
    w_expand,
    narrow_gain,
    narrow_bias,
    wide_gain,
    wide_bias,
):
    cap, hh, ww, width = frames.shape
    dims = (n_col, n_ta, cap, hh, ww, width, w_mid.shape[1])
    col, ta = lax.axis_index("col"), lax.axis_index("ta")
    lengths = 8 // lax.dynamic_index_in_dim(clip_stride, col, 0, keepdims=False)
    clips = lengths.shape[0]
    before = jnp.arange(clips)[:, None] < jnp.arange(clips)[None, :]
    starts = jnp.sum(jnp.where(before, lengths[:, None], 0), axis=0)
    ids = ta * FR + jnp.arange(FR + 1)
    begins = jnp.any(starts[None, :] == ids[:, None], axis=1) | (ids >= n_ta * FR)
    ok = jnp.logical_not(begins).astype(F32)
    okmask = jnp.stack([ok[:-1], ok[1:]])
    parts = run_main(
        dims,
        held,
        okmask,
        frames,
        out_grad,
        w_reduce,
        w_mid,
        w_expand,
        jnp.swapaxes(depth_kernel, 0, 1),
        narrow_gain,
        narrow_bias,
        wide_gain,
        wide_bias,
    )
    outs = place(dims, held, *parts)
    return outs[:4] + (jnp.swapaxes(outs[4], 0, 1),) + outs[5:]


def solution(mesh):
    split = P(("col", "ta"), None, None, None)
    return jax.shard_map(
        functools.partial(body, mesh.shape["col"], mesh.shape["ta"]),
        mesh=mesh,
        in_specs=(split, split) + (P(),) * 10,
        out_specs=(split, split) + (P(),) * 8,
        check_vma=False,
    )
```

```python
import functools

import jax
import jax.numpy as jnp
from jax import lax
from jax.experimental import pallas as pl
from jax.experimental.pallas import tpu as pltpu
from jax.sharding import PartitionSpec as P

FR = 12
EPS = 1e-05
MESH = pl.DeviceIdType.MESH
F32 = jnp.float32
BF16 = jnp.bfloat16
ANY = pl.BlockSpec(memory_space=pl.ANY)
VM = pl.BlockSpec(memory_space=pltpu.VMEM)
SM = pl.BlockSpec(memory_space=pltpu.SMEM)


def loop(low, high, step):
    lax.fori_loop(low, high, step, 0)


def dot_nn(left, right):
    return lax.dot_general(left, right, (((1,), (0,)), ((), ())), preferred_element_type=F32)


def dot_nt(left, right):
    return lax.dot_general(left, right, (((1,), (1,)), ((), ())), preferred_element_type=F32)


def dot_tn(left, right):
    return lax.dot_general(left, right, (((0,), (0,)), ((), ())), preferred_element_type=F32)


def silu(values):
    half = 0.5 * values
    return half * jnp.tanh(half) + half


def silu_and_slope(values):
    half = 0.5 * values
    tan = jnp.tanh(half)
    act = half * tan + half
    sig = 0.5 * tan + 0.5
    return act, act + sig * (1.0 - act)


def main_kernel(
    dims,
    held,
    okmask,
    frames,
    gout,
    w1,
    w2,
    w3,
    taps,
    ngain,
    nbias,
    wgain,
    wbias,
    a2w,
    a2r,
    gw,
    gr,
    o_pa,
    o_pb,
    o_ng,
    o_nb,
    o_wg,
    o_wb,
    pool,
    a0,
    a1,
    pbuf,
    tile,
    ost,
    u2b,
    hbuf,
    x1b,
    x2b,
    cbuf,
    dbuf,
    wacc,
    w2acc,
    kacc,
    ksum,
    nbuf,
    tbuf,
    gbuf,
    sacc,
    prm,
    pa_bufs,
    pb_bufs,
    in_sem,
    rem_sem,
    halo_sem,
    out_sem,
    pa_sem,
    pb_sem,
    ns_sem,
    nr_sem,
    ts_sem,
    tr_sem,
    gs_sem,
    gr_sem,
):
    n_col, n_ta, cap, hh, ww, width, bot = dims
    n_dev = n_col * n_ta
    extra = cap - FR
    N1, N3, NA, NZ2, NZ1, NW, NM = (3, 2, 2, 2, 3, 4, 2) if n_dev <= 64 else (1,) * 7
    wp = 16
    rf = hh * wp
    stride = (hh + 2) * wp
    lead = 8
    n_local = float(FR * hh * ww)
    n_total = n_local * n_dev
    chunks = width // 256
    col, ta = lax.axis_index("col"), lax.axis_index("ta")
    me = col * n_ta + ta
    odd = lax.rem(ta, 2)
    sib = (col, ta + 1 - 2 * odd)
    nxt = (col, lax.rem(ta + 1, n_ta))
    prv = (col, lax.rem(ta + n_ta - 1, n_ta))

    def peer(k):
        other = lax.rem(me + k, n_dev)
        return (lax.div(other, n_ta), lax.rem(other, n_ta))

    own_cp = pltpu.make_async_copy(frames, pool.at[pl.ds(0, cap)], in_sem.at[0])
    own_cp.start()
    barrier = pltpu.get_barrier_semaphore()

    def greet(k, carry):
        pl.semaphore_signal(barrier, inc=1, device_id=peer(k), device_id_type=MESH)
        return carry

    loop(1, n_dev, greet)

    live_row = (lax.broadcasted_iota(jnp.int32, (wp, 1), 0) < ww).astype(F32)

    def masked(values):
        c = values.shape[-1]
        return (values.reshape(-1, wp, c) * live_row[None]).reshape(-1, c)

    def rowsum(values):
        return jnp.sum(values.reshape(-1, wp, values.shape[-1]), axis=0)

    def live_total(acc):
        return jnp.sum(acc * live_row, axis=0, keepdims=True)

    def zero_tile(f, carry):
        a0[f] = jnp.zeros((hh, wp, width), BF16)
        pbuf[f] = jnp.zeros((hh, wp, width), BF16)
        return carry

    loop(0, FR, zero_tile)
    for ref in (cbuf.at[0], cbuf.at[1], dbuf):

        def zero_conv(i, carry, ref=ref):
            for h in range(2):
                ref[h, pl.ds(pl.multiple_of(i * 64, 64), 64)] = jnp.zeros((64, 128), F32)
            return carry

        loop(0, ref.shape[1] // 64, zero_conv)

    pl.semaphore_wait(barrier, n_dev - 1)

    def swap_in(src):
        cp = pltpu.make_async_remote_copy(
            src_ref=src.at[pl.ds((1 - odd) * FR, extra)],
            dst_ref=pool.at[pl.ds(cap, extra)],
            send_sem=rem_sem.at[0],
            recv_sem=rem_sem.at[1],
            device_id=sib,
            device_id_type=MESH,
        )
        cp.start()
        return cp

    first_held = held[col, ta - odd]

    def gather_into(dst):
        def pick_frame(j, carry):
            own = jnp.where(odd == 0, j, j + FR - first_held)
            far = jnp.where(odd == 0, j - first_held, j)
            mine = jnp.where(odd == 0, j < first_held, own >= 0)
            pick = jnp.where(mine, jnp.clip(own, 0, cap - 1), cap + jnp.clip(far, 0, extra - 1))
            dst[j, :, 0:ww, :] = pool[pick]
            return carry

        loop(0, FR, pick_frame)

    cp = swap_in(frames)
    own_cp.wait()
    cp.wait()
    gather_into(a0)
    own_cp = pltpu.make_async_copy(gout, pool.at[pl.ds(0, cap)], in_sem.at[0])
    own_cp.start()

    def along_ta(k):
        return (col, lax.rem(ta + k, n_ta))

    def along_col(k):
        return (lax.rem(col + k, n_col), ta)

    stages = {
        "all": (nbuf, ns_sem, nr_sem, n_dev, me, peer),
        "ta": (tbuf, ts_sem, tr_sem, n_ta, ta, along_ta),
        "col": (gbuf, gs_sem, gr_sem, n_col, col, along_col),
    }
    used = {"all": 0, "ta": 0, "col": 0}

    def exchange(name, values, between=None):
        buf, ssem, rsem, size, mine, who = stages[name]
        par = used[name] % 2
        used[name] += 1
        lanes = pl.ds(0, values.shape[1])
        buf[par, mine, :, lanes] = values

        def send(k, carry):
            pltpu.make_async_remote_copy(
                src_ref=buf.at[par, mine, :, lanes],
                dst_ref=buf.at[par, mine, :, lanes],
                send_sem=ssem.at[par],
                recv_sem=rsem.at[par],
                device_id=who(k),
                device_id_type=MESH,
            ).start()
            return carry

        loop(1, size, send)
        if between is not None:
            between()
        part = buf.at[par, pl.ds(0, size - 1), :, lanes]
        pltpu.make_async_copy(part, part, rsem.at[par]).wait()
        pltpu.make_async_copy(part, part, ssem.at[par]).wait()
        return buf[par, :, :, lanes]

    def merge(name, mean_l, m2_l, per, size, between=None):
        got = exchange(name, jnp.concatenate([mean_l, m2_l], axis=0), between)
        total = jnp.sum(got, axis=0)
        mean = total[0:1] * (1.0 / size)
        dev = got - mean[None]
        spread = jnp.sum(dev * dev, axis=0)[0:1]
        return mean, total[1:2] + per * spread

    def moments(mean_l, m2_l, wide, between=None):
        if wide or n_dev > 64:
            mean, m2 = merge("ta", mean_l, m2_l, n_local, n_ta, between)
            mean, m2 = merge("col", mean, m2, n_local * n_ta, n_col)
        else:
            mean, m2 = merge("all", mean_l, m2_l, n_local, n_dev, between)
        return mean, lax.rsqrt(m2 * (1.0 / n_total) + EPS)

    def sums(s0, s1, wide, between=None, later=None):
        total = jnp.concatenate([s0, s1], axis=0)
        if wide or n_dev > 64:
            total = jnp.sum(exchange("ta", total, between), axis=0)
            total = jnp.sum(exchange("col", total, later), axis=0)
        else:
            total = jnp.sum(exchange("all", total, between), axis=0)
        return total[0:1], total[1:2]

    def rows(f, n=1):
        return pl.ds(pl.multiple_of(f * (n * rf), rf), n * rf)

    def ld_h(f, n=1):
        return jnp.concatenate([hbuf[0, rows(f, n)], hbuf[1, rows(f, n)]], axis=1)

    def st_h(f, values, n=1):
        hbuf[0, rows(f, n)] = values[:, :128]
        hbuf[1, rows(f, n)] = values[:, 128:]

    def conv_rows(slot):
        return pl.ds(pl.multiple_of(lead + slot * stride + wp, 8), rf)

    def st_conv(ref, slot, values):
        ref[0, conv_rows(slot)] = values[:, :128]
        ref[1, conv_rows(slot)] = values[:, 128:]

    def local_m2(mean_l):
        sacc[0:wp, 0:bot] = jnp.zeros((wp, bot), F32)

        def to_m2(f, carry):
            d = ld_h(f) - mean_l
            sacc[0:wp, 0:bot] += rowsum(d * d)
            return carry

        loop(0, FR, to_m2)
        return live_total(sacc[0:wp, 0:bot])

    def conv_frame(src, wrow, f, flip):
        def half(h, carry):
            wts = []
            w_all = prm[h]
            for dt in range(3):
                scale = None
                if dt == 0:
                    scale = okmask[0, f]
                if dt == 2:
                    scale = okmask[1, f]
                for sp in range(9):
                    idx = dt * 9 + sp
                    row = w_all[26 - idx : 27 - idx] if flip else w_all[idx : idx + 1]
                    if scale is not None:
                        row = row * scale
                    wts.append(jnp.broadcast_to(row, (8, 128)))
            out = []
            for y in range(hh):
                for s in range(2):
                    acc = [None, None, None]
                    for dt in range(3):
                        for dy in range(3):
                            for dx in range(3):
                                off = lead + dt * stride + (y + dy) * wp + dx - 1 + s * 8
                                v = src[h, pl.ds(f * stride + off, 8)]
                                term = v * wts[dt * 9 + dy * 3 + dx]
                                acc[dx] = term if acc[dx] is None else acc[dx] + term
                    val = acc[0] + acc[1] + acc[2]
                    hbuf[h, pl.ds(pl.multiple_of(f * rf + y * wp + s * 8, 8), 8)] = val
            return carry

        loop(0, 2, half)

    def load_taps(b):
        k = taps[...].astype(F32)[:, b]
        prm[0, 0:27] = k[:, :128]
        prm[1, 0:27] = k[:, 128:]

    def send_halos(ref, which):
        cps = []
        for i, (slot, land, dev) in enumerate(((1, FR + 1, prv), (FR, 0, nxt))):
            cp = pltpu.make_async_remote_copy(
                src_ref=ref.at[:, pl.ds(lead + slot * stride + wp, rf)],
                dst_ref=ref.at[:, pl.ds(lead + land * stride + wp, rf)],
                send_sem=halo_sem.at[which, i, 0],
                recv_sem=halo_sem.at[which, i, 1],
                device_id=dev,
                device_id_type=MESH,
            )
            cp.start()
            cps.append(cp)
        return cps

    def edge_first(step):
        step(0, 0)
        step(FR - 1, 0)

    def chunk(c):
        return pl.ds(c * 256, 256)

    def flat(ref, f, c, n=1):
        return ref[pl.ds(f * n, n), :, :, chunk(c)].reshape(n * rf, 256)

    def put(ref, f, c, values, n=1):
        ref[pl.ds(f * n, n), :, :, chunk(c)] = values.reshape(n, hh, wp, 256)

    nz = n_ta // 2
    zpos = lax.div(ta, 2)
    if n_dev == 32:
        first = col * nz + zpos
        levels = [
            (
                n_dev // 2,
                16,
                first,
                lambda i: (lax.div(i, nz), 2 * lax.rem(i, nz) + odd),
            )
        ]
    else:
        levels = [
            (n_col, 4, col, lambda i: (i, ta)),
            (nz, 4, zpos, lambda i: (col, 2 * i + odd)),
        ]

    def package(bufs, sems, dst):
        send, land, final = bufs[0], bufs[1], bufs[2]
        halls = bufs[3:]

        def remote(src, to, i, dev):
            return pltpu.make_async_remote_copy(
                src_ref=src,
                dst_ref=to,
                send_sem=sems.at[2 * i],
                recv_sem=sems.at[2 * i + 1],
                device_id=dev,
                device_id_type=MESH,
            )

        cp = remote(send.at[1 - odd], land, 0, sib)
        cp.start()
        yield
        cp.wait()

        def add(r, carry):
            both = send[odd, r].astype(F32) + land[r].astype(F32)
            send[odd, r] = both.astype(BF16)
            return carry

        loop(0, 16, add)
        off, size = 0, 16
        spans = []
        for i, (n, m, mine, who) in enumerate(levels):
            hall = halls[i]
            size = size // m

            def scatter(k, carry, hall=hall, size=size, off=off, n=n, m=m, mine=mine, who=who, i=i):
                other = lax.rem(mine + k, n)
                part = send.at[odd, pl.ds(off + lax.rem(other, m) * size, size)]
                remote(part, hall.at[mine], 1 + i, who(other)).start()
                return carry

            loop(1, n, scatter)
            off = off + lax.rem(mine, m) * size
            hall[mine] = send[odd, pl.ds(off, size)]
            yield
            part = hall.at[pl.ds(0, n - 1)]
            pltpu.make_async_copy(part, part, sems.at[3 + 2 * i]).wait()
            pltpu.make_async_copy(part, part, sems.at[2 + 2 * i]).wait()
            last = i == len(levels) - 1

            def reduce(q, carry, hall=hall, n=n, off=off, last=last):
                total = jnp.sum(hall[:, q].astype(F32), axis=0).astype(BF16)
                if last:
                    final[odd, off + q] = total
                else:
                    send[odd, off + q] = total
                return carry

            loop(0, size, reduce)
            spans.append((off, size))
        base = 1 + len(levels)
        for i in reversed(range(len(levels))):
            n, m, mine, who = levels[i]
            off, size = spans[i]

            def spread(k, carry, off=off, size=size, m=m, mine=mine, who=who, i=i):
                other = lax.div(mine, m) * m + lax.rem(lax.rem(mine, m) + k, m)
                part = final.at[odd, pl.ds(off, size)]
                remote(part, part, base + i, who(other)).start()
                return carry

            loop(1, m, spread)
            yield
            part = final.at[odd, pl.ds(0, (m - 1) * size)]
            pltpu.make_async_copy(part, part, sems.at[2 * (base + i) + 1]).wait()
            pltpu.make_async_copy(part, part, sems.at[2 * (base + i)]).wait()
        cp = remote(final.at[odd], final.at[odd], base + len(levels), sib)
        cp.start()
        yield
        cp.wait()
        cp = pltpu.make_async_copy(final, dst, sems.at[2 * (base + len(levels)) + 2])
        cp.start()
        yield
        cp.wait()
        yield

    def finish(gen):
        for _ in gen:
            pass

    def advance(*gens):
        for gen in gens:
            next(gen, None)

    ksum[...] = jnp.zeros(ksum.shape, F32)
    pa_bufs[0][...] = jnp.zeros(pa_bufs[0].shape, BF16)
    half_w = width // 2

    def pack_a():
        def step(r, carry):
            rr = pl.ds(pl.multiple_of(r * 16, 16), 16)
            for p in range(2):
                pa_bufs[0][p, r, :, 0:half_w] = wacc[rr, p * half_w : p * half_w + half_w].astype(BF16)
                pa_bufs[0][p, r, :, half_w : half_w + 128] = w2acc[rr, p * 128 : p * 128 + 128].astype(BF16)
            return carry

        loop(0, 16, step)
        for p in range(2):
            for r in range(2):
                pa_bufs[0][p, r, :, half_w + 128 :] = ksum[p, r * 16 : r * 16 + 16].astype(BF16)

    def pack_b():
        def step(r, carry):
            rr = pl.ds(pl.multiple_of(r * 16, 16), 16)
            for p in range(2):
                pb_bufs[0][p, r] = wacc[rr, p * half_w : p * half_w + half_w].astype(BF16)
            return carry

        loop(0, 16, step)

    def first_mm(src, b):
        sacc[0:wp, 0:bot] = jnp.zeros((wp, bot), F32)

        def to_h1(f, carry):
            h1 = dot_nn(src[pl.ds(f * N1, N1)].reshape(N1 * rf, width), w1[b])
            st_h(f, h1, N1)
            sacc[0:wp, 0:bot] += rowsum(h1)
            return carry

        loop(0, FR // N1, to_h1)
        mean_l = live_total(sacc[0:wp, 0:bot]) * (1.0 / n_local)
        return mean_l, local_m2(mean_l)

    inv1, inv2, mean3, inv3 = {}, {}, {}, {}

    def vec(ref, b, j):
        return ref[b].astype(F32)[j : j + 1]

    def wvec(ref, b):
        return ref[...].astype(F32)[b : b + 1]

    def get_gout():
        own_cp.wait()

    def block_forward(b, src, after_first):
        mean_l, m2_l = first_mm(src, b)
        mean, inv = moments(mean_l, m2_l, False, None)
        inv1[b] = inv
        after_first()
        g, bb = vec(ngain, b, 0), vec(nbias, b, 0)

        def to_h2(f, carry):
            xhat = (ld_h(f) - mean) * inv
            x1b[b, rows(f)] = xhat.astype(BF16)
            u1 = masked(silu(xhat * g + bb)).astype(BF16)
            h2 = dot_nn(u1, w2[b]).astype(BF16).astype(F32)
            st_conv(cbuf.at[b], f + 1, h2)
            return carry

        edge_first(to_h2)
        cps = send_halos(cbuf.at[b], b)
        loop(1, FR - 1, to_h2)
        load_taps(b)

        def conv_step(f, carry):
            conv_frame(cbuf.at[b], None, f, False)
            return carry

        loop(1, FR - 1, conv_step)
        for cp in cps:
            cp.wait()
        conv_step(0, 0)
        conv_step(FR - 1, 0)
        sacc[0:wp, 0:bot] = jnp.zeros((wp, bot), F32)

        def dw_sum(f, carry):
            sacc[0:wp, 0:bot] += rowsum(ld_h(f))
            return carry

        loop(0, FR, dw_sum)
        mean_l = live_total(sacc[0:wp, 0:bot]) * (1.0 / n_local)
        m2_l = local_m2(mean_l)
        mean, inv = moments(mean_l, m2_l, False, None)
        inv2[b] = inv
        g, bb = vec(ngain, b, 1), vec(nbias, b, 1)
        sacc[0:wp, 0:bot] = jnp.zeros((wp, bot), F32)

        def to_u2(f, carry):
            xhat = (ld_h(f) - mean) * inv
            x2b[b, rows(f)] = xhat.astype(BF16)
            u2 = masked(silu(xhat * g + bb))
            u2b[b, rows(f)] = u2.astype(BF16)
            sacc[0:wp, 0:bot] += rowsum(u2)
            return carry

        loop(0, FR, to_u2)
        u_mean = live_total(sacc[0:wp, 0:bot]) * (1.0 / n_local)
        pivot = dot_nn(jnp.broadcast_to(u_mean, (16, bot)).astype(BF16), w3[b])[0:1]
        sacc[...] = jnp.zeros(sacc.shape, F32)

        def h3_stats(f, carry):
            left = u2b[b, rows(f, N3)]
            for c in range(chunks):
                h3 = dot_nn(left, w3[b, :, chunk(c)]) - pivot[:, c * 256 : c * 256 + 256]
                sacc[0:wp, chunk(c)] += rowsum(h3)
                sacc[wp : 2 * wp, chunk(c)] += rowsum(h3 * h3)
            return carry

        loop(0, FR // N3, h3_stats)
        s1 = live_total(sacc[0:wp]) * (1.0 / n_local)
        s2 = live_total(sacc[wp : 2 * wp])
        mean3[b], inv3[b] = moments(pivot + s1, s2 - n_local * s1 * s1, True, None)

    def second_in():
        nonlocal cp2
        cp2 = swap_in(gout)

    cp2 = None
    block_forward(0, a0, second_in)

    g3, b3 = wvec(wgain, 0), wvec(wbias, 0)
    sc, sh = g3 * inv3[0], b3 - mean3[0] * g3 * inv3[0]

    def to_a1(f, carry):
        left = u2b[0, rows(f, NA)]
        for c in range(chunks):
            s = slice(c * 256, c * 256 + 256)
            h3 = dot_nn(left, w3[0, :, chunk(c)])
            pre = flat(a0, f, c, NA).astype(F32) + (h3 * sc[:, s] + sh[:, s])
            put(a1, f, c, silu(pre).astype(BF16), NA)
        return carry

    loop(0, FR // NA, to_a1)

    def none():
        pass

    own_cp.wait()
    cp2.wait()
    gather_into(pbuf)
    block_forward(1, a1, none)

    g3, b3 = wvec(wgain, 1), wvec(wbias, 1)
    nxhat = mean3[1] * inv3[1]
    sacc[...] = jnp.zeros(sacc.shape, F32)

    def out_copy(f, dst):
        slot = lax.rem(f, 2)
        return pltpu.make_async_copy(ost.at[slot], dst.at[f], out_sem.at[slot])

    def turn(f, carry):
        @pl.when(f >= 2)
        def _():
            out_copy(f - 2, a2w).wait()

        slot = lax.rem(f, 2)
        left = u2b[1, rows(f)]
        for c in range(chunks):
            s = slice(c * 256, c * 256 + 256)
            h3 = dot_nn(left, w3[1, :, chunk(c)])
            xhat = h3 * inv3[1][:, s] - nxhat[:, s]
            pre = flat(a1, f, c).astype(F32) + (xhat * g3[:, s] + b3[:, s])
            act, slope = silu_and_slope(pre)
            ost[slot, :, :, chunk(c)] = act.astype(BF16).reshape(hh, wp, 256)[:, 0:ww]
            grad = flat(pbuf, f, c).astype(F32) * slope
            put(pbuf, f, c, grad.astype(BF16))
            sacc[0:wp, chunk(c)] += rowsum(grad)
            sacc[wp : 2 * wp, chunk(c)] += rowsum(grad * xhat)
        out_copy(f, a2w).start()
        return carry

    loop(0, FR, turn)
    out_copy(FR - 2, a2w).wait()
    out_copy(FR - 1, a2w).wait()

    def swap_out(src, dst, i):
        cp = pltpu.make_async_remote_copy(
            src_ref=src.at[pl.ds((1 - odd) * (FR - extra), extra)],
            dst_ref=dst,
            send_sem=rem_sem.at[2 + i],
            recv_sem=rem_sem.at[4 + i],
            device_id=sib,
            device_id_type=MESH,
        )
        cp.start()
        return cp

    ret_a = swap_out(a2w, a2r, 0)
    sum_p, sum_px = live_total(sacc[0:wp]), live_total(sacc[wp : 2 * wp])

    def block_backward(b, act_src, windows):
        s0, s1 = sums(sum_p, sum_px, True, windows[0], windows[1])
        o_wb[b : b + 1] = s0
        o_wg[b : b + 1] = s1
        k3 = wvec(wgain, b) * inv3[b]
        c0, c1 = s0 * (1.0 / n_total), s1 * (1.0 / n_total)
        ch = k3 * c1 * inv3[b]
        cc = ch * mean3[b] - k3 * c0
        g2, b2 = vec(ngain, b, 1), vec(nbias, b, 1)
        sacc[0 : 2 * wp, 0:bot] = jnp.zeros((2 * wp, bot), F32)
        wacc[...] = jnp.zeros((bot, width), F32)

        def to_z2(f, carry):
            left = u2b[b, rows(f, NZ2)]
            for c in range(chunks):
                s = slice(c * 256, c * 256 + 256)
                h3 = dot_nn(left, w3[b, :, chunk(c)])
                dh3 = flat(pbuf, f, c, NZ2).astype(F32) * k3[:, s] - h3 * ch[:, s] + cc[:, s]
                tile[:, chunk(c)] = dh3.astype(BF16)
            du2 = dot_nt(tile[...], w3[b])
            for c in range(chunks):
                wacc[:, chunk(c)] += dot_tn(left, tile[:, chunk(c)])
            xhat = x2b[b, rows(f, NZ2)].astype(F32)
            _, slope = silu_and_slope(xhat * g2 + b2)
            z = du2 * slope
            st_h(f, z, NZ2)
            sacc[0:wp, 0:bot] += rowsum(z)
            sacc[wp : 2 * wp, 0:bot] += rowsum(z * xhat)
            return carry

        loop(0, FR // NZ2, to_z2)
        s0, s1 = sums(
            live_total(sacc[0:wp, 0:bot]), live_total(sacc[wp : 2 * wp, 0:bot]), False, windows[2]
        )
        o_nb[b, 1:2] = s0
        o_ng[b, 1:2] = s1
        k2 = g2 * inv2[b]
        c0, c1 = s0 * (1.0 / n_total), s1 * (1.0 / n_total)

        def to_ddw(f, carry):
            xhat = x2b[b, rows(f)].astype(F32)
            st_conv(dbuf, f + 1, masked(k2 * (ld_h(f) - c0 - xhat * c1)))
            return carry

        edge_first(to_ddw)
        cps = send_halos(dbuf, 2)
        loop(1, FR - 1, to_ddw)
        load_taps(b)

        def conv_back(f, carry):
            conv_frame(dbuf, None, f, True)
            return carry

        loop(1, FR - 1, conv_back)
        windows[3]()
        for cp in cps:
            cp.wait()
        conv_back(0, 0)
        conv_back(FR - 1, 0)
        g1, b1 = vec(ngain, b, 0), vec(nbias, b, 0)
        sacc[0 : 2 * wp, 0:bot] = jnp.zeros((2 * wp, bot), F32)
        w2acc[...] = jnp.zeros((bot, bot), F32)

        def to_z1(f, carry):
            dh2 = ld_h(f, NZ1).astype(BF16)
            xhat = x1b[b, rows(f, NZ1)].astype(F32)
            act, slope = silu_and_slope(xhat * g1 + b1)
            u1 = masked(act).astype(BF16)
            w2acc[...] += dot_tn(u1, dh2)
            z = dot_nt(dh2, w2[b]) * slope
            st_h(f, z, NZ1)
            sacc[0:wp, 0:bot] += rowsum(z)
            sacc[wp : 2 * wp, 0:bot] += rowsum(z * xhat)
            return carry

        loop(0, FR // NZ1, to_z1)
        def tap_grads():
            kacc[...] = jnp.zeros(kacc.shape, F32)

            def frame(f, carry):
                def half(h, carry2):
                    for dt in range(3):
                        acc = [None] * 9
                        for y in range(hh):
                            for s in range(2):
                                base = lead + (y + 1) * wp + s * 8
                                gv = dbuf[h, pl.ds(pl.multiple_of(f * stride, 8) + stride + base, 8)]
                                for dy in range(3):
                                    for dx in range(3):
                                        off = lead + dt * stride + (y + dy) * wp + dx - 1 + s * 8
                                        v = cbuf[b, h, pl.ds(f * stride + off, 8)] * gv
                                        i = dy * 3 + dx
                                        acc[i] = v if acc[i] is None else acc[i] + v
                        for i in range(9):
                            val = acc[i]
                            if dt == 0:
                                val = val * okmask[0, f]
                            if dt == 2:
                                val = val * okmask[1, f]
                            kacc[h, dt * 9 + i] += val
                    return carry2

                loop(0, 2, half)
                return carry

            loop(0, FR, frame)
            for h in range(2):
                ksum[h, 0:27] = jnp.sum(kacc[h], axis=1)
            windows[4]()
            pack_a()
            gen = package(pa_bufs, pa_sem, o_pa.at[b])
            next(gen)
            made.append(gen)

        made = []

        s0, s1 = sums(
            live_total(sacc[0:wp, 0:bot]), live_total(sacc[wp : 2 * wp, 0:bot]), False, tap_grads
        )
        o_nb[b, 0:1] = s0
        o_ng[b, 0:1] = s1
        k1 = g1 * inv1[b]
        c0, c1 = s0 * (1.0 / n_total), s1 * (1.0 / n_total)

        def to_dh1(f, carry):
            xhat = x1b[b, rows(f)].astype(F32)
            x1b[b, rows(f)] = masked(k1 * (ld_h(f) - c0 - xhat * c1)).astype(BF16)
            return carry

        loop(0, FR, to_dh1)

        def w1_grad():
            wacc[...] = jnp.zeros((bot, width), F32)

            def to_w1(f, carry):
                left = x1b[b, rows(f, NW)]
                for c in range(chunks):
                    wacc[:, chunk(c)] += dot_tn(left, flat(act_src, f, c, NW))
                return carry

            loop(0, FR // NW, to_w1)
            pack_b()
            gen = package(pb_bufs, pb_sem, o_pb.at[b])
            next(gen)
            return gen

        return w1_grad, made[0]

    def nothing():
        pass

    w1_grad, gen_a = block_backward(1, a1, [nothing] * 5)
    g3, b3 = wvec(wgain, 0), wvec(wbias, 0)
    nxhat = mean3[0] * inv3[0]
    sacc[...] = jnp.zeros(sacc.shape, F32)

    def middle(f, carry):
        left = u2b[0, rows(f, NM)]
        dh1 = x1b[1, rows(f, NM)]
        for c in range(chunks):
            s = slice(c * 256, c * 256 + 256)
            grad = dot_nt(dh1, w1[1, chunk(c), :]) + flat(pbuf, f, c, NM).astype(F32)
            h3 = dot_nn(left, w3[0, :, chunk(c)])
            xhat = h3 * inv3[0][:, s] - nxhat[:, s]
            pre = flat(a0, f, c, NM).astype(F32) + (xhat * g3[:, s] + b3[:, s])
            _, slope = silu_and_slope(pre)
            grad = grad * slope
            put(pbuf, f, c, grad.astype(BF16), NM)
            sacc[0:wp, chunk(c)] += rowsum(grad)
            sacc[wp : 2 * wp, chunk(c)] += rowsum(grad * xhat)
        return carry

    advance(gen_a)
    loop(0, FR // NM, middle)
    sum_p, sum_px = live_total(sacc[0:wp]), live_total(sacc[wp : 2 * wp])
    gens = []

    def window0():
        gens.append(w1_grad())
        advance(gen_a)

    def window1():
        pass

    def window2():
        advance(gen_a, gens[0])

    def window3():
        advance(gen_a, gens[0])

    def window4():
        advance(gens[0])
        finish(gen_a)

    w1_last, last_a = block_backward(0, a0, [window0, window1, window2, window3, window4])
    finish(gens[0])
    advance(last_a)
    last_b = w1_last()
    advance(last_a)

    def last(f, carry):
        @pl.when(f >= 2)
        def _():
            out_copy(f - 2, gw).wait()

        slot = lax.rem(f, 2)
        dh1 = x1b[0, rows(f)]
        for c in range(chunks):
            grad = dot_nt(dh1, w1[0, chunk(c), :]) + flat(pbuf, f, c).astype(F32)
            ost[slot, :, :, chunk(c)] = grad.astype(BF16).reshape(hh, wp, 256)[:, 0:ww]
        out_copy(f, gw).start()
        return carry

    third = FR // 3
    loop(0, third, last)
    advance(last_b, last_a)
    loop(third, 2 * third, last)
    advance(last_b, last_a)
    loop(2 * third, FR, last)
    out_copy(FR - 2, gw).wait()
    out_copy(FR - 1, gw).wait()
    ret_g = swap_out(gw, gr, 1)
    for _ in range(8):
        advance(last_a, last_b)
    finish(last_a)
    finish(last_b)
    ret_a.wait()
    ret_g.wait()


def run_main(dims, held, okmask, frames, gout, w1, w2, w3, taps, ngain, nbias, wgain, wbias):
    n_col, n_ta, cap, hh, ww, width, bot = dims
    n_dev = n_col * n_ta
    extra = cap - FR
    rf = hh * 16
    conv_rows = 8 + (FR + 2) * (hh + 2) * 16 + 8
    conv_rows = -(-conv_rows // 64) * 64
    sds = jax.ShapeDtypeStruct
    la, lb = width // 2 + 256, width // 2

    def piece_bufs(lanes):
        halls = [(16, 1)] if n_dev == 32 else [(n_col, 4), (n_ta // 2, 1)]
        return [
            pltpu.VMEM((2, 16, 16, lanes), BF16),
            pltpu.VMEM((16, 16, lanes), BF16),
            pltpu.VMEM((2, 16, 16, lanes), BF16),
        ] + [pltpu.VMEM((n, size, 16, lanes), BF16) for n, size in halls]

    n_sems = 2 * (2 + 2 * (1 if n_dev == 32 else 2)) + 1
    outs = (
        sds((FR, hh, ww, width), BF16),
        sds((extra, hh, ww, width), BF16),
        sds((FR, hh, ww, width), BF16),
        sds((extra, hh, ww, width), BF16),
        sds((2, 2, 16, 16, la), BF16),
        sds((2, 2, 16, 16, lb), BF16),
        sds((2, 2, bot), F32),
        sds((2, 2, bot), F32),
        sds((2, width), F32),
        sds((2, width), F32),
    )
    vm = pltpu.VMEM
    dma = pltpu.SemaphoreType.DMA
    scratch = [
        vm((cap + extra, hh, ww, width), BF16),
        vm((FR, hh, 16, width), BF16),
        vm((FR, hh, 16, width), BF16),
        vm((FR, hh, 16, width), BF16),
        vm(((2 if n_dev <= 64 else 1) * rf, width), BF16),
        vm((2, hh, ww, width), BF16),
        vm((2, FR * rf, bot), BF16),
        vm((2, FR * rf, 128), F32),
        vm((2, FR * rf, bot), BF16),
        vm((2, FR * rf, bot), BF16),
        vm((2, 2, conv_rows, 128), F32),
        vm((2, conv_rows, 128), F32),
        vm((bot, width), F32),
        vm((bot, bot), F32),
        vm((2, 27, 8, 128), F32),
        vm((2, 32, 128), F32),
        vm((2, n_dev if n_dev <= 64 else 1, 2, bot), F32),
        vm((2, n_ta, 2, width), F32),
        vm((2, n_col, 2, width), F32),
        vm((32, width), F32),
        vm((2, 32, 128), F32),
        piece_bufs(la),
        piece_bufs(lb),
        dma((1,)),
        dma((6,)),
        dma((3, 2, 2)),
        dma((2,)),
        dma((n_sems,)),
        dma((n_sems,)),
        dma((2,)),
        dma((2,)),
        dma((2,)),
        dma((2,)),
        dma((2,)),
        dma((2,)),
    ]
    return pl.pallas_call(
        functools.partial(main_kernel, dims),
        out_shape=outs,
        in_specs=[SM, SM, ANY, ANY] + [VM] * 8,
        out_specs=(ANY,) * 6 + (VM,) * 4,
        scratch_shapes=scratch,
        compiler_params=pltpu.CompilerParams(
            collective_id=0, has_side_effects=True, vmem_limit_bytes=66_500_000
        ),
        name="blocks",
    )(held, okmask, frames, gout, w1, w2, w3, taps, ngain, nbias, wgain, wbias)


def place_kernel(
    cap,
    held,
    a2w,
    a2r,
    gw,
    gr,
    pa,
    pb,
    i_ng,
    i_nb,
    i_wg,
    i_wb,
    out,
    grad,
    o_w1,
    o_w2,
    o_k,
    o_w3,
    o_ng,
    o_nb,
    o_wg,
    o_wb,
    work,
    zero,
    in_sem,
    out_sem,
):
    half = pb.shape[-1]
    extra = cap - FR
    col, ta = lax.axis_index("col"), lax.axis_index("ta")
    odd = lax.rem(ta, 2)
    first = held[col, ta - odd]
    live = jnp.where(odd == 0, first, 2 * FR - first)
    arrays = ((a2w, a2r, out), (gw, gr, grad))

    def source(j):
        pos = jnp.where(odd == 0, j, first + j)
        mine = jnp.where(odd == 0, pos < FR, pos >= FR)
        own = jnp.where(odd == 0, pos, pos - FR)
        far = jnp.where(odd == 0, pos - FR, pos - (FR - extra))
        return mine, own, far

    def fetch(j, carry):
        mine, own, far = source(j)
        for i, (near, back, _) in enumerate(arrays):

            @pl.when((j < live) & mine)
            def _():
                pltpu.make_async_copy(near.at[own], work.at[i, j], in_sem.at[i, j]).start()

            @pl.when((j < live) & jnp.logical_not(mine))
            def _():
                pltpu.make_async_copy(back.at[far], work.at[i, j], in_sem.at[i, j]).start()

        return carry

    loop(0, cap, fetch)
    zero[...] = jnp.zeros(zero.shape, BF16)

    def clear(j, carry):
        for i, (_, _, dst) in enumerate(arrays):
            pltpu.make_async_copy(zero, dst.at[j], out_sem.at[i]).start()
        return carry

    lax.fori_loop(live, cap, clear, 0)

    def ship(j, carry):
        for i, (near, _, dst) in enumerate(arrays):
            pltpu.make_async_copy(near.at[0], work.at[i, j], in_sem.at[i, j]).wait()
            pltpu.make_async_copy(work.at[i, j], dst.at[j], out_sem.at[i]).start()
        return carry

    lax.fori_loop(0, live, ship, 0)
    o_ng[...] = i_ng[...]
    o_nb[...] = i_nb[...]
    o_wg[...] = i_wg[...]
    o_wb[...] = i_wb[...]
    for b in range(2):
        for p in range(2):
            cols = slice(p * 128, p * 128 + 128)
            taps = pa[b, p, 0:2, :, half + 128 :].astype(F32).reshape(32, 128)
            o_k[:, b, cols] = taps[0:27]
            mid = pa[b, p, :, :, half : half + 128].astype(F32)
            o_w2[b, :, cols] = mid.reshape(256, 128)
            cols = slice(p * half, p * half + half)
            o_w3[b, :, cols] = pa[b, p, :, :, 0:half].astype(F32).reshape(256, half)
            o_w1[b, cols, :] = pb[b, p].astype(F32).reshape(256, half).T
    pltpu.make_async_copy(out, out, out_sem.at[0]).wait()
    pltpu.make_async_copy(grad, grad, out_sem.at[1]).wait()


def place(dims, held, *parts):
    n_col, n_ta, cap, hh, ww, width, bot = dims
    sds = jax.ShapeDtypeStruct
    return pl.pallas_call(
        functools.partial(place_kernel, cap),
        out_shape=(sds((cap, hh, ww, width), BF16),) * 2
        + (
            sds((2, width, bot), F32),
            sds((2, bot, bot), F32),
            sds((27, 2, bot), F32),
            sds((2, bot, width), F32),
            sds((2, 2, bot), F32),
            sds((2, 2, bot), F32),
            sds((2, width), F32),
            sds((2, width), F32),
        ),
        in_specs=[SM] + [ANY] * 4 + [VM] * 6,
        out_specs=(ANY, ANY) + (VM,) * 8,
        scratch_shapes=[
            pltpu.VMEM((2, cap, hh, ww, width), BF16),
            pltpu.VMEM((hh, ww, width), BF16),
            pltpu.SemaphoreType.DMA((2, cap)),
            pltpu.SemaphoreType.DMA((2,)),
        ],
        compiler_params=pltpu.CompilerParams(vmem_limit_bytes=64_000_000),
        name="place",
    )(held, *parts)


def body(
    n_col,
    n_ta,
    frames,
    out_grad,
    held,
    clip_stride,
    w_reduce,
    w_mid,
    depth_kernel,
    w_expand,
    narrow_gain,
    narrow_bias,
    wide_gain,
    wide_bias,
):
    cap, hh, ww, width = frames.shape
    dims = (n_col, n_ta, cap, hh, ww, width, w_mid.shape[1])
    col, ta = lax.axis_index("col"), lax.axis_index("ta")
    lengths = 8 // lax.dynamic_index_in_dim(clip_stride, col, 0, keepdims=False)
    clips = lengths.shape[0]
    before = jnp.arange(clips)[:, None] < jnp.arange(clips)[None, :]
    starts = jnp.sum(jnp.where(before, lengths[:, None], 0), axis=0)
    ids = ta * FR + jnp.arange(FR + 1)
    begins = jnp.any(starts[None, :] == ids[:, None], axis=1) | (ids >= n_ta * FR)
    ok = jnp.logical_not(begins).astype(F32)
    okmask = jnp.stack([ok[:-1], ok[1:]])
    parts = run_main(
        dims,
        held,
        okmask,
        frames,
        out_grad,
        w_reduce,
        w_mid,
        w_expand,
        jnp.swapaxes(depth_kernel, 0, 1),
        narrow_gain,
        narrow_bias,
        wide_gain,
        wide_bias,
    )
    outs = place(dims, held, *parts)
    return outs[:4] + (jnp.swapaxes(outs[4], 0, 1),) + outs[5:]


def solution(mesh):
    split = P(("col", "ta"), None, None, None)
    return jax.shard_map(
        functools.partial(body, mesh.shape["col"], mesh.shape["ta"]),
        mesh=mesh,
        in_specs=(split, split) + (P(),) * 10,
        out_specs=(split, split) + (P(),) * 8,
        check_vma=False,
    )
```
